32 devices in a mesh: dp: 8 (over z, core), tensor: 4 (over y, x).
Axes of the slice: x: 2, y: 2, z: 4, core: 2. Of those that a mesh axis runs over, the one named last changes fastest.
Arguments:
- tokens: bfloat16 [8192, 2048], P(('dp', 'tensor')), may hold values from -6 to 6
- lengths: int32 [8, 3], P('dp'), may hold values from 1 to 1022, as said below
- gain_one: float32 [2048], replicated, may hold values from 0.1 to 1.9
- w_query: bfloat16 [2048, 2048], P(None, 'tensor'), may hold values from -0.125 to 0.125
- w_key: bfloat16 [2048, 512], P(None, 'tensor'), may hold values from -0.125 to 0.125
- w_value: bfloat16 [2048, 512], P(None, 'tensor'), may hold values from -0.125 to 0.125
- w_out: bfloat16 [2048, 2048], P('tensor'), may hold values from -1.5 to 1.5
- gain_two: float32 [2048], replicated, may hold values from 0.1 to 1.9
- w_gate: bfloat16 [2048, 8192], P(None, 'tensor'), may hold values from -0.125 to 0.125
- w_up: bfloat16 [2048, 8192], P(None, 'tensor'), may hold values from -0.125 to 0.125
- w_down: bfloat16 [8192, 2048], P('tensor'), may hold values from -0.0625 to 0.0625
- cotangent: bfloat16 [8192, 2048], P(('dp', 'tensor')), may hold values from -6 to 6
Outputs:
- output: bfloat16 [8192, 2048], P(('dp', 'tensor'))
- grad_tokens: bfloat16 [8192, 2048], P(('dp', 'tensor'))
- grad_gain_one: float32 [2048], P(('dp', 'tensor'))
- grad_w_query: float32 [2048, 2048], P('dp', 'tensor')
- grad_w_key: float32 [2048, 512], P('dp', 'tensor')
- grad_w_value: float32 [2048, 512], P('dp', 'tensor')
- grad_w_out: float32 [2048, 2048], P('tensor', 'dp')
- grad_gain_two: float32 [2048], P(('dp', 'tensor'))
- grad_w_gate: float32 [2048, 8192], P('dp', 'tensor')
- grad_w_up: float32 [2048, 8192], P('dp', 'tensor')
- grad_w_down: float32 [8192, 2048], P('tensor', 'dp')
The draws below stay inside these ranges and needn't reach their ends.
Inputs may be any that keep to these rules, and one draw needn't show every extreme that they name: Each group's 3 lengths are positive and sum to between 768 and 1024; some group sums to exactly 1024, and its two shorter documents hold one token each; in every group one document holds at least 512 tokens and the others at most 128; the slots after the last document are padding.
All inputs are finite; a program needn't handle non-finite values.
Results may differ from the reference program's by a relative error of at most 0.023.
Values may be sent and summed in bfloat16 or wider, within the bound.
A program may use at most 256 MiB of HBM per device.

```python
import math
import jax
import jax.numpy as jnp
from jax import lax

D = 2048
H = 32
KV = 8
HD = 64
FF = 8192
GROUP = 1024
DOCS = 3
TOKENS = 8192
N_DP = 8
N_TENSOR = 4


def draw_lengths(key, part):
    fill_key, full_key, short_key, order_key = jax.random.split(key, 4)
    filled = jax.random.randint(fill_key, (N_DP,), 3 * GROUP // 4, GROUP + 1)
    full_group = jax.random.randint(full_key, (), 0, N_DP)
    is_full = jnp.arange(N_DP) == full_group
    filled = jnp.where(is_full, GROUP, filled)
    shorter = jax.random.randint(short_key, (N_DP, DOCS - 1), 1, GROUP // 8 + 1)
    shorter = jnp.where(is_full[:, None], 1, shorter)
    longest = filled - jnp.sum(shorter, axis=1)
    joined = jnp.concatenate([longest[:, None], shorter], axis=1)
    orders = jax.vmap(lambda row_key: jax.random.permutation(row_key, DOCS))(jax.random.split(order_key, N_DP))
    return jnp.take_along_axis(joined, orders, axis=1).astype(jnp.int32)


def strengthened(array, own_key, source, target, blocks, factor):
    def block_of(dim):
        return (jnp.arange(array.shape[dim]) // (array.shape[dim] // blocks)).reshape((-1,) + (1,) * (array.ndim - 1 - dim))

    near = jax.random.permutation(own_key, blocks)[block_of(target)]
    other_side = (block_of(target) + blocks // 2) % blocks
    return jnp.where((block_of(source) == near) | (block_of(source) == other_side), factor * array, array)


def block_scale(rng, shape, pieces, smallest, top_value):
    gain = 1.0
    for dim, shards_of in pieces:
        steps = jax.random.uniform(jax.random.fold_in(jax.random.fold_in(rng, 6), dim), (shards_of,), jnp.float32, smallest / len(pieces), top_value / len(pieces))
        gain = gain * jnp.repeat(jnp.exp(steps), shape[dim] // shards_of).reshape((-1,) + (1,) * (len(shape) - 1 - dim))
    return gain


def gaussian(rng, dims, scale, limit, cuts=(), kind=jnp.bfloat16):
    gain = block_scale(rng, dims, cuts, -0.22, 0.18) if cuts else 1.0
    values = jax.random.normal(rng, dims, jnp.float32) * scale * gain
    return jnp.minimum(jnp.maximum(values, -limit), limit).astype(kind)


def noise_with(rng, dims, scale, reach, shards, heavy, kind=jnp.bfloat16):
    values = scale * jax.random.normal(rng, dims, jnp.float32)
    if shards:
        values = values * block_scale(rng, dims, shards, -0.22, 0.18)
    return jnp.clip(strengthened(values, jax.random.fold_in(rng, 3), *heavy), -reach, reach).astype(kind)


def setup_inputs(seed: int = 0) -> dict:
    splits = jax.random.split(jax.random.key(seed), 13)
    tokens = gaussian(splits[0], (TOKENS, D), 1.0, 6.0, ((0, 32),))
    lengths = draw_lengths(jax.random.fold_in(splits[12], 71), 0)
    gain_one = jnp.clip(1.0 + 0.18 * jax.random.normal(splits[2], (D,), jnp.float32), 0.1, 1.9)
    w_query = gaussian(splits[3], (D, H * HD), D ** -0.5, 0.125, ((1, 4),))
    w_key = gaussian(splits[4], (D, KV * HD), D ** -0.5, 0.125, ((1, 4),))
    w_value = gaussian(splits[5], (D, KV * HD), D ** -0.5, 0.125, ((1, 4),))
    w_out = gaussian(splits[6], (H * HD, D), (HD // 4) ** -0.5, 1.5, ((0, 4),))
    gain_two = jnp.clip(1.0 + 0.18 * jax.random.normal(splits[7], (D,), jnp.float32), 0.1, 1.9)
    w_gate = gaussian(splits[8], (D, FF), D ** -0.5, 0.125, ((1, 4),))
    w_up = gaussian(splits[9], (D, FF), D ** -0.5, 0.125, ((1, 4),))
    w_down = gaussian(splits[10], (FF, D), FF ** -0.5, 0.0625, ((0, 4),))
    cotangent = noise_with(splits[11], (TOKENS, D), 1.0, 6.0, ((0, 32),), (0, 1, 32, 2.75))
    return {"tokens": tokens, "lengths": lengths, "gain_one": gain_one, "w_query": w_query, "w_key": w_key, "w_value": w_value, "w_out": w_out, "gain_two": gain_two, "w_gate": w_gate, "w_up": w_up, "w_down": w_down, "cotangent": cotangent}


EPSILON = 1e-05
MASKED = -1e+30
HIGHEST = lax.Precision.HIGHEST

@jax.custom_vjp
def low(v):
    return lax.optimization_barrier(v.astype(jnp.bfloat16)).astype(jnp.float32)

@jax.custom_vjp
def low_back(v):
    return v

def low_keep(v):
    return (low(v), None)

def low_pass(kept, grad):
    return (grad,)

def back_keep(v):
    return (v, None)

def back_low(kept, grad):
    return (low(grad),)
low.defvjp(low_keep, low_pass)
low_back.defvjp(back_keep, back_low)

def layout(length_row, group_rows):
    boundary = jnp.cumsum(length_row).astype(jnp.int32)
    token_place = jnp.arange(group_rows, dtype=jnp.int32)
    segment = lax.optimization_barrier(jnp.sum((token_place[:, None] >= boundary[None, :]).astype(jnp.int32), axis=1)).astype(jnp.int32)
    starts = jnp.concatenate([jnp.zeros((1,), jnp.int32), boundary]).astype(jnp.int32)
    labels = jnp.arange(starts.shape[0], dtype=jnp.int32)
    seg_start = lax.optimization_barrier(jnp.sum(jnp.where(segment[:, None] == labels[None, :], starts[None, :], 0), axis=1)).astype(jnp.int32)
    return (segment, token_place, token_place - seg_start)

def rope_table(position, head_dim):
    half_dim = head_dim // 2
    freq_index = jnp.arange(half_dim, dtype=jnp.float32)
    base_freq = jnp.exp(-math.log(500000.0) * 2.0 * freq_index / head_dim)
    wavelength = 2.0 * math.pi / base_freq
    smooth = (8192.0 / wavelength - 1.0) / 3.0
    blended = (1.0 - smooth) * base_freq / 32.0 + smooth * base_freq
    frequency = jnp.where(wavelength < 2048.0, base_freq, jnp.where(wavelength > 8192.0, base_freq / 32.0, blended))
    angles = position.astype(jnp.float32)[:, None] * frequency[None, :]
    return (jnp.cos(angles), jnp.sin(angles))

def rotate(heads_in, cos_table, sin_table):
    half_dim = heads_in.shape[-1] // 2
    first_half = heads_in[..., :half_dim]
    second_half = heads_in[..., half_dim:]
    cos_wide = cos_table[:, None, :]
    sin_wide = sin_table[:, None, :]
    return jnp.concatenate([first_half * cos_wide - second_half * sin_wide, second_half * cos_wide + first_half * sin_wide], axis=-1)

def project(copies, weights, width):
    parts = copies.shape[0]
    shaped = weights.reshape(weights.shape[0], parts, width)
    joined = jnp.einsum('pgd,dpc->gpc', copies, shaped, precision=HIGHEST)
    return joined.reshape(copies.shape[1], parts * width)

def merge_back(operand, weights):
    parts = N_TENSOR
    width = operand.shape[1] // parts
    partial_sums = jnp.einsum('gpc,pcd->gpd', operand.reshape(operand.shape[0], parts, width), weights.reshape(parts, width, weights.shape[1]), precision=HIGHEST)
    return lax.optimization_barrier(jnp.sum(low(partial_sums), axis=1))

def attention(query_heads, key_heads, value_heads, segment, token_place):
    group_rows = query_heads.shape[0]
    block_rows = min(512, group_rows)
    blocks = group_rows // block_rows
    keys_full = jnp.repeat(key_heads, H // KV, axis=1)
    values_full = jnp.repeat(value_heads, H // KV, axis=1)

    def one_block(inputs):
        query_block, seg_block, place_block = inputs
        raw_scores = jnp.einsum('qhd,shd->hqs', query_block, keys_full, precision=HIGHEST)
        allowed = (seg_block[:, None] == segment[None, :]) & (token_place[None, :] <= place_block[:, None])
        scores = jnp.where(allowed[None], low_back(raw_scores) * 0.125, MASKED)
        softmax_out = low(jax.nn.softmax(scores, axis=-1))
        return jnp.einsum('hqs,shd->qhd', softmax_out, values_full, precision=HIGHEST)
    stacked = (query_heads.reshape(blocks, block_rows, H, HD), segment.reshape(blocks, block_rows), token_place.reshape(blocks, block_rows))
    return lax.map(jax.checkpoint(one_block), stacked).reshape(group_rows, H, HD)

def layer(x_rows, gain_one, w_query, w_key, w_value, w_out, gain_two, w_gate, w_up, w_down, segment, token_place, cos_table, sin_table):
    group_rows = x_rows.shape[0]
    parts = N_TENSOR
    scale_one = lax.rsqrt(lax.optimization_barrier(jnp.mean(x_rows * x_rows, axis=-1, keepdims=True)) + EPSILON)
    normed_one = low(x_rows * scale_one * gain_one)
    copies_one = low_back(jnp.broadcast_to(normed_one[None], (parts, group_rows, D)))
    query_raw = low_back(project(copies_one, w_query, H * HD // parts))
    key_raw = low_back(project(copies_one, w_key, KV * HD // parts))
    value_raw = low_back(project(copies_one, w_value, KV * HD // parts))
    query_heads = low(rotate(query_raw.reshape(group_rows, H, HD), cos_table, sin_table))
    key_heads = low(rotate(key_raw.reshape(group_rows, KV, HD), cos_table, sin_table))
    value_heads = low(value_raw.reshape(group_rows, KV, HD))
    attended = attention(query_heads, key_heads, value_heads, segment, token_place).reshape(group_rows, H * HD)
    attended = low_back(low(attended))
    mixed = low_back(merge_back(attended, w_out))
    hidden_state = x_rows + mixed
    scale_two = lax.rsqrt(lax.optimization_barrier(jnp.mean(hidden_state * hidden_state, axis=-1, keepdims=True)) + EPSILON)
    normed_two = low(hidden_state * scale_two * gain_two)
    copies_two = low_back(jnp.broadcast_to(normed_two[None], (parts, group_rows, D)))
    gate_proj = low_back(project(copies_two, w_gate, FF // parts))
    up_proj = low_back(project(copies_two, w_up, FF // parts))
    hidden = low(jax.nn.silu(gate_proj) * up_proj)
    return hidden_state + low_back(merge_back(hidden, w_down))

def reference(tokens, lengths, gain_one, w_query, w_key, w_value, w_out, gain_two, w_gate, w_up, w_down, cotangent):
    params = (gain_one.astype(jnp.float32), w_query.astype(jnp.float32), w_key.astype(jnp.float32), w_value.astype(jnp.float32), w_out.astype(jnp.float32), gain_two.astype(jnp.float32), w_gate.astype(jnp.float32), w_up.astype(jnp.float32), w_down.astype(jnp.float32))

    def one_group(running, inputs):
        x_group, grad_group, length_row = inputs
        segment, token_place, position = layout(length_row, GROUP)
        cos_table, sin_table = rope_table(position, HD)

        def forward(x_rows, *weight_list):
            return layer(x_rows, *weight_list, segment, token_place, cos_table, sin_table)
        result, pullback = jax.vjp(forward, x_group.astype(jnp.float32), *params)
        grads = pullback(grad_group.astype(jnp.float32))
        running = tuple((summed + fresh for summed, fresh in zip(running, grads[1:])))
        return (running, (result.astype(jnp.bfloat16), grads[0].astype(jnp.bfloat16)))
    initial = tuple((jnp.zeros_like(param_array) for param_array in params))
    stacked = (tokens.reshape(N_DP, GROUP, D), cotangent.reshape(N_DP, GROUP, D), lengths)
    totals, (outputs, input_grads) = lax.scan(one_group, initial, stacked)
    return (outputs.reshape(TOKENS, D), input_grads.reshape(TOKENS, D), totals[0], totals[1], totals[2], totals[3], totals[4], totals[5], totals[6], totals[7], totals[8])
```

```python
import functools
import math

import jax
import jax.numpy as jnp
import numpy as np
from jax import lax
from jax.experimental import pallas as pl
from jax.experimental.pallas import tpu as pltpu
from jax.sharding import PartitionSpec as P

HD = 64
LANES = 128
EPSILON = 1e-05
MASKED = -1e30
LOG2E = math.log2(math.e)
SCALE2 = 0.125 * LOG2E
BF16 = jnp.bfloat16
F32 = jnp.float32
MESH = pl.DeviceIdType.MESH
VMEM_LIMIT = 60 * 2**20


def dot_nn(a, b):
    return jnp.dot(a, b, preferred_element_type=F32)


def dot_nt(a, b):
    return lax.dot_general(a, b, (((1,), (1,)), ((), ())), preferred_element_type=F32)


def dot_tn(a, b):
    return lax.dot_general(a, b, (((0,), (0,)), ((), ())), preferred_element_type=F32)


def layout(length_row, group_rows):
    token_place = jnp.arange(group_rows, dtype=jnp.int32)
    start = jnp.zeros((group_rows,), jnp.int32)
    end = jnp.int32(0)
    for k in range(length_row.shape[0]):
        end = end + length_row[k]
        start = jnp.where(token_place >= end, end, start)
    return (start, token_place - start)


def rope_table(position):
    half_dim = HD // 2
    freq_index = jnp.arange(half_dim, dtype=F32)
    base_freq = jnp.exp(-math.log(500000.0) * 2.0 * freq_index / HD)
    wavelength = 2.0 * math.pi / base_freq
    smooth = (8192.0 / wavelength - 1.0) / 3.0
    blended = (1.0 - smooth) * base_freq / 32.0 + smooth * base_freq
    frequency = jnp.where(
        wavelength < 2048.0, base_freq, jnp.where(wavelength > 8192.0, base_freq / 32.0, blended)
    )
    angles = position.astype(F32)[:, None] * frequency[None, :]
    cos_half, sin_half = (jnp.cos(angles), jnp.sin(angles))
    return (
        jnp.concatenate([cos_half] * 4, axis=1),
        jnp.concatenate([-sin_half, sin_half, -sin_half, sin_half], axis=1),
    )


class Peers:
    def __init__(self):
        self.n = lax.axis_size("tensor")
        self.m = self.n // 2
        index = lax.axis_index("tensor")
        self.y = lax.div(index, np.int32(self.m))
        self.x = lax.rem(index, np.int32(self.m))

    def at(self, flip, step):
        row = 1 - self.y if flip else self.y
        return row * self.m + lax.rem(self.x + np.int32(step + self.m), np.int32(self.m))

    def minor(self, step):
        return {"tensor": self.at(0, step)}

    def major(self):
        return {"tensor": self.at(1, 0)}

    def steps(self):
        return range(1, self.m)


def core_of():
    return lax.rem(lax.axis_index("dp"), np.int32(2))


def other_core():
    return {"dp": lax.axis_index("dp") + 1 - 2 * core_of()}


def greet(peers, core=False):
    barrier = pltpu.get_barrier_semaphore()
    for step in peers.steps():
        pl.semaphore_signal(barrier, inc=1, device_id=peers.minor(step), device_id_type=MESH)
    pl.semaphore_signal(barrier, inc=1, device_id=peers.major(), device_id_type=MESH)
    if core:
        pl.semaphore_signal(barrier, inc=1, device_id=other_core(), device_id_type=MESH)
    pl.semaphore_wait(barrier, peers.m + (1 if core else 0))


class Wire:
    def __init__(self, send_sem, recv_sem):
        self.send_sem, self.recv_sem, self.copies = send_sem, recv_sem, []

    def copy(self, source, target, device):
        k = len(self.copies)
        copy = pltpu.make_async_remote_copy(
            src_ref=source,
            dst_ref=target,
            send_sem=self.send_sem.at[k],
            recv_sem=self.recv_sem.at[k],
            device_id=device,
            device_id_type=MESH,
        )
        copy.start()
        self.copies.append(copy)
        return copy

    def wait_sends(self):
        for copy in self.copies:
            copy.wait_send()


def wire_count(n):
    return 4 * (n // 2 - 1) + 2


def wires(n):
    return [pltpu.SemaphoreType.DMA((wire_count(n),))] * 2


class Local:
    def __init__(self, sem):
        self.sem, self.copies = sem, []

    def copy(self, source, target):
        copy = pltpu.make_async_copy(source, target, self.sem.at[len(self.copies)])
        copy.start()
        self.copies.append(copy)
        return copy


def block(ref, index, rows):
    return ref.at[pl.ds(pl.multiple_of(index * rows, rows), rows)]


def half_block(ref, index, rows, half):
    size = rows // 2
    return ref.at[pl.ds(pl.multiple_of(index * rows + half * size, size), size)]


def gather(peers, wire, buf, rows, use, after_forward=None):
    steps = list(peers.steps())
    part = lambda index, half: half_block(buf, index, rows, half)
    me, major = peers.at(0, 0), peers.at(1, 0)
    send = lambda ref, device: wire.copy(ref, ref, device)
    minor_a = [send(part(me, 0), peers.minor(j)) for j in steps]
    major_b = send(part(me, 1), peers.major())
    minor_b = [send(part(me, 1), peers.minor(j)) for j in steps]
    major_a = send(part(me, 0), peers.major())
    use(me)
    forward_a, forward_b = [], []
    for j, copy in zip(steps, minor_a):
        copy.wait_recv()
        forward_a.append(send(part(peers.at(0, -j), 0), peers.major()))
    major_b.wait_recv()
    for j in steps:
        forward_b.append(send(part(major, 1), peers.minor(j)))
    if after_forward is not None:
        after_forward()
    for j, copy in zip(steps, minor_b):
        copy.wait_recv()
        use(peers.at(0, -j))
    major_a.wait_recv()
    use(major)
    for j, copy_a, copy_b in zip(steps, forward_a, forward_b):
        copy_a.wait_recv()
        copy_b.wait_recv()
        use(peers.at(1, -j))


def add_rows(target, others, size):
    def some(k, carry):
        at = pl.ds(pl.multiple_of(k * 16, 16), 16)
        total = target[at, :].astype(F32)
        for other in others:
            total = total + other[at, :].astype(F32)
        target[at, :] = total.astype(target.dtype)
        return carry

    lax.fori_loop(0, size // 16, some, 0)


def scatter(peers, wire, part_ref, slots, rows, make, meanwhile=None):
    steps = list(peers.steps())
    part = lambda index, half: half_block(part_ref, index, rows, half)
    me, major = peers.at(0, 0), peers.at(1, 0)
    count = len(steps)
    via_a, via_b, direct_b, sum_a = (
        [slots.at[group * count + k] for k in range(count)] for group in range(4)
    )
    direct_a, sum_b = slots.at[4 * count], slots.at[4 * count + 1]
    make((1 - peers.y) * peers.m, peers.m)
    first_a, first_b = [], []
    for k, j in enumerate(steps):
        index = peers.at(1, j)
        first_a.append(wire.copy(part(index, 0), via_a[k], peers.major()))
        first_b.append(wire.copy(part(index, 1), via_b[k], peers.minor(j)))
    plain_a = wire.copy(part(major, 0), direct_a, peers.major())
    make(peers.y * peers.m, peers.m)
    plain_b = [
        wire.copy(part(peers.at(0, j), 1), direct_b[k], peers.minor(j))
        for k, j in enumerate(steps)
    ]
    done_a = []
    for k, j in enumerate(steps):
        first_a[k].wait_recv()
        target = part(peers.at(0, j), 0)
        add_rows(target, [via_a[k]], rows // 2)
        done_a.append(wire.copy(target, sum_a[k], peers.minor(j)))
    for copy in first_b:
        copy.wait_recv()
    target = part(major, 1)
    add_rows(target, via_b, rows // 2)
    done_b = wire.copy(target, sum_b, peers.major())
    if meanwhile is not None:
        meanwhile()
    for copy in (plain_a, *plain_b, *done_a, done_b):
        copy.wait_recv()
    return (
        (part(me, 0), direct_a, *sum_a),
        (part(me, 1), sum_b, *direct_b),
    )


def slots_for(n, rows, width):
    return pltpu.VMEM((wire_count(n), rows // 2, width), BF16)


def lane_of(rows, width=LANES):
    return lax.broadcasted_iota(jnp.int32, (rows, width), 1)


def first_head(rows):
    return lane_of(rows) < HD


def swap_halves(values):
    first = lax.rem(lane_of(values.shape[0]), np.int32(HD)) < HD // 2
    return jnp.where(first, pltpu.roll(values, LANES - HD // 2, 1), pltpu.roll(values, HD // 2, 1))


def doubled(pair, heads):
    if heads == 1:
        return [jnp.concatenate([pair, pair], axis=1)]
    out = []
    for k in range(heads // 2):
        both = pair[:, k * LANES : (k + 1) * LANES]
        swapped = pltpu.roll(both, HD, 1)
        first = first_head(both.shape[0])
        out += [jnp.where(first, both, swapped), jnp.where(first, swapped, both)]
    return out


def project_kernel(
    tokens, gain, cos_table, sin_table, w_query, w_key, w_value,
    gathered_out, query_out, key_out, value_out,
    gathered, weights, raw_key, raw_value, send_sem, recv_sem, local_sem,
):
    peers = Peers()
    rows, depth = tokens.shape
    q_width, kv_heads = w_query.shape[1], w_key.shape[1] // HD
    kv_width = kv_heads * LANES
    local = Local(local_sem)
    loads = [
        local.copy(w_key, raw_key),
        local.copy(w_value, raw_value),
        local.copy(w_query, weights.at[:, pl.ds(0, q_width)]),
    ]
    greet(peers)
    me = peers.at(0, 0)
    gain_row = gain[...]

    def normalize(k, carry):
        values = tokens[pl.ds(pl.multiple_of(k * 16, 16), 16), :].astype(F32)
        scale = lax.rsqrt(jnp.mean(values * values, axis=-1, keepdims=True) + EPSILON)
        gathered[pl.ds(pl.multiple_of(me * rows + k * 16, 16), 16), :] = (
            values * scale * gain_row
        ).astype(BF16)
        return carry

    lax.fori_loop(0, rows // 16, normalize, 0)
    started = [False]
    saves = []

    def prepare():
        for load in loads:
            load.wait()

        def some(k, carry):
            at = pl.ds(pl.multiple_of(k * 128, 128), 128)
            for raw, base in ((raw_key, q_width), (raw_value, q_width + kv_width)):
                for j, twice in enumerate(doubled(raw[at, :].astype(F32), kv_heads)):
                    weights[at, base + j * LANES : base + (j + 1) * LANES] = twice.astype(BF16)
            return carry

        lax.fori_loop(0, depth // 128, some, 0)

    def use(index):
        if not started[0]:
            started[0] = True
            prepare()
        at = pl.ds(pl.multiple_of(index * rows, rows), rows)
        saves.append(local.copy(gathered.at[at], gathered_out.at[at]))
        cos, sin = cos_table[at, :], sin_table[at, :]
        normed = gathered[at, :]
        for base, width, out, turn in (
            (0, q_width, query_out, True),
            (q_width, kv_width, key_out, True),
            (q_width + kv_width, kv_width, value_out, False),
        ):
            raw = dot_nn(normed, weights[:, base : base + width])
            for c in range(0, width, LANES):
                piece = raw[:, c : c + LANES]
                if turn:
                    piece = piece * cos + swap_halves(piece) * sin
                out[at, c : c + LANES] = piece.astype(BF16)

    wire = Wire(send_sem, recv_sem)
    gather(peers, wire, gathered, rows, use)
    wire.wait_sends()
    for save in saves:
        save.wait()


def any_spec():
    return pl.BlockSpec(memory_space=pl.ANY)


def vmem_spec():
    return pl.BlockSpec(memory_space=pltpu.VMEM)


def params(collective_id):
    return pltpu.CompilerParams(
        collective_id=collective_id, has_side_effects=True, vmem_limit_bytes=VMEM_LIMIT
    )


def project(tokens, gain, cos_table, sin_table, w_query, w_key, w_value):
    n = lax.axis_size("tensor")
    rows, depth = tokens.shape
    group = rows * n
    q_width, kv_raw = w_query.shape[1], w_key.shape[1]
    kv_width = kv_raw // HD * LANES
    return pl.pallas_call(
        project_kernel,
        out_shape=(
            jax.ShapeDtypeStruct((group, depth), BF16),
            jax.ShapeDtypeStruct((group, q_width), BF16),
            jax.ShapeDtypeStruct((group, kv_width), BF16),
            jax.ShapeDtypeStruct((group, kv_width), BF16),
        ),
        in_specs=[vmem_spec()] * 4 + [any_spec()] * 3,
        out_specs=(any_spec(), vmem_spec(), vmem_spec(), vmem_spec()),
        scratch_shapes=[
            pltpu.VMEM((group, depth), BF16),
            pltpu.VMEM((depth, q_width + 2 * kv_width), BF16),
            pltpu.VMEM((depth, kv_raw), BF16),
            pltpu.VMEM((depth, kv_raw), BF16),
            *wires(n),
            pltpu.SemaphoreType.DMA((3 + n,)),
        ],
        cost_estimate=pl.CostEstimate(
            flops=2 * group * depth * (q_width + 2 * kv_width),
            bytes_accessed=40 * 2**20,
            transcendentals=0,
        ),
        compiler_params=params(1),
    )(tokens, gain, cos_table, sin_table, w_query, w_key, w_value)


def attend_kernel(
    query, key, value, start, tokens, gain, w_out, cotangent,
    attended, log_total, state_out, normed_out, cot_a, cot_b,
    w_buf, part, slots, send_sem, recv_sem, cot_send, cot_recv, local_sem,
):
    peers = Peers()
    rows, depth = tokens.shape
    group, q_width = query.shape
    pairs_per_kv = q_width // LANES // (key.shape[1] // LANES)
    load = Local(local_sem).copy(w_out, w_buf)
    greet(peers)
    cot_wire = Wire(cot_send, cot_recv)
    for k, j in enumerate(peers.steps()):
        cot_wire.copy(half_block(cotangent, 0, rows, 0), cot_a.at[k], peers.minor(j))
    cot_wire.copy(half_block(cotangent, 0, rows, 1), cot_b, peers.major())

    tile = 256
    for i in range(group // tile):
        keys = (i + 1) * tile

        def one_pair(pair, carry, i=i, keys=keys):
            at = pl.ds(i * tile, tile)
            lanes = pl.ds(pl.multiple_of(pair * LANES, LANES), LANES)
            kv_lanes = pl.ds(
                pl.multiple_of(lax.div(pair, np.int32(pairs_per_kv)) * LANES, LANES), LANES
            )
            both = query[at, lanes]
            key_rows, value_rows = key[0:keys, kv_lanes], value[0:keys, kv_lanes]
            first = first_head(tile)
            column = lax.broadcasted_iota(jnp.int32, (tile, keys), 1)
            row = lax.broadcasted_iota(jnp.int32, (tile, keys), 0) + i * tile
            allowed = (column >= start[at, :]) & (column <= row)
            outs = []
            for h in range(2):
                own = first if h == 0 else jnp.logical_not(first)
                scores = dot_nt(jnp.where(own, both, jnp.zeros_like(both)), key_rows)
                scores = jnp.where(allowed, scores, MASKED)
                row_max = jnp.max(scores, axis=-1, keepdims=True)
                weights = jnp.exp2((scores - row_max) * SCALE2)
                row_sum = jnp.sum(weights, axis=-1, keepdims=True)
                outs.append(dot_nn(weights.astype(BF16), value_rows) / row_sum)
                log_total[pair * 2 + h, at, :] = row_max * SCALE2 + jnp.log2(row_sum)
            attended[at, lanes] = jnp.where(first, outs[0], outs[1]).astype(BF16)
            return carry

        lax.fori_loop(0, q_width // LANES, one_pair, 0)

    load.wait()

    def make(first, count):
        at = pl.ds(pl.multiple_of(first * rows, rows), count * rows)
        heads = attended[at, :]
        for c in range(0, depth, 1024):
            part[at, c : c + 1024] = dot_nn(heads, w_buf[:, c : c + 1024]).astype(BF16)

    wire = Wire(send_sem, recv_sem)
    sums = scatter(peers, wire, part, slots, rows, make)
    gain_row = gain[...]
    half = rows // 2
    for h in range(2):

        def finish(k, carry, h=h):
            inner = pl.ds(pl.multiple_of(k * 16, 16), 16)
            outer = pl.ds(pl.multiple_of(h * half + k * 16, 16), 16)
            mixed = sums[h][0][inner, :].astype(F32)
            for other in sums[h][1:]:
                mixed = mixed + other[inner, :].astype(F32)
            state = tokens[outer, :].astype(F32) + mixed
            scale = lax.rsqrt(jnp.mean(state * state, axis=-1, keepdims=True) + EPSILON)
            state_out[outer, :] = state
            normed_out[outer, :] = (state * scale * gain_row).astype(BF16)
            return carry

        lax.fori_loop(0, half // 16, finish, 0)
    wire.wait_sends()
    for copy in cot_wire.copies:
        copy.wait()


def attend(query, key, value, start, tokens, gain, w_out, cotangent):
    n = lax.axis_size("tensor")
    rows, depth = tokens.shape
    group, q_width = query.shape
    m = n // 2
    return pl.pallas_call(
        attend_kernel,
        out_shape=(
            jax.ShapeDtypeStruct((group, q_width), BF16),
            jax.ShapeDtypeStruct((q_width // HD, group, 1), F32),
            jax.ShapeDtypeStruct((rows, depth), F32),
            jax.ShapeDtypeStruct((rows, depth), BF16),
            jax.ShapeDtypeStruct((m - 1, rows // 2, depth), BF16),
            jax.ShapeDtypeStruct((rows // 2, depth), BF16),
        ),
        in_specs=[vmem_spec()] * 6 + [any_spec()] * 2,
        out_specs=(vmem_spec(), vmem_spec(), vmem_spec(), vmem_spec(), any_spec(), any_spec()),
        scratch_shapes=[
            pltpu.VMEM(w_out.shape, BF16),
            pltpu.VMEM((group, depth), BF16),
            slots_for(n, rows, depth),
            *wires(n),
            pltpu.SemaphoreType.DMA((m,)),
            pltpu.SemaphoreType.DMA((m,)),
            pltpu.SemaphoreType.DMA((1,)),
        ],
        cost_estimate=pl.CostEstimate(
            flops=2 * group * depth * q_width * 4, bytes_accessed=40 * 2**20, transcendentals=0
        ),
        compiler_params=params(2),
    )(query, key, value, start, tokens, gain, w_out, cotangent)


class Exchange:
    def __init__(self, wire, stage, received):
        self.wire, self.stage, self.received, self.sent = wire, stage, received, []

    def run(self, jobs):
        mine = core_of()
        copies = []
        for k in range(len(jobs) + 1):
            if k < len(jobs):
                tile, save, pair = jobs[k]
                slot = self.stage.at[k % 2]
                if k >= 2:
                    copies[k - 2].wait_send()
                tile(2 * pair + 1 - mine, slot, False)
                copies.append(self.wire.copy(slot, self.received.at[k], other_core()))
            if k >= 1:
                tile, save, pair = jobs[k - 1]
                copies[k - 1].wait_recv()
                tile(2 * pair + mine, self.received.at[k - 1], True)
                save(pair, self.received.at[k - 1])
        for copy in copies[-2:]:
            copy.wait_send()


def put(target, at, value, add):
    if add:
        value = value + target[at].astype(F32)
    target[at] = value.astype(BF16)


def hidden_kernel(
    normed, cotangent, cot_a, cot_b, w_gate, w_up,
    gathered_out, hidden_out, slope_gate_out, slope_up_out, cot_out, grad_down_out,
    gathered, gate_buf, up_buf, hidden, slope_gate, slope_up, cot, stage, received,
    send_sem, recv_sem, cot_send, cot_recv, core_send, core_recv, local_sem,
):
    peers = Peers()
    rows, depth = normed.shape
    units = w_gate.shape[1]
    me, major = peers.at(0, 0), peers.at(1, 0)
    local = Local(local_sem)
    first_load = local.copy(normed, block(gathered, me, rows))
    loads = [local.copy(w_gate, gate_buf), local.copy(w_up, up_buf)]
    cot_loads = [local.copy(cotangent, block(cot, me, rows))]
    for k, j in enumerate(peers.steps()):
        cot_loads.append(local.copy(cot_a.at[k], half_block(cot, peers.at(0, -j), rows, 0)))
    cot_loads.append(local.copy(cot_b, half_block(cot, major, rows, 1)))
    greet(peers, core=True)
    first_load.wait()
    saves, waiting = [], list(loads)

    def use(index):
        while waiting:
            waiting.pop().wait()
        at = pl.ds(pl.multiple_of(index * rows, rows), rows)
        saves.append(local.copy(gathered.at[at], gathered_out.at[at]))
        tile = 512

        def some(k, carry):
            lanes = pl.ds(pl.multiple_of(k * tile, tile), tile)
            x = gathered[at, :]
            gate = dot_nn(x, gate_buf[:, lanes])
            up = dot_nn(x, up_buf[:, lanes])
            sigmoid = jax.nn.sigmoid(gate)
            silu = gate * sigmoid
            hidden[at, lanes] = (silu * up).astype(BF16)
            slope_up[at, lanes] = silu.astype(BF16)
            slope_gate[at, lanes] = (up * sigmoid * (1.0 + gate * (1.0 - sigmoid))).astype(BF16)
            return carry

        lax.fori_loop(0, units // tile, some, 0)
        for source, target in (
            (hidden, hidden_out), (slope_gate, slope_gate_out), (slope_up, slope_up_out)
        ):
            saves.append(local.copy(source.at[at], target.at[at]))

    cot_wire = Wire(cot_send, cot_recv)
    cot_copies = []

    def send_rest():
        for load in cot_loads:
            load.wait()
        send = lambda index, half, device: cot_copies.append(
            cot_wire.copy(
                half_block(cot, index, rows, half), half_block(cot, index, rows, half), device
            )
        )
        for j in peers.steps():
            send(me, 1, peers.minor(j))
        send(me, 0, peers.major())
        for j in peers.steps():
            send(peers.at(0, -j), 0, peers.major())
            send(major, 1, peers.minor(j))

    wire = Wire(send_sem, recv_sem)
    gather(peers, wire, gathered, rows, use, send_rest)
    for copy in cot_copies:
        copy.wait_recv()
    saves.append(local.copy(cot, cot_out))
    columns = stage.shape[2]

    def tile(index, target, add):
        lanes = pl.ds(pl.multiple_of(index * columns, columns), columns)
        step = 512

        def some(k, carry):
            at = pl.ds(pl.multiple_of(k * step, step), step)
            put(target, (at, slice(None)), dot_tn(hidden[:, at], cot[:, lanes]), add)
            return carry

        lax.fori_loop(0, units // step, some, 0)

    def save(k, ref):
        saves.append(local.copy(ref, grad_down_out.at[pl.ds(k * units, units)]))

    pairs = received.shape[0]
    Exchange(Wire(core_send, core_recv), stage, received).run(
        [(tile, save, k) for k in range(pairs)]
    )
    wire.wait_sends()
    cot_wire.wait_sends()
    for copy in saves:
        copy.wait()


def hidden_units(normed, cotangent, cot_a, cot_b, w_gate, w_up):
    n = lax.axis_size("tensor")
    pairs = lax.axis_size("dp") // 2
    rows, depth = normed.shape
    group, units, columns = rows * n, w_gate.shape[1], depth // (2 * pairs)
    wide = lambda width: jax.ShapeDtypeStruct((group, width), BF16)
    return pl.pallas_call(
        hidden_kernel,
        out_shape=(
            wide(depth), wide(units), wide(units), wide(units), wide(depth),
            jax.ShapeDtypeStruct((pairs * units, columns), BF16),
        ),
        in_specs=[any_spec()] * 6,
        out_specs=(any_spec(),) * 6,
        scratch_shapes=[
            pltpu.VMEM((group, depth), BF16),
            pltpu.VMEM((depth, units), BF16),
            pltpu.VMEM((depth, units), BF16),
            pltpu.VMEM((group, units), BF16),
            pltpu.VMEM((group, units), BF16),
            pltpu.VMEM((group, units), BF16),
            pltpu.VMEM((group, depth), BF16),
            pltpu.VMEM((2, units, columns), BF16),
            pltpu.VMEM((pairs, units, columns), BF16),
            *wires(n),
            *wires(n),
            pltpu.SemaphoreType.DMA((pairs,)),
            pltpu.SemaphoreType.DMA((pairs,)),
            pltpu.SemaphoreType.DMA((4 * n + pairs + n + 8,)),
        ],
        cost_estimate=pl.CostEstimate(
            flops=6 * group * depth * units, bytes_accessed=60 * 2**20, transcendentals=0
        ),
        compiler_params=params(3),
    )(normed, cotangent, cot_a, cot_b, w_gate, w_up)


def norm_back(values, gain_row, grad_normed):
    scale = lax.rsqrt(jnp.mean(values * values, axis=-1, keepdims=True) + EPSILON)
    unit = values * scale
    scaled = grad_normed * gain_row
    grad = scale * (scaled - unit * jnp.mean(scaled * unit, axis=-1, keepdims=True))
    return grad, grad_normed * unit


def fold_rows(values):
    return values[:8] + values[8:]


def hidden_back_kernel(
    slope_gate, slope_up, cot_all, gathered_in, state, cotangent, gain, w_down, w_gate, w_up,
    grad_state_out, grad_mixed_out, gain_out, grad_gate_up_out,
    gate_buf, up_buf, down_buf, grad_gate, grad_up, cot, part, slots, stage, received,
    send_sem, recv_sem, core_send, core_recv, local_sem,
):
    peers = Peers()
    rows, depth = state.shape
    group, units = slope_gate.shape
    chunk = down_buf.shape[1]
    chunks = units // chunk
    local = Local(local_sem)
    load_cot = local.copy(cot_all, cot)
    down_chunk = lambda c: local.copy(w_down.at[pl.ds(c * chunk, chunk)], down_buf.at[c % 2])
    down_loads = [down_chunk(0), down_chunk(1)]
    load_slopes = [local.copy(slope_gate, grad_gate), local.copy(slope_up, grad_up)]
    loads = [local.copy(w_gate, gate_buf), local.copy(w_up, up_buf)]
    load_state = local.copy(state, grad_state_out)
    greet(peers, core=True)
    load_cot.wait()
    for c in range(chunks):
        down_loads[c].wait()
        if c == 0:
            for load in load_slopes:
                load.wait()
        lanes = slice(c * chunk, (c + 1) * chunk)
        grad_hidden = dot_nt(cot[...], down_buf[c % 2])
        grad_gate[:, lanes] = (grad_hidden * grad_gate[:, lanes].astype(F32)).astype(BF16)
        grad_up[:, lanes] = (grad_hidden * grad_up[:, lanes].astype(F32)).astype(BF16)
        if c + 2 < chunks:
            down_loads.append(down_chunk(c + 2))
    load_gathered = local.copy(gathered_in, cot)
    for load in loads:
        load.wait()

    def make(first, count):
        at = pl.ds(pl.multiple_of(first * rows, rows), count * rows)
        step = 512

        def some(k, carry):
            inner = pl.ds(pl.multiple_of(k * step, step), step)
            total = dot_nt(grad_gate[at, :], gate_buf[inner, :])
            total = total + dot_nt(grad_up[at, :], up_buf[inner, :])
            part[at, inner] = total.astype(BF16)
            return carry

        lax.fori_loop(0, depth // step, some, 0)

    deep = stage.shape[1]
    saves = []

    def tile_of(grad):
        def tile(index, target, add):
            lanes = pl.ds(pl.multiple_of(index * deep, deep), deep)
            step = min(1024, units)

            def some(k, carry):
                inner = pl.ds(pl.multiple_of(k * step, step), step)
                put(target, (slice(None), inner), dot_tn(cot[:, lanes], grad[:, inner]), add)
                return carry

            lax.fori_loop(0, units // step, some, 0)

        return tile

    def save_at(base):
        def save(k, ref):
            target = grad_gate_up_out.at[pl.ds(k * deep, deep), pl.ds(base, units)]
            saves.append(local.copy(ref, target))

        return save

    def weight_grads():
        load_gathered.wait()
        pairs = received.shape[0] // 2
        Exchange(Wire(core_send, core_recv), stage, received).run(
            [(tile_of(grad_gate), save_at(0), k) for k in range(pairs)]
            + [(tile_of(grad_up), save_at(units), k) for k in range(pairs)]
        )

    wire = Wire(send_sem, recv_sem)
    sums = scatter(peers, wire, part, slots, rows, make, weight_grads)
    load_state.wait()
    gain_row = gain[...]
    half = rows // 2
    gain_out[...] = jnp.zeros_like(gain_out)
    for h in range(2):

        def finish(k, carry, h=h):
            inner = pl.ds(pl.multiple_of(k * 16, 16), 16)
            outer = pl.ds(pl.multiple_of(h * half + k * 16, 16), 16)
            grad_normed = sums[h][0][inner, :].astype(F32)
            for other in sums[h][1:]:
                grad_normed = grad_normed + other[inner, :].astype(F32)
            grad, gain_part = norm_back(grad_state_out[outer, :], gain_row, grad_normed)
            grad = grad + cotangent[outer, :].astype(F32)
            gain_out[...] += fold_rows(gain_part)
            grad_state_out[outer, :] = grad
            grad_mixed_out[outer, :] = grad.astype(BF16)
            return carry

        lax.fori_loop(0, half // 16, finish, 0)
    wire.wait_sends()
    for copy in saves:
        copy.wait()


def hidden_back(
    slope_gate, slope_up, cot_all, gathered, state, cotangent, gain, w_down, w_gate, w_up
):
    n = lax.axis_size("tensor")
    pairs = lax.axis_size("dp") // 2
    rows, depth = state.shape
    group, units = slope_gate.shape
    deep = depth // (2 * pairs)
    chunk = 512
    return pl.pallas_call(
        hidden_back_kernel,
        out_shape=(
            jax.ShapeDtypeStruct((rows, depth), F32),
            jax.ShapeDtypeStruct((rows, depth), BF16),
            jax.ShapeDtypeStruct((8, depth), F32),
            jax.ShapeDtypeStruct((pairs * deep, 2 * units), BF16),
        ),
        in_specs=[any_spec()] * 5 + [vmem_spec()] * 2 + [any_spec()] * 3,
        out_specs=(vmem_spec(), vmem_spec(), vmem_spec(), any_spec()),
        scratch_shapes=[
            pltpu.VMEM((depth, units), BF16),
            pltpu.VMEM((depth, units), BF16),
            pltpu.VMEM((2, chunk, depth), BF16),
            pltpu.VMEM((group, units), BF16),
            pltpu.VMEM((group, units), BF16),
            pltpu.VMEM((group, depth), BF16),
            pltpu.VMEM((group, depth), BF16),
            slots_for(n, rows, depth),
            pltpu.VMEM((2, deep, units), BF16),
            pltpu.VMEM((2 * pairs, deep, units), BF16),
            *wires(n),
            pltpu.SemaphoreType.DMA((2 * pairs,)),
            pltpu.SemaphoreType.DMA((2 * pairs,)),
            pltpu.SemaphoreType.DMA((8 + units // chunk + 2 * pairs,)),
        ],
        cost_estimate=pl.CostEstimate(
            flops=10 * group * depth * units, bytes_accessed=80 * 2**20, transcendentals=0
        ),
        compiler_params=params(4),
    )(slope_gate, slope_up, cot_all, gathered, state, cotangent, gain, w_down, w_gate, w_up)


def attend_back_kernel(
    grad_mixed, query, key, value, attended, log_total, start, cos_table, sin_table,
    tokens, gain, grad_state, gathered_in, w_out, w_query, w_key, w_value,
    grad_tokens_out, gain_out, grad_out_out, grad_qkv_out,
    mixed, out_buf, query_buf, key_buf, value_buf, gathered, grad_att, key_acc, value_acc, grads, part, slots,
    stage_out, got_out, stage_qkv, got_qkv,
    send_sem, recv_sem, sums_send, sums_recv, out_send, out_recv, qkv_send, qkv_recv, local_sem,
):
    peers = Peers()
    rows, depth = tokens.shape
    group, q_width = query.shape
    kv_heads = w_key.shape[1] // HD
    kv_raw = kv_heads * HD
    pairs_per_kv = q_width // LANES // kv_heads
    me = peers.at(0, 0)
    local = Local(local_sem)
    first_load = local.copy(grad_mixed, block(mixed, me, rows))
    load_out = local.copy(w_out, out_buf)
    loads = [
        local.copy(w_query, query_buf),
        local.copy(w_key, key_buf),
        local.copy(w_value, value_buf),
        local.copy(gathered_in, gathered),
    ]
    greet(peers, core=True)
    first_load.wait()
    waiting, saves = [load_out], []

    def use(index):
        while waiting:
            waiting.pop().wait()
        at = pl.ds(pl.multiple_of(index * rows, rows), rows)
        grad_att[at, :] = dot_nt(mixed[at, :], out_buf[...]).astype(BF16)

    gather_wire = Wire(send_sem, recv_sem)
    gather(peers, gather_wire, mixed, rows, use)

    columns = stage_out.shape[2]

    def out_tile(index, target, add):
        lanes = pl.ds(pl.multiple_of(index * columns, columns), columns)
        put(target, (slice(None), slice(None)), dot_tn(attended[...], mixed[:, lanes]), add)

    def out_save(k, ref):
        saves.append(local.copy(ref, grad_out_out.at[pl.ds(k * q_width, q_width)]))

    pairs = got_out.shape[0]
    Exchange(Wire(out_send, out_recv), stage_out, got_out).run(
        [(out_tile, out_save, k) for k in range(pairs)]
    )

    key_acc[...] = jnp.zeros_like(key_acc)
    value_acc[...] = jnp.zeros_like(value_acc)
    tile = 256
    for i in range(group // tile):
        keys = (i + 1) * tile

        def one_pair(pair, carry, i=i, keys=keys):
            at = pl.ds(i * tile, tile)
            lanes = pl.ds(pl.multiple_of(pair * LANES, LANES), LANES)
            kv_lanes = pl.ds(
                pl.multiple_of(lax.div(pair, np.int32(pairs_per_kv)) * LANES, LANES), LANES
            )
            both, grad_both = query[at, lanes], grad_att[at, lanes]
            key_rows, value_rows = key[0:keys, kv_lanes], value[0:keys, kv_lanes]
            first = first_head(tile)
            dots = grad_both.astype(F32) * attended[at, lanes].astype(F32)
            column = lax.broadcasted_iota(jnp.int32, (tile, keys), 1)
            row = lax.broadcasted_iota(jnp.int32, (tile, keys), 0) + i * tile
            allowed = (column >= start[at, :]) & (column <= row)
            grad_queries, grad_keys, grad_values = [], 0.0, 0.0
            for h in range(2):
                own = first if h == 0 else jnp.logical_not(first)
                own_query = jnp.where(own, both, jnp.zeros_like(both))
                own_grad = jnp.where(own, grad_both, jnp.zeros_like(grad_both))
                row_dot = jnp.sum(jnp.where(own, dots, 0.0), axis=-1, keepdims=True)
                scores = dot_nt(own_query, key_rows)
                probs = jnp.exp2(scores * SCALE2 - log_total[pair * 2 + h, at, :])
                probs = jnp.where(allowed, probs, 0.0)
                grad_probs = dot_nt(own_grad, value_rows)
                grad_scores = (probs * (grad_probs - row_dot)).astype(BF16)
                grad_queries.append(dot_nn(grad_scores, key_rows))
                grad_keys = grad_keys + dot_tn(grad_scores, own_query)
                grad_values = grad_values + dot_tn(probs.astype(BF16), own_grad)
            key_acc[0:keys, kv_lanes] += grad_keys
            value_acc[0:keys, kv_lanes] += grad_values
            turned = jnp.where(first, grad_queries[0], grad_queries[1]) * 0.125
            turned = turned * cos_table[at, :] - swap_halves(turned) * sin_table[at, :]
            grads[at, lanes] = turned.astype(BF16)
            return carry

        lax.fori_loop(0, q_width // LANES, one_pair, 0)

    def fold(k, carry):
        at = pl.ds(pl.multiple_of(k * 128, 128), 128)
        cos, sin = cos_table[at, :], sin_table[at, :]
        key_heads, value_heads = [], []
        for j in range(kv_heads):
            lanes = slice(j * LANES, (j + 1) * LANES)
            both = key_acc[at, lanes] * 0.125
            both = both + pltpu.roll(both, HD, 1)
            key_heads.append(both * cos - swap_halves(both) * sin)
            both = value_acc[at, lanes]
            value_heads.append(both + pltpu.roll(both, HD, 1))
        for heads, base in ((key_heads, q_width), (value_heads, q_width + kv_raw)):
            if kv_heads == 1:
                grads[at, base : base + HD] = heads[0][:, :HD].astype(BF16)
            for j in range(0, kv_heads - 1, 2):
                pair = jnp.where(first_head(128), heads[j], heads[j + 1])
                grads[at, base + j * HD : base + (j + 2) * HD] = pair.astype(BF16)
        return carry

    lax.fori_loop(0, group // 128, fold, 0)
    for load in loads:
        load.wait()

    def make(first, count):
        at = pl.ds(pl.multiple_of(first * rows, rows), count * rows)
        step = 1024
        for c in range(0, depth, step):
            inner = slice(c, c + step)
            total = dot_nt(grads[at, 0:q_width], query_buf[inner, :])
            total = total + dot_nt(grads[at, q_width : q_width + kv_raw], key_buf[inner, :])
            total = total + dot_nt(grads[at, q_width + kv_raw :], value_buf[inner, :])
            part[at, inner] = total.astype(BF16)

    deep = stage_qkv.shape[1]

    def qkv_tile(index, target, add):
        lanes = pl.ds(pl.multiple_of(index * deep, deep), deep)
        put(target, (slice(None), slice(None)), dot_tn(gathered[:, lanes], grads[...]), add)

    def qkv_save(k, ref):
        saves.append(local.copy(ref, grad_qkv_out.at[pl.ds(k * deep, deep)]))

    def weight_grads():
        Exchange(Wire(qkv_send, qkv_recv), stage_qkv, got_qkv).run(
            [(qkv_tile, qkv_save, k) for k in range(pairs)]
        )

    wire = Wire(sums_send, sums_recv)
    sums = scatter(peers, wire, part, slots, rows, make, weight_grads)
    gain_row = gain[...]
    half = rows // 2
    gain_out[...] = jnp.zeros_like(gain_out)
    for h in range(2):

        def finish(k, carry, h=h):
            inner = pl.ds(pl.multiple_of(k * 16, 16), 16)
            outer = pl.ds(pl.multiple_of(h * half + k * 16, 16), 16)
            grad_normed = sums[h][0][inner, :].astype(F32)
            for other in sums[h][1:]:
                grad_normed = grad_normed + other[inner, :].astype(F32)
            grad, gain_part = norm_back(tokens[outer, :].astype(F32), gain_row, grad_normed)
            gain_out[...] += fold_rows(gain_part)
            grad_tokens_out[outer, :] = (grad + grad_state[outer, :]).astype(BF16)
            return carry

        lax.fori_loop(0, half // 16, finish, 0)
    gather_wire.wait_sends()
    wire.wait_sends()
    for copy in saves:
        copy.wait()


def attend_back(
    grad_mixed, query, key, value, attended, log_total, start, cos_table, sin_table,
    tokens, gain, grad_state, gathered, w_out, w_query, w_key, w_value,
):
    n = lax.axis_size("tensor")
    pairs = lax.axis_size("dp") // 2
    rows, depth = tokens.shape
    group, q_width = query.shape
    kv_width, kv_raw = key.shape[1], w_key.shape[1]
    width = q_width + 2 * kv_raw
    deep = depth // (2 * pairs)
    dma = lambda count: pltpu.SemaphoreType.DMA((count,))
    return pl.pallas_call(
        attend_back_kernel,
        out_shape=(
            jax.ShapeDtypeStruct((rows, depth), BF16),
            jax.ShapeDtypeStruct((8, depth), F32),
            jax.ShapeDtypeStruct((pairs * q_width, deep), BF16),
            jax.ShapeDtypeStruct((pairs * deep, width), BF16),
        ),
        in_specs=[any_spec()] + [vmem_spec()] * 11 + [any_spec()] * 5,
        out_specs=(vmem_spec(), vmem_spec(), any_spec(), any_spec()),
        scratch_shapes=[
            pltpu.VMEM((group, depth), BF16),
            pltpu.VMEM(w_out.shape, BF16),
            pltpu.VMEM(w_query.shape, BF16),
            pltpu.VMEM(w_key.shape, BF16),
            pltpu.VMEM(w_value.shape, BF16),
            pltpu.VMEM((group, depth), BF16),
            pltpu.VMEM((group, q_width), BF16),
            pltpu.VMEM((group, kv_width), F32),
            pltpu.VMEM((group, kv_width), F32),
            pltpu.VMEM((group, width), BF16),
            pltpu.VMEM((group, depth), BF16),
            slots_for(n, rows, depth),
            pltpu.VMEM((2, q_width, deep), BF16),
            pltpu.VMEM((pairs, q_width, deep), BF16),
            pltpu.VMEM((2, deep, width), BF16),
            pltpu.VMEM((pairs, deep, width), BF16),
            *wires(n),
            *wires(n),
            dma(pairs), dma(pairs), dma(pairs), dma(pairs), dma(6 + 2 * pairs),
        ],
        cost_estimate=pl.CostEstimate(
            flops=2 * group * depth * q_width * 12, bytes_accessed=60 * 2**20, transcendentals=0
        ),
        compiler_params=params(5),
    )(grad_mixed, query, key, value, attended, log_total, start, cos_table, sin_table,
      tokens, gain, grad_state, gathered, w_out, w_query, w_key, w_value)


class GainSums:
    def __init__(self, gains, tiles, from_tensor, from_dp, wire, chunk):
        self.gains, self.tiles, self.from_tensor, self.from_dp = gains, tiles, from_tensor, from_dp
        self.wire, self.n, self.dps = wire, lax.axis_size("tensor"), lax.axis_size("dp")
        self.chunk = chunk
        self.me, self.dp = lax.axis_index("tensor"), lax.axis_index("dp")

    def tensor(self, step):
        return lax.rem(self.me + np.int32(step), np.int32(self.n))

    def data(self, step):
        return lax.rem(self.dp + np.int32(step), np.int32(self.dps))

    def greet(self):
        barrier = pltpu.get_barrier_semaphore()
        for step in range(1, self.n):
            device = {"tensor": self.tensor(step)}
            pl.semaphore_signal(barrier, inc=1, device_id=device, device_id_type=MESH)
        for step in range(1, self.dps):
            device = {"dp": self.data(step)}
            pl.semaphore_signal(barrier, inc=1, device_id=device, device_id_type=MESH)
        pl.semaphore_wait(barrier, self.n + self.dps - 2)

    def start(self):
        for t in range(self.n):
            for d in range(self.dps):
                lane = (d * self.n + t) * self.chunk // LANES * LANES
                for k, gain in enumerate(self.gains):
                    self.tiles[t, d, k] = gain[:, lane : lane + LANES]
        self.first = [
            self.wire.copy(
                self.tiles.at[self.tensor(step)],
                self.from_tensor.at[step - 1],
                {"tensor": self.tensor(step)},
            )
            for step in range(1, self.n)
        ]

    def forward(self):
        for copy in self.first:
            copy.wait_recv()
        total = self.tiles[self.me]
        for step in range(1, self.n):
            total = total + self.from_tensor[step - 1]
        self.from_tensor[0] = total
        self.second = [
            self.wire.copy(
                self.from_tensor.at[0, self.data(step)],
                self.from_dp.at[step - 1],
                {"dp": self.data(step)},
            )
            for step in range(1, self.dps)
        ]

    def finish(self, out):
        for copy in self.second:
            copy.wait_recv()
        total = self.from_tensor[0, self.dp]
        for step in range(1, self.dps):
            total = total + self.from_dp[step - 1]
        out[...] = total


def output_kernel(
    hidden_in, w_down, state, gain_one, gain_two,
    output, gains_out,
    hidden, down_buf, part, slots, tiles, from_tensor, from_dp,
    send_sem, recv_sem, gain_send, gain_recv, local_sem,
):
    peers = Peers()
    rows, depth = state.shape
    local = Local(local_sem)
    loads = [local.copy(hidden_in, hidden), local.copy(w_down, down_buf)]
    chunk = depth // (lax.axis_size("tensor") * lax.axis_size("dp"))
    gains = GainSums(
        (gain_one, gain_two), tiles, from_tensor, from_dp, Wire(gain_send, gain_recv), chunk
    )
    gains.greet()
    gains.start()
    for load in loads:
        load.wait()

    def make(first, count):
        at = pl.ds(pl.multiple_of(first * rows, rows), count * rows)
        step = 512

        def some(k, carry):
            lanes = pl.ds(pl.multiple_of(k * step, step), step)
            part[at, lanes] = dot_nn(hidden[at, :], down_buf[:, lanes]).astype(BF16)
            return carry

        lax.fori_loop(0, depth // step, some, 0)

    wire = Wire(send_sem, recv_sem)
    sums = scatter(peers, wire, part, slots, rows, make, gains.forward)
    half = rows // 2
    for h in range(2):

        def finish(k, carry, h=h):
            inner = pl.ds(pl.multiple_of(k * 16, 16), 16)
            outer = pl.ds(pl.multiple_of(h * half + k * 16, 16), 16)
            total = sums[h][0][inner, :].astype(F32)
            for other in sums[h][1:]:
                total = total + other[inner, :].astype(F32)
            output[outer, :] = (state[outer, :] + total).astype(BF16)
            return carry

        lax.fori_loop(0, half // 16, finish, 0)
    gains.finish(gains_out)
    wire.wait_sends()
    gains.wire.wait_sends()


def layer_output(hidden, w_down, state, gain_one, gain_two):
    n, dps = lax.axis_size("tensor"), lax.axis_size("dp")
    rows, depth = state.shape
    dma = lambda count: pltpu.SemaphoreType.DMA((count,))
    return pl.pallas_call(
        output_kernel,
        out_shape=(
            jax.ShapeDtypeStruct((rows, depth), BF16),
            jax.ShapeDtypeStruct((2, 8, LANES), F32),
        ),
        in_specs=[any_spec(), any_spec(), vmem_spec(), vmem_spec(), vmem_spec()],
        out_specs=(vmem_spec(), vmem_spec()),
        scratch_shapes=[
            pltpu.VMEM(hidden.shape, BF16),
            pltpu.VMEM(w_down.shape, BF16),
            pltpu.VMEM((hidden.shape[0], depth), BF16),
            slots_for(n, rows, depth),
            pltpu.VMEM((n, dps, 2, 8, LANES), F32),
            pltpu.VMEM((n - 1, dps, 2, 8, LANES), F32),
            pltpu.VMEM((dps - 1, 2, 8, LANES), F32),
            *wires(n),
            dma(n + dps - 2), dma(n + dps - 2), dma(2),
        ],
        cost_estimate=pl.CostEstimate(
            flops=2 * hidden.shape[0] * depth * hidden.shape[1],
            bytes_accessed=20 * 2**20,
            transcendentals=0,
        ),
        compiler_params=params(6),
    )(hidden, w_down, state, gain_one, gain_two)


def sum_over_chips(grads):
    size = lax.axis_size("dp")
    groups = [list(range(core, size, 2)) for core in range(2)]
    return lax.psum_scatter(
        grads, "dp", scatter_dimension=0, tiled=True, axis_index_groups=groups
    ).astype(F32)


def local(
    tokens, lengths, gain_one, w_query, w_key, w_value, w_out, gain_two, w_gate, w_up, w_down,
    cotangent,
):
    depth, group = tokens.shape[1], tokens.shape[0] * lax.axis_size("tensor")
    q_width, kv_raw, units = w_query.shape[1], w_key.shape[1], w_gate.shape[1]
    start, position = layout(lengths[0], group)
    start = start[:, None]
    cos_table, sin_table = rope_table(position)
    gain_one, gain_two = gain_one[None], gain_two[None]
    gathered_one, query, key, value = project(
        tokens, gain_one, cos_table, sin_table, w_query, w_key, w_value
    )
    attended, log_total, state, normed_two, cot_a, cot_b = attend(
        query, key, value, start, tokens, gain_two, w_out, cotangent
    )
    gathered_two, hidden, slope_gate, slope_up, cot_all, grad_down = hidden_units(
        normed_two, cotangent, cot_a, cot_b, w_gate, w_up
    )
    grad_w_down = sum_over_chips(grad_down)
    grad_state, grad_mixed, gain_two_part, grad_gate_up = hidden_back(
        slope_gate, slope_up, cot_all, gathered_two, state, cotangent, gain_two,
        w_down, w_gate, w_up,
    )
    grad_gate_up, grad_w_down = lax.optimization_barrier((grad_gate_up, grad_w_down))
    grad_w_gate_up = sum_over_chips(grad_gate_up)
    grad_tokens, gain_one_part, grad_out, grad_qkv = attend_back(
        grad_mixed, query, key, value, attended, log_total, start, cos_table, sin_table,
        tokens, gain_one, grad_state, gathered_one, w_out, w_query, w_key, w_value,
    )
    grad_out, grad_w_gate_up = lax.optimization_barrier((grad_out, grad_w_gate_up))
    grad_w_out = sum_over_chips(grad_out)
    grad_qkv, grad_w_out = lax.optimization_barrier((grad_qkv, grad_w_out))
    grad_w_qkv = sum_over_chips(grad_qkv)
    output, gains = layer_output(hidden, w_down, state, gain_one_part, gain_two_part)
    share = depth // (lax.axis_size("tensor") * lax.axis_size("dp"))
    place = lax.rem(
        (lax.axis_index("dp") * lax.axis_size("tensor") + lax.axis_index("tensor")) * share, LANES
    )
    gains = lax.dynamic_slice_in_dim(jnp.sum(gains, axis=1), place, share, axis=1)
    return (
        output,
        grad_tokens,
        gains[0],
        grad_w_qkv[:, :q_width],
        grad_w_qkv[:, q_width : q_width + kv_raw],
        grad_w_qkv[:, q_width + kv_raw :],
        grad_w_out,
        gains[1],
        grad_w_gate_up[:, :units],
        grad_w_gate_up[:, units:],
        grad_w_down,
    )


def solution(mesh):
    return jax.shard_map(
        local,
        mesh=mesh,
        in_specs=(
            P(("dp", "tensor"), None),
            P("dp", None),
            P(),
            P(None, "tensor"),
            P(None, "tensor"),
            P(None, "tensor"),
            P("tensor", None),
            P(),
            P(None, "tensor"),
            P(None, "tensor"),
            P("tensor", None),
            P(("dp", "tensor"), None),
        ),
        out_specs=(
            P(("dp", "tensor"), None),
            P(("dp", "tensor"), None),
            P(("dp", "tensor")),
            P("dp", "tensor"),
            P("dp", "tensor"),
            P("dp", "tensor"),
            P("tensor", "dp"),
            P(("dp", "tensor")),
            P("dp", "tensor"),
            P("dp", "tensor"),
            P("tensor", "dp"),
        ),
        check_vma=False,
    )
```

```python
import functools
import math

import jax
import jax.numpy as jnp
import numpy as np
from jax import lax
from jax.experimental import pallas as pl
from jax.experimental.pallas import tpu as pltpu
from jax.sharding import PartitionSpec as P

HD = 64
LANES = 128
EPSILON = 1e-05
MASKED = -1e30
LOG2E = math.log2(math.e)
SCALE2 = 0.125 * LOG2E
BF16 = jnp.bfloat16
F32 = jnp.float32
MESH = pl.DeviceIdType.MESH
VMEM_LIMIT = 60 * 2**20


def dot_nn(a, b):
    return jnp.dot(a, b, preferred_element_type=F32)


def dot_nt(a, b):
    return lax.dot_general(a, b, (((1,), (1,)), ((), ())), preferred_element_type=F32)


def dot_tn(a, b):
    return lax.dot_general(a, b, (((0,), (0,)), ((), ())), preferred_element_type=F32)


def place_tables(group):
    index = np.arange(HD // 2, dtype=np.float64)
    base = np.exp(-math.log(500000.0) * 2.0 * index / HD)
    wavelength = 2.0 * math.pi / base
    smooth = (8192.0 / wavelength - 1.0) / 3.0
    blended = (1.0 - smooth) * base / 32.0 + smooth * base
    frequency = np.where(
        wavelength < 2048.0, base, np.where(wavelength > 8192.0, base / 32.0, blended)
    )
    angles = np.arange(group, dtype=np.float64)[:, None] * frequency[None, :]
    cos_half, sin_half = np.cos(angles), np.sin(angles)
    return (
        np.concatenate([cos_half] * 4, axis=1).astype(np.float32),
        np.concatenate([-sin_half, sin_half, -sin_half, sin_half], axis=1).astype(np.float32),
    )


def ends_of(lengths):
    ends, end = [], 0
    for k in range(lengths.shape[1]):
        end = end + lengths[0, k]
        ends.append(end)
    return ends


def starts_of(places, ends):
    start = jnp.zeros_like(places)
    for end in ends:
        start = jnp.where(places >= end, end, start)
    return start


def turn_tables(ends, first, count, cos_place, sin_place):
    places = lax.broadcasted_iota(jnp.int32, (count, LANES), 0) + first
    cos_start, sin_start = jnp.ones((count, LANES), F32), jnp.zeros((count, LANES), F32)
    for end in ends:
        at = pl.ds(jnp.minimum(end, cos_place.shape[0] - 1), 1)
        cos_start = jnp.where(places >= end, cos_place[at, :], cos_start)
        sin_start = jnp.where(places >= end, sin_place[at, :], sin_start)
    rows = pl.ds(first, count)
    cos, sin = cos_place[rows, :], sin_place[rows, :]
    return cos * cos_start + sin * sin_start, sin * cos_start - cos * sin_start


class Peers:
    def __init__(self):
        self.n = lax.axis_size("tensor")
        self.m = self.n // 2
        index = lax.axis_index("tensor")
        self.y = lax.div(index, np.int32(self.m))
        self.x = lax.rem(index, np.int32(self.m))

    def at(self, flip, step):
        row = 1 - self.y if flip else self.y
        return row * self.m + lax.rem(self.x + np.int32(step + self.m), np.int32(self.m))

    def minor(self, step):
        return {"tensor": self.at(0, step)}

    def major(self):
        return {"tensor": self.at(1, 0)}

    def steps(self):
        return range(1, self.m)


def core_of():
    return lax.rem(lax.axis_index("dp"), np.int32(2))


def other_core():
    return {"dp": lax.axis_index("dp") + 1 - 2 * core_of()}


def greet(peers, core=False):
    barrier = pltpu.get_barrier_semaphore()
    for step in peers.steps():
        pl.semaphore_signal(barrier, inc=1, device_id=peers.minor(step), device_id_type=MESH)
    pl.semaphore_signal(barrier, inc=1, device_id=peers.major(), device_id_type=MESH)
    if core:
        pl.semaphore_signal(barrier, inc=1, device_id=other_core(), device_id_type=MESH)
    pl.semaphore_wait(barrier, peers.m + (1 if core else 0))


class Wire:
    def __init__(self, send_sem, recv_sem):
        self.send_sem, self.recv_sem, self.copies = send_sem, recv_sem, []

    def copy(self, source, target, device):
        k = len(self.copies)
        copy = pltpu.make_async_remote_copy(
            src_ref=source,
            dst_ref=target,
            send_sem=self.send_sem.at[k],
            recv_sem=self.recv_sem.at[k],
            device_id=device,
            device_id_type=MESH,
        )
        copy.start()
        self.copies.append(copy)
        return copy

    def wait_sends(self):
        for copy in self.copies:
            copy.wait_send()


def wire_count(n):
    return 4 * (n // 2 - 1) + 2


def wires(n):
    return [pltpu.SemaphoreType.DMA((wire_count(n),))] * 2


class Local:
    def __init__(self, sem):
        self.sem, self.copies = sem, []

    def copy(self, source, target):
        copy = pltpu.make_async_copy(source, target, self.sem.at[len(self.copies)])
        copy.start()
        self.copies.append(copy)
        return copy


def block(ref, index, rows):
    return ref.at[pl.ds(pl.multiple_of(index * rows, rows), rows)]


def half_block(ref, index, rows, half):
    size = rows // 2
    return ref.at[pl.ds(pl.multiple_of(index * rows + half * size, size), size)]


def gather(peers, wire, buf, rows):
    steps, half = list(peers.steps()), rows // 2
    part = lambda index, side: half_block(buf, index, rows, side)
    span = lambda index, side: (pl.multiple_of(index * rows + side * half, half), half)
    me, major = peers.at(0, 0), peers.at(1, 0)
    send = lambda ref, device: wire.copy(ref, ref, device)
    minor_a = [send(part(me, 0), peers.minor(j)) for j in steps]
    major_b = send(part(me, 1), peers.major())
    minor_b = [send(part(me, 1), peers.minor(j)) for j in steps]
    major_a = send(part(me, 0), peers.major())
    yield [(pl.multiple_of(me * rows, rows), rows)]
    forward = []
    for j, copy in zip(steps, minor_a):
        copy.wait_recv()
        forward.append(send(part(peers.at(0, -j), 0), peers.major()))
    major_b.wait_recv()
    forward += [send(part(major, 1), peers.minor(j)) for j in steps]
    yield [span(peers.at(0, -j), 0) for j in steps] + [span(major, 1)]
    for copy in (*minor_b, major_a):
        copy.wait_recv()
    yield [span(peers.at(0, -j), 1) for j in steps] + [span(major, 0)]
    for copy in forward:
        copy.wait_recv()
    yield [(pl.multiple_of(peers.at(1, -j) * rows, rows), rows) for j in steps]


def load_rows(ref, spans):
    return jnp.concatenate([ref[pl.ds(first, count), :] for first, count in spans], axis=0)


def store_rows(ref, spans, lanes, value):
    at = 0
    for first, count in spans:
        ref[pl.ds(first, count), lanes] = value[at : at + count]
        at += count


def add_rows(target, others, size):
    def some(k, carry):
        at = pl.ds(pl.multiple_of(k * 16, 16), 16)
        total = target[at, :].astype(F32)
        for other in others:
            total = total + other[at, :].astype(F32)
        target[at, :] = total.astype(target.dtype)
        return carry

    lax.fori_loop(0, size // 16, some, 0)


def scatter(peers, wire, part_ref, slots, rows, make, meanwhile=None):
    steps = list(peers.steps())
    part = lambda index, half: half_block(part_ref, index, rows, half)
    me, major = peers.at(0, 0), peers.at(1, 0)
    count = len(steps)
    via_a, via_b, direct_b, sum_a = (
        [slots.at[group * count + k] for k in range(count)] for group in range(4)
    )
    direct_a, sum_b = slots.at[4 * count], slots.at[4 * count + 1]
    make((1 - peers.y) * peers.m, peers.m)
    first_a, first_b = [], []
    for k, j in enumerate(steps):
        index = peers.at(1, j)
        first_a.append(wire.copy(part(index, 0), via_a[k], peers.major()))
        first_b.append(wire.copy(part(index, 1), via_b[k], peers.minor(j)))
    plain_a = wire.copy(part(major, 0), direct_a, peers.major())
    make(peers.y * peers.m, peers.m)
    plain_b = [
        wire.copy(part(peers.at(0, j), 1), direct_b[k], peers.minor(j))
        for k, j in enumerate(steps)
    ]
    done_a = []
    for k, j in enumerate(steps):
        first_a[k].wait_recv()
        target = part(peers.at(0, j), 0)
        add_rows(target, [via_a[k]], rows // 2)
        done_a.append(wire.copy(target, sum_a[k], peers.minor(j)))
    for copy in first_b:
        copy.wait_recv()
    target = part(major, 1)
    add_rows(target, via_b, rows // 2)
    done_b = wire.copy(target, sum_b, peers.major())
    if meanwhile is not None:
        meanwhile()
    for copy in (plain_a, *plain_b, *done_a, done_b):
        copy.wait_recv()
    return (
        (part(me, 0), direct_a, *sum_a),
        (part(me, 1), sum_b, *direct_b),
    )


def slots_for(n, rows, width):
    return pltpu.VMEM((wire_count(n), rows // 2, width), BF16)


def lane_of(rows, width=LANES):
    return lax.broadcasted_iota(jnp.int32, (rows, width), 1)


def first_head(rows):
    return lane_of(rows) < HD


def swap_halves(values):
    first = lax.rem(lane_of(values.shape[0]), np.int32(HD)) < HD // 2
    return jnp.where(first, pltpu.roll(values, LANES - HD // 2, 1), pltpu.roll(values, HD // 2, 1))


def doubled(pair, heads):
    if heads == 1:
        return [jnp.concatenate([pair, pair], axis=1)]
    out = []
    for k in range(heads // 2):
        both = pair[:, k * LANES : (k + 1) * LANES]
        swapped = pltpu.roll(both, HD, 1)
        first = first_head(both.shape[0])
        out += [jnp.where(first, both, swapped), jnp.where(first, swapped, both)]
    return out


def project_kernel(
    lengths, tokens, gain, cos_place, sin_place, w_query, w_key, w_value,
    gathered_out, query_out, key_out, value_out, cos_out, sin_out,
    gathered, weights, raw_key, raw_value, send_sem, recv_sem, local_sem,
):
    peers = Peers()
    rows, depth = tokens.shape
    group = gathered.shape[0]
    q_width, kv_heads = w_query.shape[1], w_key.shape[1] // HD
    kv_width = kv_heads * LANES
    local = Local(local_sem)
    loads = [
        local.copy(w_key, raw_key),
        local.copy(w_value, raw_value),
        local.copy(w_query, weights.at[:, pl.ds(0, q_width)]),
    ]
    me = peers.at(0, 0)
    gain_row = gain[...]

    def normalize(k, carry):
        values = tokens[pl.ds(pl.multiple_of(k * 16, 16), 16), :].astype(F32)
        scale = lax.rsqrt(jnp.mean(values * values, axis=-1, keepdims=True) + EPSILON)
        gathered[pl.ds(pl.multiple_of(me * rows + k * 16, 16), 16), :] = (
            values * scale * gain_row
        ).astype(BF16)
        return carry

    lax.fori_loop(0, rows // 16, normalize, 0)
    greet(peers)

    def prepare():
        ends = ends_of(lengths)

        def turn(k, carry):
            first = pl.multiple_of(k * 128, 128)
            cos, sin = turn_tables(ends, first, 128, cos_place, sin_place)
            cos_out[pl.ds(first, 128), :] = cos
            sin_out[pl.ds(first, 128), :] = sin
            return carry

        lax.fori_loop(0, group // 128, turn, 0)
        for load in loads:
            load.wait()

        def some(k, carry):
            at = pl.ds(pl.multiple_of(k * 128, 128), 128)
            for raw, base in ((raw_key, q_width), (raw_value, q_width + kv_width)):
                for j, twice in enumerate(doubled(raw[at, :].astype(F32), kv_heads)):
                    weights[at, base + j * LANES : base + (j + 1) * LANES] = twice.astype(BF16)
            return carry

        lax.fori_loop(0, depth // 128, some, 0)

    wire = Wire(send_sem, recv_sem)
    for step, spans in enumerate(gather(peers, wire, gathered, rows)):
        if step == 0:
            prepare()
        if step == 3:
            save = local.copy(gathered, gathered_out)
        cos, sin = load_rows(cos_out, spans), load_rows(sin_out, spans)
        normed = load_rows(gathered, spans)
        for base, width, out, turned in (
            (0, q_width, query_out, True),
            (q_width, kv_width, key_out, True),
            (q_width + kv_width, kv_width, value_out, False),
        ):
            raw = dot_nn(normed, weights[:, base : base + width])
            for c in range(0, width, LANES):
                piece = raw[:, c : c + LANES]
                if turned:
                    piece = piece * cos + swap_halves(piece) * sin
                store_rows(out, spans, slice(c, c + LANES), piece.astype(BF16))
    wire.wait_sends()
    save.wait()


def any_spec():
    return pl.BlockSpec(memory_space=pl.ANY)


def vmem_spec():
    return pl.BlockSpec(memory_space=pltpu.VMEM)


def params(collective_id):
    return pltpu.CompilerParams(
        collective_id=collective_id, has_side_effects=True, vmem_limit_bytes=VMEM_LIMIT
    )


def smem_spec():
    return pl.BlockSpec(memory_space=pltpu.SMEM)


def project(lengths, tokens, gain, w_query, w_key, w_value):
    n = lax.axis_size("tensor")
    rows, depth = tokens.shape
    group = rows * n
    q_width, kv_raw = w_query.shape[1], w_key.shape[1]
    kv_width = kv_raw // HD * LANES
    return pl.pallas_call(
        project_kernel,
        out_shape=(
            jax.ShapeDtypeStruct((group, depth), BF16),
            jax.ShapeDtypeStruct((group, q_width), BF16),
            jax.ShapeDtypeStruct((group, kv_width), BF16),
            jax.ShapeDtypeStruct((group, kv_width), BF16),
            jax.ShapeDtypeStruct((group, LANES), F32),
            jax.ShapeDtypeStruct((group, LANES), F32),
        ),
        in_specs=[smem_spec()] + [vmem_spec()] * 4 + [any_spec()] * 3,
        out_specs=(any_spec(),) + (vmem_spec(),) * 5,
        scratch_shapes=[
            pltpu.VMEM((group, depth), BF16),
            pltpu.VMEM((depth, q_width + 2 * kv_width), BF16),
            pltpu.VMEM((depth, kv_raw), BF16),
            pltpu.VMEM((depth, kv_raw), BF16),
            *wires(n),
            pltpu.SemaphoreType.DMA((4,)),
        ],
        cost_estimate=pl.CostEstimate(
            flops=2 * group * depth * (q_width + 2 * kv_width),
            bytes_accessed=40 * 2**20,
            transcendentals=0,
        ),
        compiler_params=params(1),
    )(lengths, tokens, gain, *place_tables(group), w_query, w_key, w_value)


def attend_kernel(
    lengths, query, key, value, gain, tokens_in, w_out, cotangent,
    attended_out, log_out, state_out, normed_out, cot_a, cot_b,
    tokens, w_buf, attended, log_total, part, slots,
    send_sem, recv_sem, cot_send, cot_recv, local_sem,
):
    peers = Peers()
    rows, depth = tokens.shape
    group, q_width = query.shape
    pairs_per_kv = q_width // LANES // (key.shape[1] // LANES)
    ends = ends_of(lengths)
    local = Local(local_sem)
    loads = [local.copy(w_out, w_buf), local.copy(tokens_in, tokens)]
    greet(peers)
    log_total[...] = jnp.zeros_like(log_total)
    cot_wire = Wire(cot_send, cot_recv)
    for k, j in enumerate(peers.steps()):
        cot_wire.copy(half_block(cotangent, 0, rows, 0), cot_a.at[k], peers.minor(j))
    cot_wire.copy(half_block(cotangent, 0, rows, 1), cot_b, peers.major())

    tile = 256
    for i in range(group // tile):
        keys = (i + 1) * tile

        def one_pair(pair, carry, i=i, keys=keys):
            at = pl.ds(i * tile, tile)
            lanes = pl.ds(pl.multiple_of(pair * LANES, LANES), LANES)
            kv_lanes = pl.ds(
                pl.multiple_of(lax.div(pair, np.int32(pairs_per_kv)) * LANES, LANES), LANES
            )
            both = query[at, lanes]
            key_rows, value_rows = key[0:keys, kv_lanes], value[0:keys, kv_lanes]
            first = first_head(tile)
            column = lax.broadcasted_iota(jnp.int32, (tile, keys), 1)
            row = lax.broadcasted_iota(jnp.int32, (tile, keys), 0) + i * tile
            start = starts_of(lax.broadcasted_iota(jnp.int32, (tile, 1), 0) + i * tile, ends)
            allowed = (column >= start) & (column <= row)
            logs = log_total[at, :]
            outs = []
            for h in range(2):
                own = first if h == 0 else jnp.logical_not(first)
                scores = dot_nt(jnp.where(own, both, jnp.zeros_like(both)), key_rows)
                scores = jnp.where(allowed, scores, MASKED)
                row_max = jnp.max(scores, axis=-1, keepdims=True)
                weights = jnp.exp2((scores - row_max) * SCALE2)
                row_sum = jnp.sum(weights, axis=-1, keepdims=True)
                outs.append(dot_nn(weights.astype(BF16), value_rows) / row_sum)
                logs = jnp.where(
                    lane_of(tile) == pair * 2 + h, row_max * SCALE2 + jnp.log2(row_sum), logs
                )
            log_total[at, :] = logs
            attended[at, lanes] = jnp.where(first, outs[0], outs[1]).astype(BF16)
            return carry

        lax.fori_loop(0, q_width // LANES, one_pair, 0)

    saves = [local.copy(attended, attended_out), local.copy(log_total, log_out)]
    for load in loads:
        load.wait()

    def make(first, count):
        at = pl.ds(pl.multiple_of(first * rows, rows), count * rows)
        heads = attended[at, :]
        for c in range(0, depth, 1024):
            part[at, c : c + 1024] = dot_nn(heads, w_buf[:, c : c + 1024]).astype(BF16)

    wire = Wire(send_sem, recv_sem)
    sums = scatter(peers, wire, part, slots, rows, make)
    gain_row = gain[...]
    half = rows // 2
    for h in range(2):

        def finish(k, carry, h=h):
            inner = pl.ds(pl.multiple_of(k * 16, 16), 16)
            outer = pl.ds(pl.multiple_of(h * half + k * 16, 16), 16)
            mixed = sums[h][0][inner, :].astype(F32)
            for other in sums[h][1:]:
                mixed = mixed + other[inner, :].astype(F32)
            state = tokens[outer, :].astype(F32) + mixed
            scale = lax.rsqrt(jnp.mean(state * state, axis=-1, keepdims=True) + EPSILON)
            state_out[outer, :] = state
            normed_out[outer, :] = (state * scale * gain_row).astype(BF16)
            return carry

        lax.fori_loop(0, half // 16, finish, 0)
    wire.wait_sends()
    for copy in (*cot_wire.copies, *saves):
        copy.wait()


def attend(lengths, query, key, value, tokens, gain, w_out, cotangent):
    n = lax.axis_size("tensor")
    rows, depth = tokens.shape
    group, q_width = query.shape
    m = n // 2
    return pl.pallas_call(
        attend_kernel,
        out_shape=(
            jax.ShapeDtypeStruct((group, q_width), BF16),
            jax.ShapeDtypeStruct((group, LANES), F32),
            jax.ShapeDtypeStruct((rows, depth), F32),
            jax.ShapeDtypeStruct((rows, depth), BF16),
            jax.ShapeDtypeStruct((m - 1, rows // 2, depth), BF16),
            jax.ShapeDtypeStruct((rows // 2, depth), BF16),
        ),
        in_specs=[smem_spec()] + [vmem_spec()] * 4 + [any_spec()] * 3,
        out_specs=(any_spec(), any_spec(), vmem_spec(), vmem_spec(), any_spec(), any_spec()),
        scratch_shapes=[
            pltpu.VMEM((rows, depth), BF16),
            pltpu.VMEM(w_out.shape, BF16),
            pltpu.VMEM((group, q_width), BF16),
            pltpu.VMEM((group, LANES), F32),
            pltpu.VMEM((group, depth), BF16),
            slots_for(n, rows, depth),
            *wires(n),
            pltpu.SemaphoreType.DMA((m,)),
            pltpu.SemaphoreType.DMA((m,)),
            pltpu.SemaphoreType.DMA((4,)),
        ],
        cost_estimate=pl.CostEstimate(
            flops=2 * group * depth * q_width * 4, bytes_accessed=40 * 2**20, transcendentals=0
        ),
        compiler_params=params(2),
    )(lengths, query, key, value, gain, tokens, w_out, cotangent)


class Exchange:
    def __init__(self, wire, stage, received):
        self.wire, self.stage, self.received, self.sent = wire, stage, received, []

    def run(self, jobs):
        mine = core_of()
        copies = []
        for k in range(len(jobs) + 1):
            if k < len(jobs):
                tile, save, pair = jobs[k]
                slot = self.stage.at[k % 2]
                if k >= 2:
                    copies[k - 2].wait_send()
                tile(2 * pair + 1 - mine, slot, False)
                copies.append(self.wire.copy(slot, self.received.at[k], other_core()))
            if k >= 1:
                tile, save, pair = jobs[k - 1]
                copies[k - 1].wait_recv()
                tile(2 * pair + mine, self.received.at[k - 1], True)
                save(pair, self.received.at[k - 1])
        for copy in copies[-2:]:
            copy.wait_send()


def put(target, at, value, add):
    if add:
        value = value + target[at].astype(F32)
    target[at] = value.astype(BF16)


def hidden_kernel(
    normed, cotangent, cot_a, cot_b, w_gate, w_up,
    gathered_out, hidden_out, slope_gate_out, slope_up_out, cot_out, grad_down_out,
    gathered, gate_buf, up_buf, hidden, slope_gate, slope_up, cot, stage, received,
    send_sem, recv_sem, cot_send, cot_recv, core_send, core_recv, local_sem,
):
    peers = Peers()
    rows, depth = normed.shape
    units = w_gate.shape[1]
    me, major = peers.at(0, 0), peers.at(1, 0)
    local = Local(local_sem)
    first_load = local.copy(normed, block(gathered, me, rows))
    loads = [local.copy(w_gate, gate_buf), local.copy(w_up, up_buf)]
    cot_loads = [local.copy(cotangent, block(cot, me, rows))]
    for k, j in enumerate(peers.steps()):
        cot_loads.append(local.copy(cot_a.at[k], half_block(cot, peers.at(0, -j), rows, 0)))
    cot_loads.append(local.copy(cot_b, half_block(cot, major, rows, 1)))
    greet(peers, core=True)
    first_load.wait()

    def use(spans):
        tile = 512

        def some(k, carry):
            lanes = pl.ds(pl.multiple_of(k * tile, tile), tile)
            x = load_rows(gathered, spans)
            gate = dot_nn(x, gate_buf[:, lanes])
            up = dot_nn(x, up_buf[:, lanes])
            sigmoid = jax.nn.sigmoid(gate)
            silu = gate * sigmoid
            slope = up * sigmoid * (1.0 + gate * (1.0 - sigmoid))
            store_rows(hidden, spans, lanes, (silu * up).astype(BF16))
            store_rows(slope_up, spans, lanes, silu.astype(BF16))
            store_rows(slope_gate, spans, lanes, slope.astype(BF16))
            return carry

        lax.fori_loop(0, units // tile, some, 0)

    cot_wire = Wire(cot_send, cot_recv)
    rest = ([], [])
    width = depth // 2

    def send_rest():
        for load in cot_loads:
            load.wait()
        for side in range(2):
            lanes = pl.ds(side * width, width)

            def send(index, half, device):
                ref = half_block(cot, index, rows, half).at[:, lanes]
                rest[side].append(cot_wire.copy(ref, ref, device))

            for j in peers.steps():
                send(me, 1, peers.minor(j))
                send(major, 1, peers.minor(j))
            send(me, 0, peers.major())
            for j in peers.steps():
                send(peers.at(0, -j), 0, peers.major())

    wire = Wire(send_sem, recv_sem)
    for step, spans in enumerate(gather(peers, wire, gathered, rows)):
        if step == 0:
            for load in loads:
                load.wait()
        if step == 3:
            send_rest()
        use(spans)
    saves = [
        local.copy(gathered, gathered_out),
        local.copy(hidden, hidden_out),
        local.copy(slope_gate, slope_gate_out),
        local.copy(slope_up, slope_up_out),
    ]
    columns = stage.shape[2]
    pairs = received.shape[0]
    arrived = set()

    def tile_of(side):
        def tile(index, target, add):
            if side not in arrived:
                arrived.add(side)
                for copy in rest[side]:
                    copy.wait_recv()
            lanes = pl.ds(pl.multiple_of(index * columns, columns), columns)
            step = 512

            def some(k, carry):
                at = pl.ds(pl.multiple_of(k * step, step), step)
                put(target, (at, slice(None)), dot_tn(hidden[:, at], cot[:, lanes]), add)
                return carry

            lax.fori_loop(0, units // step, some, 0)

        return tile

    def save(k, ref):
        saves.append(local.copy(ref, grad_down_out.at[pl.ds(k * units, units)]))

    Exchange(Wire(core_send, core_recv), stage, received).run(
        [(tile_of(2 * k // pairs), save, k) for k in range(pairs)]
    )
    saves.append(local.copy(cot, cot_out))
    wire.wait_sends()
    cot_wire.wait_sends()
    for copy in saves:
        copy.wait()


def hidden_units(normed, cotangent, cot_a, cot_b, w_gate, w_up):
    n = lax.axis_size("tensor")
    pairs = lax.axis_size("dp") // 2
    rows, depth = normed.shape
    group, units, columns = rows * n, w_gate.shape[1], depth // (2 * pairs)
    wide = lambda width: jax.ShapeDtypeStruct((group, width), BF16)
    return pl.pallas_call(
        hidden_kernel,
        out_shape=(
            wide(depth), wide(units), wide(units), wide(units), wide(depth),
            jax.ShapeDtypeStruct((pairs * units, columns), BF16),
        ),
        in_specs=[any_spec()] * 6,
        out_specs=(any_spec(),) * 6,
        scratch_shapes=[
            pltpu.VMEM((group, depth), BF16),
            pltpu.VMEM((depth, units), BF16),
            pltpu.VMEM((depth, units), BF16),
            pltpu.VMEM((group, units), BF16),
            pltpu.VMEM((group, units), BF16),
            pltpu.VMEM((group, units), BF16),
            pltpu.VMEM((group, depth), BF16),
            pltpu.VMEM((2, units, columns), BF16),
            pltpu.VMEM((pairs, units, columns), BF16),
            *wires(n),
            pltpu.SemaphoreType.DMA((2 * wire_count(n),)),
            pltpu.SemaphoreType.DMA((2 * wire_count(n),)),
            pltpu.SemaphoreType.DMA((pairs,)),
            pltpu.SemaphoreType.DMA((pairs,)),
            pltpu.SemaphoreType.DMA((3 + n // 2 + 1 + 5 + pairs,)),
        ],
        cost_estimate=pl.CostEstimate(
            flops=6 * group * depth * units, bytes_accessed=60 * 2**20, transcendentals=0
        ),
        compiler_params=params(3),
    )(normed, cotangent, cot_a, cot_b, w_gate, w_up)


def norm_back(values, gain_row, grad_normed):
    scale = lax.rsqrt(jnp.mean(values * values, axis=-1, keepdims=True) + EPSILON)
    unit = values * scale
    scaled = grad_normed * gain_row
    grad = scale * (scaled - unit * jnp.mean(scaled * unit, axis=-1, keepdims=True))
    return grad, grad_normed * unit


def fold_rows(values):
    return values[:8] + values[8:]


def hidden_back_kernel(
    slope_gate, slope_up, cot_all, gathered_in, state, cotangent, gain, w_down, w_gate, w_up,
    grad_state_out, grad_mixed_out, gain_out, grad_gate_up_out,
    gate_buf, up_buf, down_buf, grad_gate, grad_up, cot, part, slots, stage, received,
    send_sem, recv_sem, core_send, core_recv, local_sem,
):
    peers = Peers()
    rows, depth = state.shape
    group, units = slope_gate.shape
    chunk = down_buf.shape[1]
    chunks = units // chunk
    local = Local(local_sem)
    load_cot = local.copy(cot_all, cot)

    def load_down(k):
        source = w_down.at[pl.ds(k % chunks * chunk, chunk)]
        return local.copy(source, down_buf.at[k % 2])

    downs = [load_down(0)]
    slopes = [local.copy(slope_gate, grad_gate), local.copy(slope_up, grad_up)]
    downs.append(load_down(1))
    greet(peers, core=True)
    later = []

    def make(first, count):
        at = pl.ds(pl.multiple_of(first * rows, rows), count * rows)
        base = chunks if later else 0
        for c in range(chunks):
            downs[base + c].wait()
            if not later:
                load_cot.wait()
                for load in slopes:
                    load.wait()
                later.extend(
                    [
                        local.copy(w_gate, gate_buf),
                        local.copy(w_up, up_buf),
                        local.copy(state, grad_state_out),
                    ]
                )
            lanes = slice(c * chunk, (c + 1) * chunk)
            grad_hidden = dot_nt(cot[at, :], down_buf[c % 2])
            grad_gate[at, lanes] = (grad_hidden * grad_gate[at, lanes].astype(F32)).astype(BF16)
            grad_up[at, lanes] = (grad_hidden * grad_up[at, lanes].astype(F32)).astype(BF16)
            if base + c + 2 < 2 * chunks:
                downs.append(load_down(base + c + 2))
        if base == 0:
            for load in later[:2]:
                load.wait()
        else:
            later.append(local.copy(gathered_in, cot))
        step = 512

        def some(k, carry):
            inner = pl.ds(pl.multiple_of(k * step, step), step)
            total = dot_nt(grad_gate[at, :], gate_buf[inner, :])
            total = total + dot_nt(grad_up[at, :], up_buf[inner, :])
            part[at, inner] = total.astype(BF16)
            return carry

        lax.fori_loop(0, depth // step, some, 0)

    deep = stage.shape[1]
    saves = []

    def tile_of(grad):
        def tile(index, target, add):
            lanes = pl.ds(pl.multiple_of(index * deep, deep), deep)
            step = min(1024, units)

            def some(k, carry):
                inner = pl.ds(pl.multiple_of(k * step, step), step)
                put(target, (slice(None), inner), dot_tn(cot[:, lanes], grad[:, inner]), add)
                return carry

            lax.fori_loop(0, units // step, some, 0)

        return tile

    def save_at(base):
        def save(k, ref):
            target = grad_gate_up_out.at[pl.ds(k * deep, deep), pl.ds(base, units)]
            saves.append(local.copy(ref, target))

        return save

    def weight_grads():
        later[3].wait()
        pairs = received.shape[0] // 2
        Exchange(Wire(core_send, core_recv), stage, received).run(
            [(tile_of(grad_gate), save_at(0), k) for k in range(pairs)]
            + [(tile_of(grad_up), save_at(units), k) for k in range(pairs)]
        )

    wire = Wire(send_sem, recv_sem)
    sums = scatter(peers, wire, part, slots, rows, make, weight_grads)
    later[2].wait()
    gain_row = gain[...]
    half = rows // 2
    gain_out[...] = jnp.zeros_like(gain_out)
    for h in range(2):

        def finish(k, carry, h=h):
            inner = pl.ds(pl.multiple_of(k * 16, 16), 16)
            outer = pl.ds(pl.multiple_of(h * half + k * 16, 16), 16)
            grad_normed = sums[h][0][inner, :].astype(F32)
            for other in sums[h][1:]:
                grad_normed = grad_normed + other[inner, :].astype(F32)
            grad, gain_part = norm_back(grad_state_out[outer, :], gain_row, grad_normed)
            grad = grad + cotangent[outer, :].astype(F32)
            gain_out[...] += fold_rows(gain_part)
            grad_state_out[outer, :] = grad
            grad_mixed_out[outer, :] = grad.astype(BF16)
            return carry

        lax.fori_loop(0, half // 16, finish, 0)
    wire.wait_sends()
    for copy in saves:
        copy.wait()


def hidden_back(
    slope_gate, slope_up, cot_all, gathered, state, cotangent, gain, w_down, w_gate, w_up
):
    n = lax.axis_size("tensor")
    pairs = lax.axis_size("dp") // 2
    rows, depth = state.shape
    group, units = slope_gate.shape
    deep = depth // (2 * pairs)
    chunk = 512
    return pl.pallas_call(
        hidden_back_kernel,
        out_shape=(
            jax.ShapeDtypeStruct((rows, depth), F32),
            jax.ShapeDtypeStruct((rows, depth), BF16),
            jax.ShapeDtypeStruct((8, depth), F32),
            jax.ShapeDtypeStruct((pairs * deep, 2 * units), BF16),
        ),
        in_specs=[any_spec()] * 5 + [vmem_spec()] * 2 + [any_spec()] * 3,
        out_specs=(vmem_spec(), vmem_spec(), vmem_spec(), any_spec()),
        scratch_shapes=[
            pltpu.VMEM((depth, units), BF16),
            pltpu.VMEM((depth, units), BF16),
            pltpu.VMEM((2, chunk, depth), BF16),
            pltpu.VMEM((group, units), BF16),
            pltpu.VMEM((group, units), BF16),
            pltpu.VMEM((group, depth), BF16),
            pltpu.VMEM((group, depth), BF16),
            slots_for(n, rows, depth),
            pltpu.VMEM((2, deep, units), BF16),
            pltpu.VMEM((2 * pairs, deep, units), BF16),
            *wires(n),
            pltpu.SemaphoreType.DMA((2 * pairs,)),
            pltpu.SemaphoreType.DMA((2 * pairs,)),
            pltpu.SemaphoreType.DMA((7 + 2 * (units // chunk) + 2 * pairs,)),
        ],
        cost_estimate=pl.CostEstimate(
            flops=10 * group * depth * units, bytes_accessed=80 * 2**20, transcendentals=0
        ),
        compiler_params=params(4),
    )(slope_gate, slope_up, cot_all, gathered, state, cotangent, gain, w_down, w_gate, w_up)


def attend_back_kernel(
    lengths, gain, grad_mixed, query_in, key_in, value_in, attended_in, log_in, cos_in, sin_in,
    tokens_in, state_in, gathered_in, w_out, w_query, w_key, w_value,
    grad_tokens_out, gain_out, grads_out,
    query, key, value, attended, log_total, cos_table, sin_table, tokens, grad_state,
    mixed, out_buf, query_buf, key_buf, value_buf, gathered, grad_att, key_acc, value_acc, grads, part, slots,
    stage_out, got_out, stage_qkv, got_qkv,
    send_sem, recv_sem, sums_send, sums_recv, out_send, out_recv, qkv_send, qkv_recv, local_sem,
):
    peers = Peers()
    rows, depth = tokens.shape
    group, q_width = query.shape
    kv_heads = w_key.shape[1] // HD
    kv_raw = kv_heads * HD
    pairs_per_kv = q_width // LANES // kv_heads
    me = peers.at(0, 0)
    local = Local(local_sem)
    first_load = local.copy(grad_mixed, block(mixed, me, rows))
    load_out = local.copy(w_out, out_buf)
    sources = (
        query_in, key_in, value_in, attended_in, log_in, cos_in, sin_in, tokens_in, state_in
    )
    buffers = (query, key, value, attended, log_total, cos_table, sin_table, tokens, grad_state)
    loads = [local.copy(source, buffer) for source, buffer in zip(sources, buffers)]
    loads += [
        local.copy(w_query, query_buf),
        local.copy(w_key, key_buf),
        local.copy(w_value, value_buf),
        local.copy(gathered_in, gathered),
    ]
    greet(peers, core=True)
    first_load.wait()
    ends, saves = ends_of(lengths), []
    gather_wire = Wire(send_sem, recv_sem)
    for step, spans in enumerate(gather(peers, gather_wire, mixed, rows)):
        if step == 0:
            load_out.wait()
        grad_rows = dot_nt(load_rows(mixed, spans), out_buf[...]).astype(BF16)
        store_rows(grad_att, spans, slice(None), grad_rows)

    for load in loads:
        load.wait()
    columns = stage_out.shape[2]

    def out_tile(index, target, add):
        lanes = pl.ds(pl.multiple_of(index * columns, columns), columns)
        put(target, (slice(None), slice(None)), dot_tn(attended[...], mixed[:, lanes]), add)

    pairs = got_out.shape[0]
    width = grads.shape[1]

    def out_save(k, ref):
        for c in range(q_width // columns):
            target = grads_out.at[
                pl.ds(k * columns, columns), pl.ds(width + c * columns, columns)
            ]
            saves.append(local.copy(ref.at[pl.ds(c * columns, columns)], target))

    Exchange(Wire(out_send, out_recv), stage_out, got_out).run(
        [(out_tile, out_save, k) for k in range(pairs)]
    )

    key_acc[...] = jnp.zeros_like(key_acc)
    value_acc[...] = jnp.zeros_like(value_acc)
    tile = 256
    for i in range(group // tile):
        keys = (i + 1) * tile

        def one_pair(pair, carry, i=i, keys=keys):
            at = pl.ds(i * tile, tile)
            lanes = pl.ds(pl.multiple_of(pair * LANES, LANES), LANES)
            kv_lanes = pl.ds(
                pl.multiple_of(lax.div(pair, np.int32(pairs_per_kv)) * LANES, LANES), LANES
            )
            both, grad_both = query[at, lanes], grad_att[at, lanes]
            key_rows, value_rows = key[0:keys, kv_lanes], value[0:keys, kv_lanes]
            first = first_head(tile)
            dots = grad_both.astype(F32) * attended[at, lanes].astype(F32)
            column = lax.broadcasted_iota(jnp.int32, (tile, keys), 1)
            row = lax.broadcasted_iota(jnp.int32, (tile, keys), 0) + i * tile
            start = starts_of(lax.broadcasted_iota(jnp.int32, (tile, 1), 0) + i * tile, ends)
            allowed = (column >= start) & (column <= row)
            logs = log_total[at, :]
            grad_queries, grad_keys, grad_values = [], 0.0, 0.0
            for h in range(2):
                own = first if h == 0 else jnp.logical_not(first)
                own_query = jnp.where(own, both, jnp.zeros_like(both))
                own_grad = jnp.where(own, grad_both, jnp.zeros_like(grad_both))
                row_dot = jnp.sum(jnp.where(own, dots, 0.0), axis=-1, keepdims=True)
                scores = dot_nt(own_query, key_rows)
                log_row = jnp.sum(
                    jnp.where(lane_of(tile) == pair * 2 + h, logs, 0.0), axis=-1, keepdims=True
                )
                probs = jnp.exp2(scores * SCALE2 - log_row)
                probs = jnp.where(allowed, probs, 0.0)
                grad_probs = dot_nt(own_grad, value_rows)
                grad_scores = (probs * (grad_probs - row_dot)).astype(BF16)
                grad_queries.append(dot_nn(grad_scores, key_rows))
                grad_keys = grad_keys + dot_tn(grad_scores, own_query)
                grad_values = grad_values + dot_tn(probs.astype(BF16), own_grad)
            key_acc[0:keys, kv_lanes] += grad_keys
            value_acc[0:keys, kv_lanes] += grad_values
            turned = jnp.where(first, grad_queries[0], grad_queries[1]) * 0.125
            turned = turned * cos_table[at, :] - swap_halves(turned) * sin_table[at, :]
            grads[at, lanes] = turned.astype(BF16)
            return carry

        lax.fori_loop(0, q_width // LANES, one_pair, 0)

    def fold(k, carry):
        at = pl.ds(pl.multiple_of(k * 128, 128), 128)
        cos, sin = cos_table[at, :], sin_table[at, :]
        key_heads, value_heads = [], []
        for j in range(kv_heads):
            lanes = slice(j * LANES, (j + 1) * LANES)
            both = key_acc[at, lanes] * 0.125
            both = both + pltpu.roll(both, HD, 1)
            key_heads.append(both * cos - swap_halves(both) * sin)
            both = value_acc[at, lanes]
            value_heads.append(both + pltpu.roll(both, HD, 1))
        for heads, base in ((key_heads, q_width), (value_heads, q_width + kv_raw)):
            if kv_heads == 1:
                grads[at, base : base + HD] = heads[0][:, :HD].astype(BF16)
            for j in range(0, kv_heads - 1, 2):
                pair = jnp.where(first_head(128), heads[j], heads[j + 1])
                grads[at, base + j * HD : base + (j + 2) * HD] = pair.astype(BF16)
        return carry

    lax.fori_loop(0, group // 128, fold, 0)

    def make(first, count):
        at = pl.ds(pl.multiple_of(first * rows, rows), count * rows)
        step = 1024
        for c in range(0, depth, step):
            inner = slice(c, c + step)
            total = dot_nt(grads[at, 0:q_width], query_buf[inner, :])
            total = total + dot_nt(grads[at, q_width : q_width + kv_raw], key_buf[inner, :])
            total = total + dot_nt(grads[at, q_width + kv_raw :], value_buf[inner, :])
            part[at, inner] = total.astype(BF16)

    deep = stage_qkv.shape[1]

    def qkv_tile(index, target, add):
        lanes = pl.ds(pl.multiple_of(index * deep, deep), deep)
        put(target, (slice(None), slice(None)), dot_tn(gathered[:, lanes], grads[...]), add)

    def qkv_save(k, ref):
        target = grads_out.at[pl.ds(k * deep, deep), pl.ds(0, width)]
        saves.append(local.copy(ref, target))

    def weight_grads():
        Exchange(Wire(qkv_send, qkv_recv), stage_qkv, got_qkv).run(
            [(qkv_tile, qkv_save, k) for k in range(pairs)]
        )

    wire = Wire(sums_send, sums_recv)
    sums = scatter(peers, wire, part, slots, rows, make, weight_grads)
    gain_row = gain[...]
    half = rows // 2
    gain_out[...] = jnp.zeros_like(gain_out)
    for h in range(2):

        def finish(k, carry, h=h):
            inner = pl.ds(pl.multiple_of(k * 16, 16), 16)
            outer = pl.ds(pl.multiple_of(h * half + k * 16, 16), 16)
            grad_normed = sums[h][0][inner, :].astype(F32)
            for other in sums[h][1:]:
                grad_normed = grad_normed + other[inner, :].astype(F32)
            grad, gain_part = norm_back(tokens[outer, :].astype(F32), gain_row, grad_normed)
            gain_out[...] += fold_rows(gain_part)
            grad_tokens_out[outer, :] = (grad + grad_state[outer, :]).astype(BF16)
            return carry

        lax.fori_loop(0, half // 16, finish, 0)
    gather_wire.wait_sends()
    wire.wait_sends()
    for copy in saves:
        copy.wait()


def attend_back(
    lengths, grad_mixed, query, key, value, attended, log_total, cos_table, sin_table,
    tokens, gain, grad_state, gathered, w_out, w_query, w_key, w_value,
):
    n = lax.axis_size("tensor")
    pairs = lax.axis_size("dp") // 2
    rows, depth = tokens.shape
    group, q_width = query.shape
    kv_width, kv_raw = key.shape[1], w_key.shape[1]
    width = q_width + 2 * kv_raw
    deep = depth // (2 * pairs)
    dma = lambda count: pltpu.SemaphoreType.DMA((count,))
    return pl.pallas_call(
        attend_back_kernel,
        out_shape=(
            jax.ShapeDtypeStruct((rows, depth), BF16),
            jax.ShapeDtypeStruct((8, depth), F32),
            jax.ShapeDtypeStruct((pairs * deep, width + q_width), BF16),
        ),
        in_specs=[smem_spec(), vmem_spec()] + [any_spec()] * 15,
        out_specs=(vmem_spec(), vmem_spec(), any_spec()),
        scratch_shapes=[
            *[
                pltpu.VMEM(source.shape, source.dtype)
                for source in (
                    query, key, value, attended, log_total, cos_table, sin_table, tokens, grad_state
                )
            ],
            pltpu.VMEM((group, depth), BF16),
            pltpu.VMEM(w_out.shape, BF16),
            pltpu.VMEM(w_query.shape, BF16),
            pltpu.VMEM(w_key.shape, BF16),
            pltpu.VMEM(w_value.shape, BF16),
            pltpu.VMEM((group, depth), BF16),
            pltpu.VMEM((group, q_width), BF16),
            pltpu.VMEM((group, kv_width), F32),
            pltpu.VMEM((group, kv_width), F32),
            pltpu.VMEM((group, width), BF16),
            pltpu.VMEM((group, depth), BF16),
            slots_for(n, rows, depth),
            pltpu.VMEM((2, q_width, deep), BF16),
            pltpu.VMEM((pairs, q_width, deep), BF16),
            pltpu.VMEM((2, deep, width), BF16),
            pltpu.VMEM((pairs, deep, width), BF16),
            *wires(n),
            *wires(n),
            dma(pairs), dma(pairs), dma(pairs), dma(pairs), dma(15 + pairs * (1 + q_width // deep)),
        ],
        cost_estimate=pl.CostEstimate(
            flops=2 * group * depth * q_width * 12, bytes_accessed=60 * 2**20, transcendentals=0
        ),
        compiler_params=params(5),
    )(lengths, gain, grad_mixed, query, key, value, attended, log_total, cos_table, sin_table,
      tokens, grad_state, gathered, w_out, w_query, w_key, w_value)


class GainSums:
    def __init__(self, gains, tiles, from_tensor, from_dp, wire, chunk):
        self.gains, self.tiles, self.from_tensor, self.from_dp = gains, tiles, from_tensor, from_dp
        self.wire, self.n, self.dps = wire, lax.axis_size("tensor"), lax.axis_size("dp")
        self.chunk = chunk
        self.me, self.dp = lax.axis_index("tensor"), lax.axis_index("dp")

    def tensor(self, step):
        return lax.rem(self.me + np.int32(step), np.int32(self.n))

    def data(self, step):
        return lax.rem(self.dp + np.int32(step), np.int32(self.dps))

    def greet(self):
        barrier = pltpu.get_barrier_semaphore()
        for step in range(1, self.n):
            device = {"tensor": self.tensor(step)}
            pl.semaphore_signal(barrier, inc=1, device_id=device, device_id_type=MESH)
        for step in range(1, self.dps):
            device = {"dp": self.data(step)}
            pl.semaphore_signal(barrier, inc=1, device_id=device, device_id_type=MESH)
        pl.semaphore_wait(barrier, self.n + self.dps - 2)

    def start(self):
        for t in range(self.n):
            for d in range(self.dps):
                lane = (d * self.n + t) * self.chunk // LANES * LANES
                for k, gain in enumerate(self.gains):
                    self.tiles[t, d, k] = gain[:, lane : lane + LANES]
        self.first = [
            self.wire.copy(
                self.tiles.at[self.tensor(step)],
                self.from_tensor.at[step - 1],
                {"tensor": self.tensor(step)},
            )
            for step in range(1, self.n)
        ]

    def forward(self):
        for copy in self.first:
            copy.wait_recv()
        total = self.tiles[self.me]
        for step in range(1, self.n):
            total = total + self.from_tensor[step - 1]
        self.from_tensor[0] = total
        self.second = [
            self.wire.copy(
                self.from_tensor.at[0, self.data(step)],
                self.from_dp.at[step - 1],
                {"dp": self.data(step)},
            )
            for step in range(1, self.dps)
        ]

    def finish(self, out):
        for copy in self.second:
            copy.wait_recv()
        total = self.from_tensor[0, self.dp]
        for step in range(1, self.dps):
            total = total + self.from_dp[step - 1]
        out[...] = total


def output_kernel(
    hidden_in, w_down, state, gain_one, gain_two,
    output, gains_out,
    hidden, down_buf, part, slots, tiles, from_tensor, from_dp,
    send_sem, recv_sem, gain_send, gain_recv, local_sem,
):
    peers = Peers()
    rows, depth = state.shape
    local = Local(local_sem)
    loads = [local.copy(hidden_in, hidden), local.copy(w_down, down_buf)]
    chunk = depth // (lax.axis_size("tensor") * lax.axis_size("dp"))
    gains = GainSums(
        (gain_one, gain_two), tiles, from_tensor, from_dp, Wire(gain_send, gain_recv), chunk
    )
    gains.greet()
    gains.start()
    for load in loads:
        load.wait()

    def make(first, count):
        at = pl.ds(pl.multiple_of(first * rows, rows), count * rows)
        step = 512

        def some(k, carry):
            lanes = pl.ds(pl.multiple_of(k * step, step), step)
            part[at, lanes] = dot_nn(hidden[at, :], down_buf[:, lanes]).astype(BF16)
            return carry

        lax.fori_loop(0, depth // step, some, 0)

    wire = Wire(send_sem, recv_sem)
    sums = scatter(peers, wire, part, slots, rows, make, gains.forward)
    half = rows // 2
    for h in range(2):

        def finish(k, carry, h=h):
            inner = pl.ds(pl.multiple_of(k * 16, 16), 16)
            outer = pl.ds(pl.multiple_of(h * half + k * 16, 16), 16)
            total = sums[h][0][inner, :].astype(F32)
            for other in sums[h][1:]:
                total = total + other[inner, :].astype(F32)
            output[outer, :] = (state[outer, :] + total).astype(BF16)
            return carry

        lax.fori_loop(0, half // 16, finish, 0)
    gains.finish(gains_out)
    wire.wait_sends()
    gains.wire.wait_sends()


def layer_output(hidden, w_down, state, gain_one, gain_two):
    n, dps = lax.axis_size("tensor"), lax.axis_size("dp")
    rows, depth = state.shape
    dma = lambda count: pltpu.SemaphoreType.DMA((count,))
    return pl.pallas_call(
        output_kernel,
        out_shape=(
            jax.ShapeDtypeStruct((rows, depth), BF16),
            jax.ShapeDtypeStruct((2, 8, LANES), F32),
        ),
        in_specs=[any_spec(), any_spec(), vmem_spec(), vmem_spec(), vmem_spec()],
        out_specs=(vmem_spec(), vmem_spec()),
        scratch_shapes=[
            pltpu.VMEM(hidden.shape, BF16),
            pltpu.VMEM(w_down.shape, BF16),
            pltpu.VMEM((hidden.shape[0], depth), BF16),
            slots_for(n, rows, depth),
            pltpu.VMEM((n, dps, 2, 8, LANES), F32),
            pltpu.VMEM((n - 1, dps, 2, 8, LANES), F32),
            pltpu.VMEM((dps - 1, 2, 8, LANES), F32),
            *wires(n),
            dma(n + dps - 2), dma(n + dps - 2), dma(2),
        ],
        cost_estimate=pl.CostEstimate(
            flops=2 * hidden.shape[0] * depth * hidden.shape[1],
            bytes_accessed=20 * 2**20,
            transcendentals=0,
        ),
        compiler_params=params(6),
    )(hidden, w_down, state, gain_one, gain_two)


def unpack_kernel(packed, grad_query, grad_key, grad_value, grad_out):
    first = 0
    for target in (grad_query, grad_key, grad_value):
        width = target.shape[1]
        target[...] = packed[:, first : first + width].astype(F32)
        first += width
    deep = packed.shape[0]
    for c in range(grad_out.shape[0] // deep):
        at = slice(c * deep, (c + 1) * deep)
        grad_out[at, :] = packed[:, first + c * deep : first + (c + 1) * deep].astype(F32)


def unpack(packed, q_width, kv_raw):
    deep = packed.shape[0]
    return pl.pallas_call(
        unpack_kernel,
        out_shape=(
            jax.ShapeDtypeStruct((deep, q_width), F32),
            jax.ShapeDtypeStruct((deep, kv_raw), F32),
            jax.ShapeDtypeStruct((deep, kv_raw), F32),
            jax.ShapeDtypeStruct((q_width, deep), F32),
        ),
    )(packed)


def sum_over_chips(grads):
    size = lax.axis_size("dp")
    groups = [list(range(core, size, 2)) for core in range(2)]
    return lax.psum_scatter(
        grads, "dp", scatter_dimension=0, tiled=True, axis_index_groups=groups
    )


def local(
    tokens, lengths, gain_one, w_query, w_key, w_value, w_out, gain_two, w_gate, w_up, w_down,
    cotangent,
):
    depth = tokens.shape[1]
    q_width, kv_raw, units = w_query.shape[1], w_key.shape[1], w_gate.shape[1]
    gain_one, gain_two = gain_one[None], gain_two[None]
    gathered_one, query, key, value, cos_table, sin_table = project(
        lengths, tokens, gain_one, w_query, w_key, w_value
    )
    attended, log_total, state, normed_two, cot_a, cot_b = attend(
        lengths, query, key, value, tokens, gain_two, w_out, cotangent
    )
    gathered_two, hidden, slope_gate, slope_up, cot_all, grad_down = hidden_units(
        normed_two, cotangent, cot_a, cot_b, w_gate, w_up
    )
    grad_w_down = sum_over_chips(grad_down)
    grad_state, grad_mixed, gain_two_part, grad_gate_up = hidden_back(
        slope_gate, slope_up, cot_all, gathered_two, state, cotangent, gain_two,
        w_down, w_gate, w_up,
    )
    grad_gate_up, grad_w_down = lax.optimization_barrier((grad_gate_up, grad_w_down))
    grad_w_gate_up = sum_over_chips(grad_gate_up)
    grad_tokens, gain_one_part, grads = attend_back(
        lengths, grad_mixed, query, key, value, attended, log_total, cos_table, sin_table,
        tokens, gain_one, grad_state, gathered_one, w_out, w_query, w_key, w_value,
    )
    grads, grad_w_gate_up = lax.optimization_barrier((grads, grad_w_gate_up))
    grads = sum_over_chips(grads)
    grad_w_query, grad_w_key, grad_w_value, grad_w_out = unpack(grads, q_width, kv_raw)
    output, gains = layer_output(hidden, w_down, state, gain_one_part, gain_two_part)
    share = depth // (lax.axis_size("tensor") * lax.axis_size("dp"))
    place = lax.rem(
        (lax.axis_index("dp") * lax.axis_size("tensor") + lax.axis_index("tensor")) * share, LANES
    )
    gains = lax.dynamic_slice_in_dim(jnp.sum(gains, axis=1), place, share, axis=1)
    return (
        output,
        grad_tokens,
        gains[0],
        grad_w_query,
        grad_w_key,
        grad_w_value,
        grad_w_out,
        gains[1],
        grad_w_gate_up[:, :units].astype(F32),
        grad_w_gate_up[:, units:].astype(F32),
        grad_w_down.astype(F32),
    )


def solution(mesh):
    return jax.shard_map(
        local,
        mesh=mesh,
        in_specs=(
            P(("dp", "tensor"), None),
            P("dp", None),
            P(),
            P(None, "tensor"),
            P(None, "tensor"),
            P(None, "tensor"),
            P("tensor", None),
            P(),
            P(None, "tensor"),
            P(None, "tensor"),
            P("tensor", None),
            P(("dp", "tensor"), None),
        ),
        out_specs=(
            P(("dp", "tensor"), None),
            P(("dp", "tensor"), None),
            P(("dp", "tensor")),
            P("dp", "tensor"),
            P("dp", "tensor"),
            P("dp", "tensor"),
            P("tensor", "dp"),
            P(("dp", "tensor")),
            P("dp", "tensor"),
            P("dp", "tensor"),
            P("tensor", "dp"),
        ),
        check_vma=False,
    )
```

```python
import functools
import math

import jax
import jax.numpy as jnp
import numpy as np
from jax import lax
from jax.experimental import pallas as pl
from jax.experimental.pallas import tpu as pltpu
from jax.sharding import PartitionSpec as P

HD = 64
LANES = 128
EPSILON = 1e-05
MASKED = -1e30
LOG2E = math.log2(math.e)
SCALE2 = 0.125 * LOG2E
BF16 = jnp.bfloat16
F32 = jnp.float32
MESH = pl.DeviceIdType.MESH
VMEM_LIMIT = 60 * 2**20


def dot_nn(a, b):
    return jnp.dot(a, b, preferred_element_type=F32)


def dot_nt(a, b):
    return lax.dot_general(a, b, (((1,), (1,)), ((), ())), preferred_element_type=F32)


def dot_tn(a, b):
    return lax.dot_general(a, b, (((0,), (0,)), ((), ())), preferred_element_type=F32)


def place_tables(group):
    index = np.arange(HD // 2, dtype=np.float64)
    base = np.exp(-math.log(500000.0) * 2.0 * index / HD)
    wavelength = 2.0 * math.pi / base
    smooth = (8192.0 / wavelength - 1.0) / 3.0
    blended = (1.0 - smooth) * base / 32.0 + smooth * base
    frequency = np.where(
        wavelength < 2048.0, base, np.where(wavelength > 8192.0, base / 32.0, blended)
    )
    angles = np.arange(group, dtype=np.float64)[:, None] * frequency[None, :]
    cos_half, sin_half = np.cos(angles), np.sin(angles)
    return (
        np.concatenate([cos_half] * 4, axis=1).astype(np.float32),
        np.concatenate([-sin_half, sin_half, -sin_half, sin_half], axis=1).astype(np.float32),
    )


def ends_of(lengths):
    ends, end = [], 0
    for k in range(lengths.shape[1]):
        end = end + lengths[0, k]
        ends.append(end)
    return ends


def starts_of(places, ends):
    start = jnp.zeros_like(places)
    for end in ends:
        start = jnp.where(places >= end, end, start)
    return start


def turn_tables(ends, first, count, cos_place, sin_place):
    places = lax.broadcasted_iota(jnp.int32, (count, LANES), 0) + first
    cos_start, sin_start = jnp.ones((count, LANES), F32), jnp.zeros((count, LANES), F32)
    for end in ends:
        at = pl.ds(jnp.minimum(end, cos_place.shape[0] - 1), 1)
        cos_start = jnp.where(places >= end, cos_place[at, :], cos_start)
        sin_start = jnp.where(places >= end, sin_place[at, :], sin_start)
    rows = pl.ds(first, count)
    cos, sin = cos_place[rows, :], sin_place[rows, :]
    return cos * cos_start + sin * sin_start, sin * cos_start - cos * sin_start


class Peers:
    def __init__(self):
        self.n = lax.axis_size("tensor")
        self.m = self.n // 2
        index = lax.axis_index("tensor")
        self.y = lax.div(index, np.int32(self.m))
        self.x = lax.rem(index, np.int32(self.m))

    def at(self, flip, step):
        row = 1 - self.y if flip else self.y
        return row * self.m + lax.rem(self.x + np.int32(step + self.m), np.int32(self.m))

    def minor(self, step):
        return {"tensor": self.at(0, step)}

    def major(self):
        return {"tensor": self.at(1, 0)}

    def steps(self):
        return range(1, self.m)


def core_of():
    return lax.rem(lax.axis_index("dp"), np.int32(2))


def other_core():
    return {"dp": lax.axis_index("dp") + 1 - 2 * core_of()}


def greet(peers, core=False, chips=False):
    barrier = pltpu.get_barrier_semaphore()
    for step in peers.steps():
        pl.semaphore_signal(barrier, inc=1, device_id=peers.minor(step), device_id_type=MESH)
    pl.semaphore_signal(barrier, inc=1, device_id=peers.major(), device_id_type=MESH)
    if core:
        pl.semaphore_signal(barrier, inc=1, device_id=other_core(), device_id_type=MESH)
    more = greet_chips() if chips else 0
    pl.semaphore_wait(barrier, peers.m + (1 if core else 0) + more)


class Wire:
    def __init__(self, send_sem, recv_sem):
        self.send_sem, self.recv_sem, self.copies = send_sem, recv_sem, []

    def copy(self, source, target, device):
        k = len(self.copies)
        copy = pltpu.make_async_remote_copy(
            src_ref=source,
            dst_ref=target,
            send_sem=self.send_sem.at[k],
            recv_sem=self.recv_sem.at[k],
            device_id=device,
            device_id_type=MESH,
        )
        copy.start()
        self.copies.append(copy)
        return copy

    def wait_sends(self):
        for copy in self.copies:
            copy.wait_send()


def wire_count(n):
    return 4 * (n // 2 - 1) + 2


def wires(n):
    return [pltpu.SemaphoreType.DMA((wire_count(n),))] * 2


class Local:
    def __init__(self, sem):
        self.sem, self.copies = sem, []

    def copy(self, source, target):
        copy = pltpu.make_async_copy(source, target, self.sem.at[len(self.copies)])
        copy.start()
        self.copies.append(copy)
        return copy


def block(ref, index, rows):
    return ref.at[pl.ds(pl.multiple_of(index * rows, rows), rows)]


def half_block(ref, index, rows, half):
    size = rows // 2
    return ref.at[pl.ds(pl.multiple_of(index * rows + half * size, size), size)]


def gather(peers, wire, buf, rows):
    steps, half = list(peers.steps()), rows // 2
    part = lambda index, side: half_block(buf, index, rows, side)
    span = lambda index, side: (pl.multiple_of(index * rows + side * half, half), half)
    me, major = peers.at(0, 0), peers.at(1, 0)
    send = lambda ref, device: wire.copy(ref, ref, device)
    minor_a = [send(part(me, 0), peers.minor(j)) for j in steps]
    major_b = send(part(me, 1), peers.major())
    minor_b = [send(part(me, 1), peers.minor(j)) for j in steps]
    major_a = send(part(me, 0), peers.major())
    yield [(pl.multiple_of(me * rows, rows), rows)]
    forward = []
    for j, copy in zip(steps, minor_a):
        copy.wait_recv()
        forward.append(send(part(peers.at(0, -j), 0), peers.major()))
    major_b.wait_recv()
    forward += [send(part(major, 1), peers.minor(j)) for j in steps]
    yield [span(peers.at(0, -j), 0) for j in steps] + [span(major, 1)]
    for copy in (*minor_b, major_a):
        copy.wait_recv()
    yield [span(peers.at(0, -j), 1) for j in steps] + [span(major, 0)]
    for copy in forward:
        copy.wait_recv()
    yield [(pl.multiple_of(peers.at(1, -j) * rows, rows), rows) for j in steps]


def load_rows(ref, spans):
    return jnp.concatenate([ref[pl.ds(first, count), :] for first, count in spans], axis=0)


def store_rows(ref, spans, lanes, value):
    at = 0
    for first, count in spans:
        ref[pl.ds(first, count), lanes] = value[at : at + count]
        at += count


def add_rows(target, others, size):
    def some(k, carry):
        at = pl.ds(pl.multiple_of(k * 16, 16), 16)
        total = target[at, :].astype(F32)
        for other in others:
            total = total + other[at, :].astype(F32)
        target[at, :] = total.astype(target.dtype)
        return carry

    lax.fori_loop(0, size // 16, some, 0)


def scatter(peers, wire, part_ref, slots, rows, make, meanwhile=None, tick=lambda: None, early=None):
    steps = list(peers.steps())
    part = lambda index, half: half_block(part_ref, index, rows, half)
    me, major = peers.at(0, 0), peers.at(1, 0)
    count = len(steps)
    via_a, via_b, direct_b, sum_a = (
        [slots.at[group * count + k] for k in range(count)] for group in range(4)
    )
    direct_a, sum_b = slots.at[4 * count], slots.at[4 * count + 1]
    make((1 - peers.y) * peers.m, peers.m)
    first_a, first_b = [], []
    for k, j in enumerate(steps):
        index = peers.at(1, j)
        first_a.append(wire.copy(part(index, 0), via_a[k], peers.major()))
        first_b.append(wire.copy(part(index, 1), via_b[k], peers.minor(j)))
    plain_a = wire.copy(part(major, 0), direct_a, peers.major())
    make(peers.y * peers.m, peers.m)
    plain_b = [
        wire.copy(part(peers.at(0, j), 1), direct_b[k], peers.minor(j))
        for k, j in enumerate(steps)
    ]
    tick()
    if early is not None:
        early()
    done_a = []
    for k, j in enumerate(steps):
        first_a[k].wait_recv()
        target = part(peers.at(0, j), 0)
        add_rows(target, [via_a[k]], rows // 2)
        done_a.append(wire.copy(target, sum_a[k], peers.minor(j)))
    for copy in first_b:
        copy.wait_recv()
    target = part(major, 1)
    add_rows(target, via_b, rows // 2)
    done_b = wire.copy(target, sum_b, peers.major())
    tick()
    if meanwhile is not None:
        meanwhile()
    for copy in (plain_a, *plain_b):
        copy.wait_recv()
    tick()
    for copy in (*done_a, done_b):
        copy.wait_recv()
    tick()
    return (
        (part(me, 0), direct_a, *sum_a),
        (part(me, 1), sum_b, *direct_b),
    )


def slots_for(n, rows, width):
    return pltpu.VMEM((wire_count(n), rows // 2, width), BF16)


def lane_of(rows, width=LANES):
    return lax.broadcasted_iota(jnp.int32, (rows, width), 1)


def first_head(rows):
    return lane_of(rows) < HD


def swap_halves(values):
    first = lax.rem(lane_of(values.shape[0]), np.int32(HD)) < HD // 2
    return jnp.where(first, pltpu.roll(values, LANES - HD // 2, 1), pltpu.roll(values, HD // 2, 1))


def doubled(pair, heads):
    if heads == 1:
        return [jnp.concatenate([pair, pair], axis=1)]
    out = []
    for k in range(heads // 2):
        both = pair[:, k * LANES : (k + 1) * LANES]
        swapped = pltpu.roll(both, HD, 1)
        first = first_head(both.shape[0])
        out += [jnp.where(first, both, swapped), jnp.where(first, swapped, both)]
    return out


class ChipSum:
    def __init__(self, source, base, scratch, landing, total, first, span):
        self.source, self.base, self.landing, self.total = source, base, landing, total
        self.stage, self.last, *sems = scratch
        self.send_sem, self.recv_sem, self.load_sem = sems
        self.size = lax.axis_size("dp") // 2
        self.pitch = source.shape[0] // self.size
        self.dp = lax.axis_index("dp")
        place = lax.div(self.dp, np.int32(2))
        self.place, self.along = place, (place, self.size - 1 - place)
        self.chunks = self.send_sem.shape[2]
        self.deep = landing.shape[2]
        self.rows = self.deep // self.chunks
        self.pending = None
        events = []
        step = span / ((self.size - 1) * self.chunks)
        for hop in range(self.size - 1):
            for rank in range(self.size - 1 - hop):
                for c in range(self.chunks):
                    order = rank * self.chunks + c
                    due = first if hop == 0 else first + step * (order + hop) + 3.0 * hop
                    events.append((due, hop, rank, c))
        for c in range(self.chunks):
            due = first + span - step * (self.chunks - 1 - c) + 3.0
            events.append((max(due, max(events)[0]), self.size, 0, c))
        self.events = sorted(events)

    def dest(self, flow, rank):
        return self.size - 1 - rank if flow == 0 else rank

    def chunk(self, d, c):
        return self.source.at[pl.ds(pl.multiple_of(d * self.pitch + self.base + c * self.rows, 16), self.rows)]

    def landed(self, flow, rank, c):
        return self.landing.at[flow, rank, pl.ds(c * self.rows, self.rows)]

    def remote(self, flow, rank, c, source):
        return pltpu.make_async_remote_copy(
            src_ref=source,
            dst_ref=self.landed(flow, rank, c),
            send_sem=self.send_sem.at[flow, rank, c],
            recv_sem=self.recv_sem.at[flow, rank, c],
            device_id={"dp": self.dp + (2 if flow == 0 else -2)},
            device_id_type=MESH,
        )

    def loads(self, flow, slot, sources):
        return [
            pltpu.make_async_copy(ref, self.stage.at[flow, slot, k], self.load_sem.at[flow, slot, k])
            for k, ref in enumerate(sources)
        ]

    def sources(self, flow, rank, c):
        return (self.landed(flow, rank, c), self.chunk(self.dest(flow, rank), c))

    def begin(self, hop, rank, c):
        order = rank * self.chunks + c
        for flow in range(2):
            if hop == 0:

                @pl.when(self.along[flow] == 0)
                def _():
                    if order >= AHEAD:
                        before = divmod(order - AHEAD, self.chunks)
                        self.remote(flow, *before, self.chunk(self.dest(flow, before[0]), before[1])).wait_send()
                    self.remote(flow, rank, c, self.chunk(self.dest(flow, rank), c)).start()

            else:

                @pl.when(self.along[flow] == hop)
                def _():
                    slot = order % 2
                    if order >= 2:
                        before = divmod(order - 2, self.chunks)
                        self.remote(flow, *before, self.stage.at[flow, slot, 0]).wait_send()
                    self.remote(flow, rank, c, self.stage.at[flow, slot, 0]).wait_recv()
                    for load in self.loads(flow, slot, self.sources(flow, rank, c)):
                        load.start()

    def end(self, hop, rank, c):
        order = rank * self.chunks + c
        if hop == 0:
            return
        for flow in range(2):

            @pl.when(self.along[flow] == hop)
            def _():
                slot = order % 2
                for load in self.loads(flow, slot, self.sources(flow, rank, c)):
                    load.wait()
                target = self.stage.at[flow, slot, 0]
                add_rows(target, [self.stage.at[flow, slot, 1]], self.rows)
                self.remote(flow, rank, c, target).start()

    def last_loads(self, c):
        slot = c % 2
        copies = [
            pltpu.make_async_copy(
                self.landing.at[flow, self.size - 1 - self.along[flow], pl.ds(c * self.rows, self.rows)],
                self.last.at[slot, flow],
                self.load_sem.at[flow, slot, 2],
            )
            for flow in range(2)
        ]
        own = pltpu.make_async_copy(
            self.chunk(self.place, c), self.last.at[slot, 2], self.load_sem.at[slot, 0, 3]
        )
        return copies, own

    def last_begin(self, c):
        copies, own = self.last_loads(c)
        own.start()
        for flow in range(2):

            @pl.when(self.along[flow] > 0)
            def _():
                rank = self.size - 1 - self.along[flow]
                landed = self.landing.at[flow, rank, pl.ds(c * self.rows, self.rows)]
                pltpu.make_async_remote_copy(
                    src_ref=landed,
                    dst_ref=landed,
                    send_sem=self.send_sem.at[flow, rank, c],
                    recv_sem=self.recv_sem.at[flow, rank, c],
                    device_id={"dp": self.dp},
                    device_id_type=MESH,
                ).wait_recv()
                copies[flow].start()

    def last_end(self, c):
        copies, own = self.last_loads(c)
        own.wait()
        slot = c % 2
        for flow in range(2):

            @pl.when(self.along[flow] > 0)
            def _():
                copies[flow].wait()
                add_rows(self.last.at[slot, 2], [self.last.at[slot, flow]], self.rows)

        self.save(c).start()

    def save(self, c):
        return pltpu.make_async_copy(
            self.last.at[c % 2, 2],
            self.total.at[pl.ds(c * self.rows, self.rows)],
            self.load_sem.at[c % 2, 1, 3],
        )

    def advance(self, time):
        while self.events and self.events[0][0] <= time:
            _, hop, rank, c = self.events.pop(0)
            self.settle()
            if hop == self.size:
                if c >= 2:
                    self.save(c - 2).wait()
                self.last_begin(c)
            else:
                self.begin(hop, rank, c)
            self.pending = (hop, rank, c)

    def settle(self):
        if self.pending is not None:
            hop, rank, c = self.pending
            self.pending = None
            if hop == self.size:
                self.last_end(c)
            else:
                self.end(hop, rank, c)

    def finish(self):
        self.advance(1e9)
        self.settle()
        for c in range(max(self.chunks - 2, 0), self.chunks):
            self.save(c).wait()
        for flow in range(2):
            for hop in range(self.size - 1):
                depth = AHEAD if hop == 0 else 2
                count = (self.size - 1 - hop) * self.chunks

                @pl.when(self.along[flow] == hop)
                def _():
                    for order in range(max(count - depth, 0), count):
                        rank, c = divmod(order, self.chunks)
                        if hop == 0:
                            source = self.chunk(self.dest(flow, rank), c)
                        else:
                            source = self.stage.at[flow, order % 2, 0]
                        self.remote(flow, rank, c, source).wait_send()


AHEAD = 100


class Clock:
    def __init__(self, sums):
        self.sums, self.time = sums, 0.0

    def start(self):
        for one in self.sums:
            one.start()

    def to(self, time):
        self.time = time
        for one in self.sums:
            one.advance(time)

    def by(self, step):
        self.to(self.time + step)

    def at(self, *times):
        left = list(times)
        return lambda: self.to(left.pop(0))

    def finish(self):
        for one in self.sums:
            one.finish()


MARGIN = 12.0


class NearChipSum:
    def __init__(self, source, base, scratch, total, first, span):
        self.source, self.base, self.total = source, base, total
        self.blocks, self.landing, self.send_sem, self.recv_sem, load_sem, self.save_sem = scratch
        self.size = lax.axis_size("dp") // 2
        self.pitch = source.shape[0] // self.size
        self.dp = lax.axis_index("dp")
        self.place = lax.div(self.dp, np.int32(2))
        self.along = (self.place, self.size - 1 - self.place)
        self.chunks = self.send_sem.shape[2]
        self.deep = self.landing.shape[2]
        self.rows = self.deep // self.chunks
        self.loads = [
            pltpu.make_async_copy(
                source.at[pl.ds(d * self.pitch + base, self.deep)], self.blocks.at[d], load_sem.at[d]
            )
            for d in range(self.size)
        ]
        self.step = span / ((self.size - 1) * self.chunks)
        events = []
        for rank in range(self.size - 1):
            due = first + self.step * self.chunks * rank - MARGIN
            events += [(due, 0, rank, c) for c in range(self.chunks)]
        for hop in range(1, self.size - 1):
            for rank in range(self.size - 1 - hop):
                for c in range(self.chunks):
                    due = first + self.step * (rank * self.chunks + c + hop) + hop
                    events.append((due, hop, rank, c))
        latest = max(events)[0]
        for c in range(self.chunks):
            due = max(first + span - self.step * (self.chunks - 1 - c) + 1.0, latest)
            events.append((due, self.size, 0, c))
        self.events = sorted(events)

    def dest(self, flow, rank):
        return self.size - 1 - rank if flow == 0 else rank

    def landed(self, flow, rank, c):
        return self.landing.at[flow, rank, pl.ds(c * self.rows, self.rows)]

    def remote(self, flow, rank, c, source=None):
        landed = self.landed(flow, rank, c)
        return pltpu.make_async_remote_copy(
            src_ref=landed if source is None else source,
            dst_ref=landed,
            send_sem=self.send_sem.at[flow, rank, c],
            recv_sem=self.recv_sem.at[flow, rank, c],
            device_id={"dp": self.dp + (2 if flow == 0 else -2)},
            device_id_type=MESH,
        )

    def outer(self, flow, rank, c):
        first = self.dest(flow, rank) * self.pitch + self.base + c * self.rows
        return self.remote(flow, rank, c, self.source.at[pl.ds(first, self.rows)])

    def start(self):
        for load in self.loads:
            load.start()

    def send(self, rank, c):
        for flow in range(2):

            @pl.when(self.along[flow] == 0)
            def _():
                self.outer(flow, rank, c).start()

    def pass_on(self, hop, rank, c):
        for flow in range(2):

            @pl.when(self.along[flow] == hop)
            def _():
                copy = self.remote(flow, rank, c)
                copy.wait_recv()
                own = self.blocks.at[self.dest(flow, rank), pl.ds(c * self.rows, self.rows)]
                add_rows(self.landed(flow, rank, c), [own], self.rows)
                copy.start()

    def own(self, c):
        return self.blocks.at[self.place, pl.ds(c * self.rows, self.rows)]

    def save(self, c):
        target = self.total.at[pl.ds(c * self.rows, self.rows)]
        return pltpu.make_async_copy(self.own(c), target, self.save_sem.at[c])

    def take(self, c):
        for flow in range(2):

            @pl.when(self.along[flow] > 0)
            def _():
                rank = self.size - 1 - self.along[flow]
                self.remote(flow, rank, c).wait_recv()
                add_rows(self.own(c), [self.landed(flow, rank, c)], self.rows)

        self.save(c).start()

    def advance(self, time):
        while self.events and self.events[0][0] <= time:
            _, hop, rank, c = self.events.pop(0)
            if hop == 0:
                self.send(rank, c)
                continue
            while self.loads:
                self.loads.pop().wait()
            if hop == self.size:
                self.take(c)
            else:
                self.pass_on(hop, rank, c)

    def finish(self):
        self.advance(1e9)
        for c in range(self.chunks):
            self.save(c).wait()
        for flow in range(2):
            for hop in range(self.size - 1):

                @pl.when(self.along[flow] == hop)
                def _():
                    for rank in range(self.size - 1 - hop):
                        for c in range(self.chunks):
                            copy = self.outer if hop == 0 else self.remote
                            copy(flow, rank, c).wait_send()


def near_chip_sum_scratch(size, deep, width):
    chunks = chip_chunks(size)
    dma = lambda *shape: pltpu.SemaphoreType.DMA(shape)
    return [
        pltpu.VMEM((size, deep, width), BF16),
        pltpu.VMEM((2, size - 1, deep, width), BF16),
        dma(2, size - 1, chunks),
        dma(2, size - 1, chunks),
        dma(size),
        dma(chunks),
    ]


def greet_chips():
    barrier = pltpu.get_barrier_semaphore()
    dp, dps = lax.axis_index("dp"), lax.axis_size("dp")
    for step in (2, dps - 2):
        device = {"dp": lax.rem(dp + np.int32(step), np.int32(dps))}
        pl.semaphore_signal(barrier, inc=1, device_id=device, device_id_type=MESH)
    return 2


def chip_chunks(size):
    return 4 if size == 4 else 1


def chip_sum_shapes(size, deep, width):
    chunks = chip_chunks(size)
    rows = deep // chunks
    dma = lambda *shape: pltpu.SemaphoreType.DMA(shape)
    return (
        jax.ShapeDtypeStruct((2, size - 1, deep, width), BF16),
        [
            pltpu.VMEM((2, 2, 2, rows, width), BF16),
            pltpu.VMEM((2, 3, rows, width), BF16),
            dma(2, size - 1, chunks),
            dma(2, size - 1, chunks),
            dma(2, 2, 4),
        ],
    )


def project_kernel(
    lengths, tokens, gain, cos_place, sin_place, w_query, w_key, w_value,
    gathered_out, query_out, key_out, value_out, cos_out, sin_out,
    gathered, weights, raw_key, raw_value, send_sem, recv_sem, local_sem,
):
    peers = Peers()
    rows, depth = tokens.shape
    group = gathered.shape[0]
    q_width, kv_heads = w_query.shape[1], w_key.shape[1] // HD
    kv_width = kv_heads * LANES
    local = Local(local_sem)
    loads = [
        local.copy(w_key, raw_key),
        local.copy(w_value, raw_value),
        local.copy(w_query, weights.at[:, pl.ds(0, q_width)]),
    ]
    me = peers.at(0, 0)
    gain_row = gain[...]

    def normalize(k, carry):
        values = tokens[pl.ds(pl.multiple_of(k * 16, 16), 16), :].astype(F32)
        scale = lax.rsqrt(jnp.mean(values * values, axis=-1, keepdims=True) + EPSILON)
        gathered[pl.ds(pl.multiple_of(me * rows + k * 16, 16), 16), :] = (
            values * scale * gain_row
        ).astype(BF16)
        return carry

    lax.fori_loop(0, rows // 16, normalize, 0)
    greet(peers)

    def prepare():
        ends = ends_of(lengths)

        def turn(k, carry):
            first = pl.multiple_of(k * 128, 128)
            cos, sin = turn_tables(ends, first, 128, cos_place, sin_place)
            cos_out[pl.ds(first, 128), :] = cos
            sin_out[pl.ds(first, 128), :] = sin
            return carry

        lax.fori_loop(0, group // 128, turn, 0)
        for load in loads:
            load.wait()

        def some(k, carry):
            at = pl.ds(pl.multiple_of(k * 128, 128), 128)
            for raw, base in ((raw_key, q_width), (raw_value, q_width + kv_width)):
                for j, twice in enumerate(doubled(raw[at, :].astype(F32), kv_heads)):
                    weights[at, base + j * LANES : base + (j + 1) * LANES] = twice.astype(BF16)
            return carry

        lax.fori_loop(0, depth // 128, some, 0)

    wire = Wire(send_sem, recv_sem)
    for step, spans in enumerate(gather(peers, wire, gathered, rows)):
        if step == 0:
            prepare()
        if step == 3:
            save = local.copy(gathered, gathered_out)
        cos, sin = load_rows(cos_out, spans), load_rows(sin_out, spans)
        normed = load_rows(gathered, spans)
        for base, width, out, turned in (
            (0, q_width, query_out, True),
            (q_width, kv_width, key_out, True),
            (q_width + kv_width, kv_width, value_out, False),
        ):
            raw = dot_nn(normed, weights[:, base : base + width])
            for c in range(0, width, LANES):
                piece = raw[:, c : c + LANES]
                if turned:
                    piece = piece * cos + swap_halves(piece) * sin
                store_rows(out, spans, slice(c, c + LANES), piece.astype(BF16))
    wire.wait_sends()
    save.wait()


def any_spec():
    return pl.BlockSpec(memory_space=pl.ANY)


def vmem_spec():
    return pl.BlockSpec(memory_space=pltpu.VMEM)


def params(collective_id):
    return pltpu.CompilerParams(
        collective_id=collective_id, has_side_effects=True, vmem_limit_bytes=VMEM_LIMIT
    )


def smem_spec():
    return pl.BlockSpec(memory_space=pltpu.SMEM)


def project(lengths, tokens, gain, w_query, w_key, w_value):
    n = lax.axis_size("tensor")
    rows, depth = tokens.shape
    group = rows * n
    q_width, kv_raw = w_query.shape[1], w_key.shape[1]
    kv_width = kv_raw // HD * LANES
    return pl.pallas_call(
        project_kernel,
        out_shape=(
            jax.ShapeDtypeStruct((group, depth), BF16),
            jax.ShapeDtypeStruct((group, q_width), BF16),
            jax.ShapeDtypeStruct((group, kv_width), BF16),
            jax.ShapeDtypeStruct((group, kv_width), BF16),
            jax.ShapeDtypeStruct((group, LANES), F32),
            jax.ShapeDtypeStruct((group, LANES), F32),
        ),
        in_specs=[smem_spec()] + [vmem_spec()] * 4 + [any_spec()] * 3,
        out_specs=(any_spec(),) + (vmem_spec(),) * 5,
        scratch_shapes=[
            pltpu.VMEM((group, depth), BF16),
            pltpu.VMEM((depth, q_width + 2 * kv_width), BF16),
            pltpu.VMEM((depth, kv_raw), BF16),
            pltpu.VMEM((depth, kv_raw), BF16),
            *wires(n),
            pltpu.SemaphoreType.DMA((4,)),
        ],
        cost_estimate=pl.CostEstimate(
            flops=2 * group * depth * (q_width + 2 * kv_width),
            bytes_accessed=40 * 2**20,
            transcendentals=0,
        ),
        compiler_params=params(1),
    )(lengths, tokens, gain, *place_tables(group), w_query, w_key, w_value)


def attend_kernel(
    lengths, query, key, value, gain, tokens_in, w_out, cotangent,
    attended_out, log_out, state_out, normed_out, cot_a, cot_b,
    tokens, w_buf, attended, log_total, part, slots,
    send_sem, recv_sem, cot_send, cot_recv, local_sem,
):
    peers = Peers()
    rows, depth = tokens.shape
    group, q_width = query.shape
    pairs_per_kv = q_width // LANES // (key.shape[1] // LANES)
    ends = ends_of(lengths)
    local = Local(local_sem)
    loads = [local.copy(w_out, w_buf), local.copy(tokens_in, tokens)]
    greet(peers)
    log_total[...] = jnp.zeros_like(log_total)
    cot_wire = Wire(cot_send, cot_recv)
    for k, j in enumerate(peers.steps()):
        cot_wire.copy(half_block(cotangent, 0, rows, 0), cot_a.at[k], peers.minor(j))
    cot_wire.copy(half_block(cotangent, 0, rows, 1), cot_b, peers.major())

    tile = 256
    for i in range(group // tile):
        keys = (i + 1) * tile

        def one_pair(pair, carry, i=i, keys=keys):
            at = pl.ds(i * tile, tile)
            lanes = pl.ds(pl.multiple_of(pair * LANES, LANES), LANES)
            kv_lanes = pl.ds(
                pl.multiple_of(lax.div(pair, np.int32(pairs_per_kv)) * LANES, LANES), LANES
            )
            both = query[at, lanes]
            key_rows, value_rows = key[0:keys, kv_lanes], value[0:keys, kv_lanes]
            first = first_head(tile)
            column = lax.broadcasted_iota(jnp.int32, (tile, keys), 1)
            row = lax.broadcasted_iota(jnp.int32, (tile, keys), 0) + i * tile
            start = starts_of(lax.broadcasted_iota(jnp.int32, (tile, 1), 0) + i * tile, ends)
            allowed = (column >= start) & (column <= row)
            logs = log_total[at, :]
            outs = []
            for h in range(2):
                own = first if h == 0 else jnp.logical_not(first)
                scores = dot_nt(jnp.where(own, both, jnp.zeros_like(both)), key_rows)
                scores = jnp.where(allowed, scores, MASKED)
                row_max = jnp.max(scores, axis=-1, keepdims=True)
                weights = jnp.exp2((scores - row_max) * SCALE2)
                row_sum = jnp.sum(weights, axis=-1, keepdims=True)
                outs.append(dot_nn(weights.astype(BF16), value_rows) / row_sum)
                logs = jnp.where(
                    lane_of(tile) == pair * 2 + h, row_max * SCALE2 + jnp.log2(row_sum), logs
                )
            log_total[at, :] = logs
            attended[at, lanes] = jnp.where(first, outs[0], outs[1]).astype(BF16)
            return carry

        lax.fori_loop(0, q_width // LANES, one_pair, 0)

    saves = [local.copy(attended, attended_out), local.copy(log_total, log_out)]
    for load in loads:
        load.wait()

    def make(first, count):
        at = pl.ds(pl.multiple_of(first * rows, rows), count * rows)
        heads = attended[at, :]
        for c in range(0, depth, 1024):
            part[at, c : c + 1024] = dot_nn(heads, w_buf[:, c : c + 1024]).astype(BF16)

    wire = Wire(send_sem, recv_sem)
    sums = scatter(peers, wire, part, slots, rows, make)
    gain_row = gain[...]
    half = rows // 2
    for h in range(2):

        def finish(k, carry, h=h):
            inner = pl.ds(pl.multiple_of(k * 16, 16), 16)
            outer = pl.ds(pl.multiple_of(h * half + k * 16, 16), 16)
            mixed = sums[h][0][inner, :].astype(F32)
            for other in sums[h][1:]:
                mixed = mixed + other[inner, :].astype(F32)
            state = tokens[outer, :].astype(F32) + mixed
            scale = lax.rsqrt(jnp.mean(state * state, axis=-1, keepdims=True) + EPSILON)
            state_out[outer, :] = state
            normed_out[outer, :] = (state * scale * gain_row).astype(BF16)
            return carry

        lax.fori_loop(0, half // 16, finish, 0)
    wire.wait_sends()
    for copy in (*cot_wire.copies, *saves):
        copy.wait()


def attend(lengths, query, key, value, tokens, gain, w_out, cotangent):
    n = lax.axis_size("tensor")
    rows, depth = tokens.shape
    group, q_width = query.shape
    m = n // 2
    return pl.pallas_call(
        attend_kernel,
        out_shape=(
            jax.ShapeDtypeStruct((group, q_width), BF16),
            jax.ShapeDtypeStruct((group, LANES), F32),
            jax.ShapeDtypeStruct((rows, depth), F32),
            jax.ShapeDtypeStruct((rows, depth), BF16),
            jax.ShapeDtypeStruct((m - 1, rows // 2, depth), BF16),
            jax.ShapeDtypeStruct((rows // 2, depth), BF16),
        ),
        in_specs=[smem_spec()] + [vmem_spec()] * 4 + [any_spec()] * 3,
        out_specs=(any_spec(), any_spec(), vmem_spec(), vmem_spec(), any_spec(), any_spec()),
        scratch_shapes=[
            pltpu.VMEM((rows, depth), BF16),
            pltpu.VMEM(w_out.shape, BF16),
            pltpu.VMEM((group, q_width), BF16),
            pltpu.VMEM((group, LANES), F32),
            pltpu.VMEM((group, depth), BF16),
            slots_for(n, rows, depth),
            *wires(n),
            pltpu.SemaphoreType.DMA((m,)),
            pltpu.SemaphoreType.DMA((m,)),
            pltpu.SemaphoreType.DMA((4,)),
        ],
        cost_estimate=pl.CostEstimate(
            flops=2 * group * depth * q_width * 4, bytes_accessed=40 * 2**20, transcendentals=0
        ),
        compiler_params=params(2),
    )(lengths, query, key, value, gain, tokens, w_out, cotangent)


class Exchange:
    def __init__(self, wire, stage, received):
        self.wire, self.stage, self.received, self.sent = wire, stage, received, []

    def run(self, jobs, tick=lambda: None):
        mine = core_of()
        copies = []
        for k in range(len(jobs) + 1):
            if k < len(jobs):
                tile, save, pair = jobs[k]
                slot = self.stage.at[k % 2]
                if k >= 2:
                    copies[k - 2].wait_send()
                tile(2 * pair + 1 - mine, slot, False)
                copies.append(self.wire.copy(slot, self.received.at[k], other_core()))
                tick()
            if k >= 1:
                tile, save, pair = jobs[k - 1]
                copies[k - 1].wait_recv()
                tile(2 * pair + mine, self.received.at[k - 1], True)
                save(pair, self.received.at[k - 1])
                tick()
        for copy in copies[-2:]:
            copy.wait_send()


def put(target, at, value, add):
    if add:
        value = value + target[at].astype(F32)
    target[at] = value.astype(BF16)


def hidden_kernel(
    normed, cotangent, cot_a, cot_b, w_gate, w_up,
    gathered_out, hidden_out, slope_gate_out, slope_up_out, cot_out, grad_down_out,
    gathered, gate_buf, up_buf, hidden, slope_gate, slope_up, cot, stage, received,
    send_sem, recv_sem, cot_send, cot_recv, core_send, core_recv, local_sem,
):
    peers = Peers()
    rows, depth = normed.shape
    units = w_gate.shape[1]
    me, major = peers.at(0, 0), peers.at(1, 0)
    local = Local(local_sem)
    first_load = local.copy(normed, block(gathered, me, rows))
    loads = [local.copy(w_gate, gate_buf), local.copy(w_up, up_buf)]
    cot_loads = [local.copy(cotangent, block(cot, me, rows))]
    for k, j in enumerate(peers.steps()):
        cot_loads.append(local.copy(cot_a.at[k], half_block(cot, peers.at(0, -j), rows, 0)))
    cot_loads.append(local.copy(cot_b, half_block(cot, major, rows, 1)))
    greet(peers, core=True)
    first_load.wait()

    def use(spans):
        tile = 512

        def some(k, carry):
            lanes = pl.ds(pl.multiple_of(k * tile, tile), tile)
            x = load_rows(gathered, spans)
            gate = dot_nn(x, gate_buf[:, lanes])
            up = dot_nn(x, up_buf[:, lanes])
            sigmoid = jax.nn.sigmoid(gate)
            silu = gate * sigmoid
            slope = up * sigmoid * (1.0 + gate * (1.0 - sigmoid))
            store_rows(hidden, spans, lanes, (silu * up).astype(BF16))
            store_rows(slope_up, spans, lanes, silu.astype(BF16))
            store_rows(slope_gate, spans, lanes, slope.astype(BF16))
            return carry

        lax.fori_loop(0, units // tile, some, 0)

    cot_wire = Wire(cot_send, cot_recv)
    rest = ([], [])
    width = depth // 2

    def send_rest():
        for load in cot_loads:
            load.wait()
        for side in range(2):
            lanes = pl.ds(side * width, width)

            def send(index, half, device):
                ref = half_block(cot, index, rows, half).at[:, lanes]
                rest[side].append(cot_wire.copy(ref, ref, device))

            for j in peers.steps():
                send(me, 1, peers.minor(j))
                send(major, 1, peers.minor(j))
            send(me, 0, peers.major())
            for j in peers.steps():
                send(peers.at(0, -j), 0, peers.major())

    wire = Wire(send_sem, recv_sem)
    for step, spans in enumerate(gather(peers, wire, gathered, rows)):
        if step == 0:
            for load in loads:
                load.wait()
        if step == 3:
            send_rest()
        use(spans)
    saves = [
        local.copy(gathered, gathered_out),
        local.copy(hidden, hidden_out),
        local.copy(slope_gate, slope_gate_out),
        local.copy(slope_up, slope_up_out),
    ]
    columns = stage.shape[2]
    pairs = received.shape[0]
    arrived = set()

    def tile_of(side):
        def tile(index, target, add):
            if side not in arrived:
                arrived.add(side)
                for copy in rest[side]:
                    copy.wait_recv()
            lanes = pl.ds(pl.multiple_of(index * columns, columns), columns)
            step = 512

            def some(k, carry):
                at = pl.ds(pl.multiple_of(k * step, step), step)
                put(target, (at, slice(None)), dot_tn(hidden[:, at], cot[:, lanes]), add)
                return carry

            lax.fori_loop(0, units // step, some, 0)

        return tile

    def save(k, ref):
        saves.append(local.copy(ref, grad_down_out.at[pl.ds(k * units, units)]))

    Exchange(Wire(core_send, core_recv), stage, received).run(
        [(tile_of(2 * k // pairs), save, k) for k in range(pairs)]
    )
    saves.append(local.copy(cot, cot_out))
    wire.wait_sends()
    cot_wire.wait_sends()
    for copy in saves:
        copy.wait()


def hidden_units(normed, cotangent, cot_a, cot_b, w_gate, w_up):
    n = lax.axis_size("tensor")
    pairs = lax.axis_size("dp") // 2
    rows, depth = normed.shape
    group, units, columns = rows * n, w_gate.shape[1], depth // (2 * pairs)
    wide = lambda width: jax.ShapeDtypeStruct((group, width), BF16)
    return pl.pallas_call(
        hidden_kernel,
        out_shape=(
            wide(depth), wide(units), wide(units), wide(units), wide(depth),
            jax.ShapeDtypeStruct((pairs * units, columns), BF16),
        ),
        in_specs=[any_spec()] * 6,
        out_specs=(any_spec(),) * 6,
        scratch_shapes=[
            pltpu.VMEM((group, depth), BF16),
            pltpu.VMEM((depth, units), BF16),
            pltpu.VMEM((depth, units), BF16),
            pltpu.VMEM((group, units), BF16),
            pltpu.VMEM((group, units), BF16),
            pltpu.VMEM((group, units), BF16),
            pltpu.VMEM((group, depth), BF16),
            pltpu.VMEM((2, units, columns), BF16),
            pltpu.VMEM((pairs, units, columns), BF16),
            *wires(n),
            pltpu.SemaphoreType.DMA((2 * wire_count(n),)),
            pltpu.SemaphoreType.DMA((2 * wire_count(n),)),
            pltpu.SemaphoreType.DMA((pairs,)),
            pltpu.SemaphoreType.DMA((pairs,)),
            pltpu.SemaphoreType.DMA((3 + n // 2 + 1 + 5 + pairs,)),
        ],
        cost_estimate=pl.CostEstimate(
            flops=6 * group * depth * units, bytes_accessed=60 * 2**20, transcendentals=0
        ),
        compiler_params=params(3),
    )(normed, cotangent, cot_a, cot_b, w_gate, w_up)


def norm_back(values, gain_row, grad_normed):
    scale = lax.rsqrt(jnp.mean(values * values, axis=-1, keepdims=True) + EPSILON)
    unit = values * scale
    scaled = grad_normed * gain_row
    grad = scale * (scaled - unit * jnp.mean(scaled * unit, axis=-1, keepdims=True))
    return grad, grad_normed * unit


def fold_rows(values):
    return values[:8] + values[8:]


def hidden_back_kernel(
    slope_gate, slope_up, cot_all, gathered_in, state, cotangent, gain, w_down, w_gate, w_up, grad_down,
    grad_state_out, grad_mixed_out, gain_out, grad_gate_up_out, landing, total_down,
    gate_buf, up_buf, down_buf, grad_gate, grad_up, cot, part, slots, stage, received,
    send_sem, recv_sem, core_send, core_recv, local_sem, *chip_scratch,
):
    peers = Peers()
    rows, depth = state.shape
    group, units = slope_gate.shape
    chunk = down_buf.shape[1]
    chunks = units // chunk
    local = Local(local_sem)
    load_cot = local.copy(cot_all, cot)

    def load_down(k):
        source = w_down.at[pl.ds(k % chunks * chunk, chunk)]
        return local.copy(source, down_buf.at[k % 2])

    downs = [load_down(0)]
    slopes = [local.copy(slope_gate, grad_gate), local.copy(slope_up, grad_up)]
    downs.append(load_down(1))
    greet(peers, core=True, chips=True)
    clock = Clock([ChipSum(grad_down, 0, chip_scratch, landing, total_down, 0.0, 72.0)])
    clock.to(1.0)
    later = []

    def make(first, count):
        at = pl.ds(pl.multiple_of(first * rows, rows), count * rows)
        base = chunks if later else 0
        for c in range(chunks):
            downs[base + c].wait()
            if not later:
                load_cot.wait()
                for load in slopes:
                    load.wait()
                later.extend(
                    [
                        local.copy(w_gate, gate_buf),
                        local.copy(w_up, up_buf),
                        local.copy(state, grad_state_out),
                    ]
                )
            lanes = slice(c * chunk, (c + 1) * chunk)
            grad_hidden = dot_nt(cot[at, :], down_buf[c % 2])
            grad_gate[at, lanes] = (grad_hidden * grad_gate[at, lanes].astype(F32)).astype(BF16)
            grad_up[at, lanes] = (grad_hidden * grad_up[at, lanes].astype(F32)).astype(BF16)
            if base + c + 2 < 2 * chunks:
                downs.append(load_down(base + c + 2))
            clock.by(7.0 if base + c == 0 else 1.5)
        if base == 0:
            for load in later[:2]:
                load.wait()
        else:
            later.append(local.copy(gathered_in, cot))
        step = 512

        for k in range(depth // step):
            inner = slice(k * step, (k + 1) * step)
            total = dot_nt(grad_gate[at, :], gate_buf[inner, :])
            total = total + dot_nt(grad_up[at, :], up_buf[inner, :])
            part[at, inner] = total.astype(BF16)
            clock.by(2.7)

    deep = stage.shape[1]
    saves = []

    def tile_of(grad):
        def tile(index, target, add):
            lanes = pl.ds(pl.multiple_of(index * deep, deep), deep)
            step = min(1024, units)

            def some(k, carry):
                inner = pl.ds(pl.multiple_of(k * step, step), step)
                put(target, (slice(None), inner), dot_tn(cot[:, lanes], grad[:, inner]), add)
                return carry

            lax.fori_loop(0, units // step, some, 0)

        return tile

    def save_at(base):
        def save(k, ref):
            target = grad_gate_up_out.at[pl.ds(k * deep, deep), pl.ds(base, units)]
            saves.append(local.copy(ref, target))

        return save

    def weight_grads():
        later[3].wait()
        pairs = received.shape[0] // 2
        Exchange(Wire(core_send, core_recv), stage, received).run(
            [(tile_of(grad_gate), save_at(0), k) for k in range(pairs)]
            + [(tile_of(grad_up), save_at(units), k) for k in range(pairs)],
            lambda: clock.by(1.6),
        )

    wire = Wire(send_sem, recv_sem)
    sums = scatter(peers, wire, part, slots, rows, make, weight_grads, lambda: clock.by(0.5))
    later[2].wait()
    gain_row = gain[...]
    half = rows // 2
    gain_out[...] = jnp.zeros_like(gain_out)
    for h in range(2):

        def finish(k, carry, h=h):
            inner = pl.ds(pl.multiple_of(k * 16, 16), 16)
            outer = pl.ds(pl.multiple_of(h * half + k * 16, 16), 16)
            grad_normed = sums[h][0][inner, :].astype(F32)
            for other in sums[h][1:]:
                grad_normed = grad_normed + other[inner, :].astype(F32)
            grad, gain_part = norm_back(grad_state_out[outer, :], gain_row, grad_normed)
            grad = grad + cotangent[outer, :].astype(F32)
            gain_out[...] += fold_rows(gain_part)
            grad_state_out[outer, :] = grad
            grad_mixed_out[outer, :] = grad.astype(BF16)
            return carry

        lax.fori_loop(0, half // 16, finish, 0)
    clock.finish()
    wire.wait_sends()
    for copy in saves:
        copy.wait()


def hidden_back(
    slope_gate, slope_up, cot_all, gathered, state, cotangent, gain, w_down, w_gate, w_up, grad_down
):
    n = lax.axis_size("tensor")
    pairs = lax.axis_size("dp") // 2
    rows, depth = state.shape
    group, units = slope_gate.shape
    deep = depth // (2 * pairs)
    chunk = 512
    landing, chip_scratch = chip_sum_shapes(pairs, units, grad_down.shape[1])
    return pl.pallas_call(
        hidden_back_kernel,
        out_shape=(
            jax.ShapeDtypeStruct((rows, depth), F32),
            jax.ShapeDtypeStruct((rows, depth), BF16),
            jax.ShapeDtypeStruct((8, depth), F32),
            jax.ShapeDtypeStruct((pairs * deep, 2 * units), BF16),
            landing,
            jax.ShapeDtypeStruct((units, grad_down.shape[1]), BF16),
        ),
        in_specs=[any_spec()] * 5 + [vmem_spec()] * 2 + [any_spec()] * 4,
        out_specs=(vmem_spec(), vmem_spec(), vmem_spec(), any_spec(), any_spec(), any_spec()),
        scratch_shapes=[
            pltpu.VMEM((depth, units), BF16),
            pltpu.VMEM((depth, units), BF16),
            pltpu.VMEM((2, chunk, depth), BF16),
            pltpu.VMEM((group, units), BF16),
            pltpu.VMEM((group, units), BF16),
            pltpu.VMEM((group, depth), BF16),
            pltpu.VMEM((group, depth), BF16),
            slots_for(n, rows, depth),
            pltpu.VMEM((2, deep, units), BF16),
            pltpu.VMEM((2 * pairs, deep, units), BF16),
            *wires(n),
            pltpu.SemaphoreType.DMA((2 * pairs,)),
            pltpu.SemaphoreType.DMA((2 * pairs,)),
            pltpu.SemaphoreType.DMA((7 + 2 * (units // chunk) + 2 * pairs,)),
            *chip_scratch,
        ],
        cost_estimate=pl.CostEstimate(
            flops=10 * group * depth * units, bytes_accessed=80 * 2**20, transcendentals=0
        ),
        compiler_params=params(4),
    )(
        slope_gate, slope_up, cot_all, gathered, state, cotangent, gain, w_down, w_gate, w_up,
        grad_down,
    )


def attend_back_kernel(
    lengths, gain, grad_mixed, query_in, key_in, value_in, attended_in, log_in, cos_in, sin_in,
    tokens_in, state_in, gathered_in, w_out, w_query, w_key, w_value, grad_gate_up,
    grad_tokens_out, gain_out, grads_out, total_gate_up,
    query, key, value, attended, log_total, cos_table, sin_table, tokens, grad_state,
    mixed, out_buf, query_buf, key_buf, value_buf, gathered, grad_att, key_acc, value_acc, grads, part, slots,
    stage_out, got_out, stage_qkv, got_qkv,
    send_sem, recv_sem, sums_send, sums_recv, out_send, out_recv, qkv_send, qkv_recv, local_sem, *chip_scratch,
):
    peers = Peers()
    rows, depth = tokens.shape
    group, q_width = query.shape
    kv_heads = w_key.shape[1] // HD
    kv_raw = kv_heads * HD
    pairs_per_kv = q_width // LANES // kv_heads
    me = peers.at(0, 0)
    local = Local(local_sem)
    first_load = local.copy(grad_mixed, block(mixed, me, rows))
    load_out = local.copy(w_out, out_buf)
    sources = (
        query_in, key_in, value_in, attended_in, log_in, cos_in, sin_in, tokens_in, state_in
    )
    buffers = (query, key, value, attended, log_total, cos_table, sin_table, tokens, grad_state)
    loads = [local.copy(source, buffer) for source, buffer in zip(sources, buffers)]
    loads += [
        local.copy(w_query, query_buf),
        local.copy(w_key, key_buf),
        local.copy(w_value, value_buf),
        local.copy(gathered_in, gathered),
    ]
    greet(peers, core=True, chips=True)
    clock = Clock([NearChipSum(grad_gate_up, 0, chip_scratch, total_gate_up, 0.0, 108.0)])
    clock.start()
    clock.to(0.5)
    first_load.wait()
    ends, saves = ends_of(lengths), []
    gather_wire = Wire(send_sem, recv_sem)
    for step, spans in enumerate(gather(peers, gather_wire, mixed, rows)):
        if step == 0:
            load_out.wait()
        grad_rows = dot_nt(load_rows(mixed, spans), out_buf[...]).astype(BF16)
        store_rows(grad_att, spans, slice(None), grad_rows)
        clock.to(1.0 + 12.0 * step)

    for load in loads:
        load.wait()
    columns = stage_out.shape[2]

    def out_tile(index, target, add):
        lanes = pl.ds(pl.multiple_of(index * columns, columns), columns)
        put(target, (slice(None), slice(None)), dot_tn(attended[...], mixed[:, lanes]), add)

    pairs = got_out.shape[0]
    width = grads.shape[1]

    def out_save(k, ref):
        for c in range(q_width // columns):
            target = grads_out.at[
                pl.ds(k * columns, columns), pl.ds(width + c * columns, columns)
            ]
            saves.append(local.copy(ref.at[pl.ds(c * columns, columns)], target))

    key_acc[...] = jnp.zeros_like(key_acc)
    value_acc[...] = jnp.zeros_like(value_acc)
    tile = 256
    for i in range(group // tile):
        keys = (i + 1) * tile

        def one_pair(pair, carry, i=i, keys=keys):
            at = pl.ds(i * tile, tile)
            lanes = pl.ds(pl.multiple_of(pair * LANES, LANES), LANES)
            kv_lanes = pl.ds(
                pl.multiple_of(lax.div(pair, np.int32(pairs_per_kv)) * LANES, LANES), LANES
            )
            both, grad_both = query[at, lanes], grad_att[at, lanes]
            key_rows, value_rows = key[0:keys, kv_lanes], value[0:keys, kv_lanes]
            first = first_head(tile)
            dots = grad_both.astype(F32) * attended[at, lanes].astype(F32)
            column = lax.broadcasted_iota(jnp.int32, (tile, keys), 1)
            row = lax.broadcasted_iota(jnp.int32, (tile, keys), 0) + i * tile
            start = starts_of(lax.broadcasted_iota(jnp.int32, (tile, 1), 0) + i * tile, ends)
            allowed = (column >= start) & (column <= row)
            logs = log_total[at, :]
            grad_queries, grad_keys, grad_values = [], 0.0, 0.0
            for h in range(2):
                own = first if h == 0 else jnp.logical_not(first)
                own_query = jnp.where(own, both, jnp.zeros_like(both))
                own_grad = jnp.where(own, grad_both, jnp.zeros_like(grad_both))
                row_dot = jnp.sum(jnp.where(own, dots, 0.0), axis=-1, keepdims=True)
                scores = dot_nt(own_query, key_rows)
                log_row = jnp.sum(
                    jnp.where(lane_of(tile) == pair * 2 + h, logs, 0.0), axis=-1, keepdims=True
                )
                probs = jnp.exp2(scores * SCALE2 - log_row)
                probs = jnp.where(allowed, probs, 0.0)
                grad_probs = dot_nt(own_grad, value_rows)
                grad_scores = (probs * (grad_probs - row_dot)).astype(BF16)
                grad_queries.append(dot_nn(grad_scores, key_rows))
                grad_keys = grad_keys + dot_tn(grad_scores, own_query)
                grad_values = grad_values + dot_tn(probs.astype(BF16), own_grad)
            key_acc[0:keys, kv_lanes] += grad_keys
            value_acc[0:keys, kv_lanes] += grad_values
            turned = jnp.where(first, grad_queries[0], grad_queries[1]) * 0.125
            turned = turned * cos_table[at, :] - swap_halves(turned) * sin_table[at, :]
            grads[at, lanes] = turned.astype(BF16)
            return carry

        lax.fori_loop(0, q_width // LANES, one_pair, 0)
        clock.by(2.1 * (i + 1))

    def fold(k, carry):
        at = pl.ds(pl.multiple_of(k * 128, 128), 128)
        cos, sin = cos_table[at, :], sin_table[at, :]
        key_heads, value_heads = [], []
        for j in range(kv_heads):
            lanes = slice(j * LANES, (j + 1) * LANES)
            both = key_acc[at, lanes] * 0.125
            both = both + pltpu.roll(both, HD, 1)
            key_heads.append(both * cos - swap_halves(both) * sin)
            both = value_acc[at, lanes]
            value_heads.append(both + pltpu.roll(both, HD, 1))
        for heads, base in ((key_heads, q_width), (value_heads, q_width + kv_raw)):
            if kv_heads == 1:
                grads[at, base : base + HD] = heads[0][:, :HD].astype(BF16)
            for j in range(0, kv_heads - 1, 2):
                pair = jnp.where(first_head(128), heads[j], heads[j + 1])
                grads[at, base + j * HD : base + (j + 2) * HD] = pair.astype(BF16)
        return carry

    lax.fori_loop(0, group // 128, fold, 0)

    def make(first, count):
        at = pl.ds(pl.multiple_of(first * rows, rows), count * rows)
        step = 1024
        for c in range(0, depth, step):
            inner = slice(c, c + step)
            total = dot_nt(grads[at, 0:q_width], query_buf[inner, :])
            total = total + dot_nt(grads[at, q_width : q_width + kv_raw], key_buf[inner, :])
            total = total + dot_nt(grads[at, q_width + kv_raw :], value_buf[inner, :])
            part[at, inner] = total.astype(BF16)
            clock.by(1.2)

    deep = stage_qkv.shape[1]

    def qkv_tile(index, target, add):
        lanes = pl.ds(pl.multiple_of(index * deep, deep), deep)
        put(target, (slice(None), slice(None)), dot_tn(gathered[:, lanes], grads[...]), add)

    def qkv_save(k, ref):
        target = grads_out.at[pl.ds(k * deep, deep), pl.ds(0, width)]
        saves.append(local.copy(ref, target))

    def weight_grads():
        Exchange(Wire(out_send, out_recv), stage_out, got_out).run(
            [(out_tile, out_save, k) for k in range(pairs)], lambda: clock.by(0.5)
        )
        Exchange(Wire(qkv_send, qkv_recv), stage_qkv, got_qkv).run(
            [(qkv_tile, qkv_save, k) for k in range(pairs)], lambda: clock.by(0.9)
        )

    wire = Wire(sums_send, sums_recv)
    sums = scatter(
        peers, wire, part, slots, rows, make, tick=clock.at(66.0, 80.0, 90.0, 101.0), early=weight_grads
    )
    gain_row = gain[...]
    half = rows // 2
    gain_out[...] = jnp.zeros_like(gain_out)
    for h in range(2):

        def finish(k, carry, h=h):
            inner = pl.ds(pl.multiple_of(k * 16, 16), 16)
            outer = pl.ds(pl.multiple_of(h * half + k * 16, 16), 16)
            grad_normed = sums[h][0][inner, :].astype(F32)
            for other in sums[h][1:]:
                grad_normed = grad_normed + other[inner, :].astype(F32)
            grad, gain_part = norm_back(tokens[outer, :].astype(F32), gain_row, grad_normed)
            gain_out[...] += fold_rows(gain_part)
            grad_tokens_out[outer, :] = (grad + grad_state[outer, :]).astype(BF16)
            return carry

        lax.fori_loop(0, half // 16, finish, 0)
    clock.finish()
    gather_wire.wait_sends()
    wire.wait_sends()
    for copy in saves:
        copy.wait()


def attend_back(
    lengths, grad_mixed, query, key, value, attended, log_total, cos_table, sin_table,
    tokens, gain, grad_state, gathered, w_out, w_query, w_key, w_value, grad_gate_up,
):
    n = lax.axis_size("tensor")
    pairs = lax.axis_size("dp") // 2
    rows, depth = tokens.shape
    group, q_width = query.shape
    kv_width, kv_raw = key.shape[1], w_key.shape[1]
    width = q_width + 2 * kv_raw
    deep = depth // (2 * pairs)
    dma = lambda count: pltpu.SemaphoreType.DMA((count,))
    early = deep - deep // 4
    chip_scratch = near_chip_sum_scratch(pairs, early, grad_gate_up.shape[1])
    return pl.pallas_call(
        attend_back_kernel,
        out_shape=(
            jax.ShapeDtypeStruct((rows, depth), BF16),
            jax.ShapeDtypeStruct((8, depth), F32),
            jax.ShapeDtypeStruct((pairs * deep, width + q_width), BF16),
            jax.ShapeDtypeStruct((early, grad_gate_up.shape[1]), BF16),
        ),
        in_specs=[smem_spec(), vmem_spec()] + [any_spec()] * 16,
        out_specs=(vmem_spec(), vmem_spec(), any_spec(), any_spec()),
        scratch_shapes=[
            *[
                pltpu.VMEM(source.shape, source.dtype)
                for source in (
                    query, key, value, attended, log_total, cos_table, sin_table, tokens, grad_state
                )
            ],
            pltpu.VMEM((group, depth), BF16),
            pltpu.VMEM(w_out.shape, BF16),
            pltpu.VMEM(w_query.shape, BF16),
            pltpu.VMEM(w_key.shape, BF16),
            pltpu.VMEM(w_value.shape, BF16),
            pltpu.VMEM((group, depth), BF16),
            pltpu.VMEM((group, q_width), BF16),
            pltpu.VMEM((group, kv_width), F32),
            pltpu.VMEM((group, kv_width), F32),
            pltpu.VMEM((group, width), BF16),
            pltpu.VMEM((group, depth), BF16),
            slots_for(n, rows, depth),
            pltpu.VMEM((2, q_width, deep), BF16),
            pltpu.VMEM((pairs, q_width, deep), BF16),
            pltpu.VMEM((2, deep, width), BF16),
            pltpu.VMEM((pairs, deep, width), BF16),
            *wires(n),
            *wires(n),
            dma(pairs), dma(pairs), dma(pairs), dma(pairs), dma(15 + pairs * (1 + q_width // deep)),
            *chip_scratch,
        ],
        cost_estimate=pl.CostEstimate(
            flops=2 * group * depth * q_width * 12, bytes_accessed=60 * 2**20, transcendentals=0
        ),
        compiler_params=params(5),
    )(lengths, gain, grad_mixed, query, key, value, attended, log_total, cos_table, sin_table,
      tokens, grad_state, gathered, w_out, w_query, w_key, w_value, grad_gate_up)


class GainSums:
    def __init__(self, gains, tiles, from_tensor, from_dp, wire, chunk):
        self.gains, self.tiles, self.from_tensor, self.from_dp = gains, tiles, from_tensor, from_dp
        self.wire, self.n, self.dps = wire, lax.axis_size("tensor"), lax.axis_size("dp")
        self.chunk = chunk
        self.me, self.dp = lax.axis_index("tensor"), lax.axis_index("dp")

    def tensor(self, step):
        return lax.rem(self.me + np.int32(step), np.int32(self.n))

    def data(self, step):
        return lax.rem(self.dp + np.int32(step), np.int32(self.dps))

    def greet(self):
        barrier = pltpu.get_barrier_semaphore()
        for step in range(1, self.n):
            device = {"tensor": self.tensor(step)}
            pl.semaphore_signal(barrier, inc=1, device_id=device, device_id_type=MESH)
        for step in range(1, self.dps):
            device = {"dp": self.data(step)}
            pl.semaphore_signal(barrier, inc=1, device_id=device, device_id_type=MESH)
        pl.semaphore_wait(barrier, self.n + self.dps - 2)

    def start(self):
        for t in range(self.n):
            for d in range(self.dps):
                lane = (d * self.n + t) * self.chunk // LANES * LANES
                for k, gain in enumerate(self.gains):
                    self.tiles[t, d, k] = gain[:, lane : lane + LANES]
        self.first = [
            self.wire.copy(
                self.tiles.at[self.tensor(step)],
                self.from_tensor.at[step - 1],
                {"tensor": self.tensor(step)},
            )
            for step in range(1, self.n)
        ]

    def forward(self):
        for copy in self.first:
            copy.wait_recv()
        total = self.tiles[self.me]
        for step in range(1, self.n):
            total = total + self.from_tensor[step - 1]
        self.from_tensor[0] = total
        self.second = [
            self.wire.copy(
                self.from_tensor.at[0, self.data(step)],
                self.from_dp.at[step - 1],
                {"dp": self.data(step)},
            )
            for step in range(1, self.dps)
        ]

    def finish(self, out):
        for copy in self.second:
            copy.wait_recv()
        total = self.from_tensor[0, self.dp]
        for step in range(1, self.dps):
            total = total + self.from_dp[step - 1]
        out[...] = total


def output_kernel(
    hidden_in, w_down, state, gain_one, gain_two, grad_gate_up, grads,
    output, gains_out, total_gate_up, total_grads,
    hidden, down_buf, part, slots, tiles, from_tensor, from_dp,
    send_sem, recv_sem, gain_send, gain_recv, local_sem, *chip_scratch,
):
    peers = Peers()
    rows, depth = state.shape
    local = Local(local_sem)
    loads = [local.copy(hidden_in, hidden), local.copy(w_down, down_buf)]
    chunk = depth // (lax.axis_size("tensor") * lax.axis_size("dp"))
    gains = GainSums(
        (gain_one, gain_two), tiles, from_tensor, from_dp, Wire(gain_send, gain_recv), chunk
    )
    gains.greet()
    base = grad_gate_up.shape[0] // (lax.axis_size("dp") // 2) - total_gate_up.shape[0]
    half = len(chip_scratch) // 2
    clock = Clock(
        [
            NearChipSum(grad_gate_up, base, chip_scratch[:half], total_gate_up, 0.0, 36.0),
            NearChipSum(grads, 0, chip_scratch[half:], total_grads, 36.0, 45.0),
        ]
    )
    clock.start()
    clock.to(0.5)
    gains.start()
    for load in loads:
        load.wait()

    def make(first, count):
        at = pl.ds(pl.multiple_of(first * rows, rows), count * rows)
        step = 512

        for k in range(depth // step):
            lanes = slice(k * step, (k + 1) * step)
            part[at, lanes] = dot_nn(hidden[at, :], down_buf[:, lanes]).astype(BF16)
            clock.by(1.6)

    wire = Wire(send_sem, recv_sem)
    ticks = clock.at(17.0, 29.0, 35.0, 47.0)
    sums = scatter(peers, wire, part, slots, rows, make, gains.forward, ticks)
    half = rows // 2
    for h in range(2):

        def finish(k, carry, h=h):
            inner = pl.ds(pl.multiple_of(k * 16, 16), 16)
            outer = pl.ds(pl.multiple_of(h * half + k * 16, 16), 16)
            total = sums[h][0][inner, :].astype(F32)
            for other in sums[h][1:]:
                total = total + other[inner, :].astype(F32)
            output[outer, :] = (state[outer, :] + total).astype(BF16)
            return carry

        lax.fori_loop(0, half // 16, finish, 0)
    gains.finish(gains_out)
    clock.finish()
    wire.wait_sends()
    gains.wire.wait_sends()


def layer_output(hidden, w_down, state, gain_one, gain_two, grad_gate_up, grads):
    n, dps = lax.axis_size("tensor"), lax.axis_size("dp")
    rows, depth = state.shape
    dma = lambda count: pltpu.SemaphoreType.DMA((count,))
    pairs = dps // 2
    deep = grads.shape[0] // pairs
    scratch_a = near_chip_sum_scratch(pairs, deep // 4, grad_gate_up.shape[1])
    scratch_b = near_chip_sum_scratch(pairs, deep, grads.shape[1])
    return pl.pallas_call(
        output_kernel,
        out_shape=(
            jax.ShapeDtypeStruct((rows, depth), BF16),
            jax.ShapeDtypeStruct((2, 8, LANES), F32),
            jax.ShapeDtypeStruct((deep // 4, grad_gate_up.shape[1]), BF16),
            jax.ShapeDtypeStruct((deep, grads.shape[1]), BF16),
        ),
        in_specs=[any_spec()] * 2 + [vmem_spec()] * 3 + [any_spec()] * 2,
        out_specs=(vmem_spec(), vmem_spec()) + (any_spec(),) * 2,
        scratch_shapes=[
            pltpu.VMEM(hidden.shape, BF16),
            pltpu.VMEM(w_down.shape, BF16),
            pltpu.VMEM((hidden.shape[0], depth), BF16),
            slots_for(n, rows, depth),
            pltpu.VMEM((n, dps, 2, 8, LANES), F32),
            pltpu.VMEM((n - 1, dps, 2, 8, LANES), F32),
            pltpu.VMEM((dps - 1, 2, 8, LANES), F32),
            *wires(n),
            dma(n + dps - 2), dma(n + dps - 2), dma(2),
            *scratch_a,
            *scratch_b,
        ],
        cost_estimate=pl.CostEstimate(
            flops=2 * hidden.shape[0] * depth * hidden.shape[1],
            bytes_accessed=20 * 2**20,
            transcendentals=0,
        ),
        compiler_params=params(6),
    )(hidden, w_down, state, gain_one, gain_two, grad_gate_up, grads)


def unpack_kernel(
    down, gate_up_a, gate_up_b, packed, output_in, tokens_in,
    grad_down, grad_gate, grad_up, grad_query, grad_key, grad_value, grad_out, output, grad_tokens,
):
    output[...] = output_in[...]
    grad_tokens[...] = tokens_in[...]
    grad_down[...] = down[...].astype(F32)
    units = grad_gate.shape[1]
    last = pl.num_programs(0) - 1

    @pl.when(pl.program_id(0) < last)
    def _():
        grad_gate[...] = gate_up_a[:, :units].astype(F32)
        grad_up[...] = gate_up_a[:, units:].astype(F32)

    @pl.when(pl.program_id(0) == last)
    def _():
        grad_gate[...] = gate_up_b[:, :units].astype(F32)
        grad_up[...] = gate_up_b[:, units:].astype(F32)

    first = 0
    for target in (grad_query, grad_key, grad_value):
        width = target.shape[1]
        target[...] = packed[:, first : first + width].astype(F32)
        first += width
    deep = grad_out.shape[2]
    for c in range(grad_out.shape[0]):
        grad_out[c] = packed[:, first + c * deep : first + (c + 1) * deep].astype(F32)


def unpack(down, gate_up_a, gate_up_b, packed, output, tokens, q_width, kv_raw):
    deep, units = packed.shape[0], gate_up_a.shape[1] // 2
    steps = 4
    rows = lambda array: (array[0] // steps, array[1])
    spec = lambda array: pl.BlockSpec(rows(array), lambda i: (i, 0))
    early = pl.BlockSpec((deep // steps, 2 * units), lambda i: (jnp.minimum(i, steps - 2), 0))
    late = pl.BlockSpec((deep // steps, 2 * units), lambda i: (0, 0))
    flat = (
        (down.shape, F32), ((deep, units), F32), ((deep, units), F32),
        ((deep, q_width), F32), ((deep, kv_raw), F32), ((deep, kv_raw), F32),
    )
    pieces = q_width // deep
    *grads, grad_out, output, tokens = pl.pallas_call(
        unpack_kernel,
        grid=(steps,),
        out_shape=(
            *[jax.ShapeDtypeStruct(shape, kind) for shape, kind in flat],
            jax.ShapeDtypeStruct((pieces, deep, deep), F32),
            jax.ShapeDtypeStruct(output.shape, BF16),
            jax.ShapeDtypeStruct(tokens.shape, BF16),
        ),
        in_specs=[
            spec(down.shape), early, late, spec(packed.shape), spec(output.shape),
            spec(tokens.shape),
        ],
        out_specs=(
            *[spec(shape) for shape, _ in flat],
            pl.BlockSpec((pieces, deep // steps, deep), lambda i: (0, i, 0)),
            spec(output.shape),
            spec(tokens.shape),
        ),
    )(down, gate_up_a, gate_up_b, packed, output, tokens)
    return *grads, grad_out.reshape(q_width, deep), output, tokens


def local(
    tokens, lengths, gain_one, w_query, w_key, w_value, w_out, gain_two, w_gate, w_up, w_down,
    cotangent,
):
    depth = tokens.shape[1]
    gain_one, gain_two = gain_one[None], gain_two[None]
    gathered_one, query, key, value, cos_table, sin_table = project(
        lengths, tokens, gain_one, w_query, w_key, w_value
    )
    attended, log_total, state, normed_two, cot_a, cot_b = attend(
        lengths, query, key, value, tokens, gain_two, w_out, cotangent
    )
    gathered_two, hidden, slope_gate, slope_up, cot_all, grad_down = hidden_units(
        normed_two, cotangent, cot_a, cot_b, w_gate, w_up
    )
    grad_state, grad_mixed, gain_two_part, grad_gate_up, _, total_down = hidden_back(
        slope_gate, slope_up, cot_all, gathered_two, state, cotangent, gain_two,
        w_down, w_gate, w_up, grad_down,
    )
    grad_tokens, gain_one_part, grads, gate_up_a = attend_back(
        lengths, grad_mixed, query, key, value, attended, log_total, cos_table, sin_table,
        tokens, gain_one, grad_state, gathered_one, w_out, w_query, w_key, w_value, grad_gate_up,
    )
    output, gains, gate_up_b, packed = layer_output(
        hidden, w_down, state, gain_one_part, gain_two_part, grad_gate_up, grads
    )
    share = depth // (lax.axis_size("tensor") * lax.axis_size("dp"))
    place = lax.rem(
        (lax.axis_index("dp") * lax.axis_size("tensor") + lax.axis_index("tensor")) * share, LANES
    )
    gains = lax.dynamic_slice_in_dim(jnp.sum(gains, axis=1), place, share, axis=1)
    (
        grad_w_down, grad_w_gate, grad_w_up, grad_w_query, grad_w_key, grad_w_value, grad_w_out,
        output, grad_tokens,
    ) = unpack(
        total_down, gate_up_a, gate_up_b, packed, output, grad_tokens,
        w_query.shape[1], w_key.shape[1],
    )
    return (
        output, grad_tokens, gains[0], grad_w_query, grad_w_key, grad_w_value, grad_w_out,
        gains[1], grad_w_gate, grad_w_up, grad_w_down,
    )


def solution(mesh):
    return jax.shard_map(
        local,
        mesh=mesh,
        in_specs=(
            P(("dp", "tensor"), None),
            P("dp", None),
            P(),
            P(None, "tensor"),
            P(None, "tensor"),
            P(None, "tensor"),
            P("tensor", None),
            P(),
            P(None, "tensor"),
            P(None, "tensor"),
            P("tensor", None),
            P(("dp", "tensor"), None),
        ),
        out_specs=(
            P(("dp", "tensor"), None),
            P(("dp", "tensor"), None),
            P(("dp", "tensor")),
            P("dp", "tensor"),
            P("dp", "tensor"),
            P("dp", "tensor"),
            P("tensor", "dp"),
            P(("dp", "tensor")),
            P("dp", "tensor"),
            P("dp", "tensor"),
            P("tensor", "dp"),
        ),
        check_vma=False,
    )
```

```python
import functools
import math

import jax
import jax.numpy as jnp
import numpy as np
from jax import lax
from jax.experimental import pallas as pl
from jax.experimental.pallas import tpu as pltpu
from jax.sharding import PartitionSpec as P

HD = 64
LANES = 128
EPSILON = 1e-05
MASKED = -1e30
LOG2E = math.log2(math.e)
SCALE2 = 0.125 * LOG2E
BF16 = jnp.bfloat16
F32 = jnp.float32
MESH = pl.DeviceIdType.MESH
VMEM_LIMIT = 60 * 2**20


def dot_nn(a, b):
    return jnp.dot(a, b, preferred_element_type=F32)


def dot_nt(a, b):
    return lax.dot_general(a, b, (((1,), (1,)), ((), ())), preferred_element_type=F32)


def dot_tn(a, b):
    return lax.dot_general(a, b, (((0,), (0,)), ((), ())), preferred_element_type=F32)


def place_tables(group):
    index = np.arange(HD // 2, dtype=np.float64)
    base = np.exp(-math.log(500000.0) * 2.0 * index / HD)
    wavelength = 2.0 * math.pi / base
    smooth = (8192.0 / wavelength - 1.0) / 3.0
    blended = (1.0 - smooth) * base / 32.0 + smooth * base
    frequency = np.where(
        wavelength < 2048.0, base, np.where(wavelength > 8192.0, base / 32.0, blended)
    )
    angles = np.arange(group, dtype=np.float64)[:, None] * frequency[None, :]
    cos_half, sin_half = np.cos(angles), np.sin(angles)
    return (
        np.concatenate([cos_half] * 4, axis=1).astype(np.float32),
        np.concatenate([-sin_half, sin_half, -sin_half, sin_half], axis=1).astype(np.float32),
    )


def ends_of(lengths):
    ends, end = [], 0
    for k in range(lengths.shape[1]):
        end = end + lengths[0, k]
        ends.append(end)
    return ends


def starts_of(places, ends):
    start = jnp.zeros_like(places)
    for end in ends:
        start = jnp.where(places >= end, end, start)
    return start


def turn_tables(ends, first, count, cos_place, sin_place):
    places = lax.broadcasted_iota(jnp.int32, (count, LANES), 0) + first
    cos_start, sin_start = jnp.ones((count, LANES), F32), jnp.zeros((count, LANES), F32)
    for end in ends:
        at = pl.ds(jnp.minimum(end, cos_place.shape[0] - 1), 1)
        cos_start = jnp.where(places >= end, cos_place[at, :], cos_start)
        sin_start = jnp.where(places >= end, sin_place[at, :], sin_start)
    rows = pl.ds(first, count)
    cos, sin = cos_place[rows, :], sin_place[rows, :]
    return cos * cos_start + sin * sin_start, sin * cos_start - cos * sin_start


class Peers:
    def __init__(self):
        self.n = lax.axis_size("tensor")
        self.m = self.n // 2
        index = lax.axis_index("tensor")
        self.y = lax.div(index, np.int32(self.m))
        self.x = lax.rem(index, np.int32(self.m))

    def at(self, flip, step):
        row = 1 - self.y if flip else self.y
        return row * self.m + lax.rem(self.x + np.int32(step + self.m), np.int32(self.m))

    def minor(self, step):
        return {"tensor": self.at(0, step)}

    def major(self):
        return {"tensor": self.at(1, 0)}

    def steps(self):
        return range(1, self.m)


def core_of():
    return lax.rem(lax.axis_index("dp"), np.int32(2))


def other_core():
    return {"dp": lax.axis_index("dp") + 1 - 2 * core_of()}


def greet(peers, core=False, chips=False):
    barrier = pltpu.get_barrier_semaphore()
    for step in peers.steps():
        pl.semaphore_signal(barrier, inc=1, device_id=peers.minor(step), device_id_type=MESH)
    pl.semaphore_signal(barrier, inc=1, device_id=peers.major(), device_id_type=MESH)
    if core:
        pl.semaphore_signal(barrier, inc=1, device_id=other_core(), device_id_type=MESH)
    more = greet_chips() if chips else 0
    pl.semaphore_wait(barrier, peers.m + (1 if core else 0) + more)


class Wire:
    def __init__(self, send_sem, recv_sem):
        self.send_sem, self.recv_sem, self.copies = send_sem, recv_sem, []

    def copy(self, source, target, device):
        k = len(self.copies)
        copy = pltpu.make_async_remote_copy(
            src_ref=source,
            dst_ref=target,
            send_sem=self.send_sem.at[k],
            recv_sem=self.recv_sem.at[k],
            device_id=device,
            device_id_type=MESH,
        )
        copy.start()
        self.copies.append(copy)
        return copy

    def wait_sends(self):
        for copy in self.copies:
            copy.wait_send()


def wire_count(n):
    return 4 * (n // 2 - 1) + 2


def wires(n):
    return [pltpu.SemaphoreType.DMA((wire_count(n),))] * 2


class Local:
    def __init__(self, sem):
        self.sem, self.copies = sem, []

    def copy(self, source, target):
        copy = pltpu.make_async_copy(source, target, self.sem.at[len(self.copies)])
        copy.start()
        self.copies.append(copy)
        return copy


def block(ref, index, rows):
    return ref.at[pl.ds(pl.multiple_of(index * rows, rows), rows)]


def half_block(ref, index, rows, half):
    size = rows // 2
    return ref.at[pl.ds(pl.multiple_of(index * rows + half * size, size), size)]


def gather(peers, wire, buf, rows):
    steps, half = list(peers.steps()), rows // 2
    part = lambda index, side: half_block(buf, index, rows, side)
    span = lambda index, side: (pl.multiple_of(index * rows + side * half, half), half)
    me, major = peers.at(0, 0), peers.at(1, 0)
    send = lambda ref, device: wire.copy(ref, ref, device)
    minor_a = [send(part(me, 0), peers.minor(j)) for j in steps]
    major_b = send(part(me, 1), peers.major())
    minor_b = [send(part(me, 1), peers.minor(j)) for j in steps]
    major_a = send(part(me, 0), peers.major())
    yield [(pl.multiple_of(me * rows, rows), rows)]
    forward = []
    for j, copy in zip(steps, minor_a):
        copy.wait_recv()
        forward.append(send(part(peers.at(0, -j), 0), peers.major()))
    major_b.wait_recv()
    forward += [send(part(major, 1), peers.minor(j)) for j in steps]
    yield [span(peers.at(0, -j), 0) for j in steps] + [span(major, 1)]
    for copy in (*minor_b, major_a):
        copy.wait_recv()
    yield [span(peers.at(0, -j), 1) for j in steps] + [span(major, 0)]
    for copy in forward:
        copy.wait_recv()
    yield [(pl.multiple_of(peers.at(1, -j) * rows, rows), rows) for j in steps]


def load_rows(ref, spans):
    return jnp.concatenate([ref[pl.ds(first, count), :] for first, count in spans], axis=0)


def store_rows(ref, spans, lanes, value):
    at = 0
    for first, count in spans:
        ref[pl.ds(first, count), lanes] = value[at : at + count]
        at += count


def add_rows(target, others, size):
    step = 16
    while step * target.shape[1] < 32768 and size % (2 * step) == 0:
        step *= 2

    def some(k, carry):
        at = pl.ds(pl.multiple_of(k * step, step), step)
        total = target[at, :].astype(F32)
        for other in others:
            total = total + other[at, :].astype(F32)
        target[at, :] = total.astype(target.dtype)
        return carry

    lax.fori_loop(0, size // step, some, 0)


def scatter(peers, wire, part_ref, slots, rows, make, meanwhile=None, tick=lambda: None, early=None):
    steps = list(peers.steps())
    part = lambda index, half: half_block(part_ref, index, rows, half)
    me, major = peers.at(0, 0), peers.at(1, 0)
    count = len(steps)
    via_a, via_b, direct_b, sum_a = (
        [slots.at[group * count + k] for k in range(count)] for group in range(4)
    )
    direct_a, sum_b = slots.at[4 * count], slots.at[4 * count + 1]
    make((1 - peers.y) * peers.m, peers.m)
    first_a, first_b = [], []
    for k, j in enumerate(steps):
        index = peers.at(1, j)
        first_a.append(wire.copy(part(index, 0), via_a[k], peers.major()))
        first_b.append(wire.copy(part(index, 1), via_b[k], peers.minor(j)))
    plain_a = wire.copy(part(major, 0), direct_a, peers.major())
    make(peers.y * peers.m, peers.m)
    plain_b = [
        wire.copy(part(peers.at(0, j), 1), direct_b[k], peers.minor(j))
        for k, j in enumerate(steps)
    ]
    tick()
    if early is not None:
        early()
    done_a = []
    for k, j in enumerate(steps):
        first_a[k].wait_recv()
        target = part(peers.at(0, j), 0)
        add_rows(target, [via_a[k]], rows // 2)
        done_a.append(wire.copy(target, sum_a[k], peers.minor(j)))
    for copy in first_b:
        copy.wait_recv()
    target = part(major, 1)
    add_rows(target, via_b, rows // 2)
    done_b = wire.copy(target, sum_b, peers.major())
    tick()
    if meanwhile is not None:
        meanwhile()
    for copy in (plain_a, *plain_b):
        copy.wait_recv()
    tick()
    for copy in (*done_a, done_b):
        copy.wait_recv()
    tick()
    return (
        (part(me, 0), direct_a, *sum_a),
        (part(me, 1), sum_b, *direct_b),
    )


def slots_for(n, rows, width):
    return pltpu.VMEM((wire_count(n), rows // 2, width), BF16)


def lane_of(rows, width=LANES):
    return lax.broadcasted_iota(jnp.int32, (rows, width), 1)


def first_head(rows):
    return lane_of(rows) < HD


def swap_halves(values):
    first = lax.rem(lane_of(values.shape[0]), np.int32(HD)) < HD // 2
    return jnp.where(first, pltpu.roll(values, LANES - HD // 2, 1), pltpu.roll(values, HD // 2, 1))


def doubled(pair, heads):
    if heads == 1:
        return [jnp.concatenate([pair, pair], axis=1)]
    out = []
    for k in range(heads // 2):
        both = pair[:, k * LANES : (k + 1) * LANES]
        swapped = pltpu.roll(both, HD, 1)
        first = first_head(both.shape[0])
        out += [jnp.where(first, both, swapped), jnp.where(first, swapped, both)]
    return out


class ChipSum:
    def __init__(self, source, base, scratch, landing, total, first, span):
        self.source, self.base, self.landing, self.total = source, base, landing, total
        self.stage, self.last, *sems = scratch
        self.send_sem, self.recv_sem, self.load_sem = sems
        self.size = lax.axis_size("dp") // 2
        self.pitch = source.shape[0] // self.size
        self.dp = lax.axis_index("dp")
        place = lax.div(self.dp, np.int32(2))
        self.place, self.along = place, (place, self.size - 1 - place)
        self.chunks = self.send_sem.shape[2]
        self.deep = landing.shape[2]
        self.rows = self.deep // self.chunks
        self.pending = None
        events = []
        step = span / ((self.size - 1) * self.chunks)
        for hop in range(self.size - 1):
            for rank in range(self.size - 1 - hop):
                for c in range(self.chunks):
                    order = rank * self.chunks + c
                    due = first + step * (order + hop) + 3.0 * hop
                    if hop == 0:
                        due = first + step * self.chunks * rank - MARGIN
                    events.append((due, hop, rank, c))
        for c in range(self.chunks):
            due = first + span - step * (self.chunks - 1 - c) + 3.0
            events.append((max(due, max(events)[0]), self.size, 0, c))
        self.events = sorted(events)

    def dest(self, flow, rank):
        return self.size - 1 - rank if flow == 0 else rank

    def chunk(self, d, c):
        return self.source.at[pl.ds(pl.multiple_of(d * self.pitch + self.base + c * self.rows, 16), self.rows)]

    def landed(self, flow, rank, c):
        return self.landing.at[flow, rank, pl.ds(c * self.rows, self.rows)]

    def remote(self, flow, rank, c, source):
        return pltpu.make_async_remote_copy(
            src_ref=source,
            dst_ref=self.landed(flow, rank, c),
            send_sem=self.send_sem.at[flow, rank, c],
            recv_sem=self.recv_sem.at[flow, rank, c],
            device_id={"dp": self.dp + (2 if flow == 0 else -2)},
            device_id_type=MESH,
        )

    def loads(self, flow, slot, sources):
        return [
            pltpu.make_async_copy(ref, self.stage.at[flow, slot, k], self.load_sem.at[flow, slot, k])
            for k, ref in enumerate(sources)
        ]

    def sources(self, flow, rank, c):
        return (self.landed(flow, rank, c), self.chunk(self.dest(flow, rank), c))

    def begin(self, hop, rank, c):
        order = rank * self.chunks + c
        for flow in range(2):
            if hop == 0:

                @pl.when(self.along[flow] == 0)
                def _():
                    if order >= AHEAD:
                        before = divmod(order - AHEAD, self.chunks)
                        self.remote(flow, *before, self.chunk(self.dest(flow, before[0]), before[1])).wait_send()
                    self.remote(flow, rank, c, self.chunk(self.dest(flow, rank), c)).start()

            else:

                @pl.when(self.along[flow] == hop)
                def _():
                    slot = order % 2
                    if order >= 2:
                        before = divmod(order - 2, self.chunks)
                        self.remote(flow, *before, self.stage.at[flow, slot, 0]).wait_send()
                    self.remote(flow, rank, c, self.stage.at[flow, slot, 0]).wait_recv()
                    for load in self.loads(flow, slot, self.sources(flow, rank, c)):
                        load.start()

    def end(self, hop, rank, c):
        order = rank * self.chunks + c
        if hop == 0:
            return
        for flow in range(2):

            @pl.when(self.along[flow] == hop)
            def _():
                slot = order % 2
                for load in self.loads(flow, slot, self.sources(flow, rank, c)):
                    load.wait()
                target = self.stage.at[flow, slot, 0]
                add_rows(target, [self.stage.at[flow, slot, 1]], self.rows)
                self.remote(flow, rank, c, target).start()

    def last_loads(self, c):
        slot = c % 2
        copies = [
            pltpu.make_async_copy(
                self.landing.at[flow, self.size - 1 - self.along[flow], pl.ds(c * self.rows, self.rows)],
                self.last.at[slot, flow],
                self.load_sem.at[flow, slot, 2],
            )
            for flow in range(2)
        ]
        own = pltpu.make_async_copy(
            self.chunk(self.place, c), self.last.at[slot, 2], self.load_sem.at[slot, 0, 3]
        )
        return copies, own

    def last_begin(self, c):
        copies, own = self.last_loads(c)
        own.start()
        for flow in range(2):

            @pl.when(self.along[flow] > 0)
            def _():
                rank = self.size - 1 - self.along[flow]
                landed = self.landing.at[flow, rank, pl.ds(c * self.rows, self.rows)]
                pltpu.make_async_remote_copy(
                    src_ref=landed,
                    dst_ref=landed,
                    send_sem=self.send_sem.at[flow, rank, c],
                    recv_sem=self.recv_sem.at[flow, rank, c],
                    device_id={"dp": self.dp},
                    device_id_type=MESH,
                ).wait_recv()
                copies[flow].start()

    def last_end(self, c):
        copies, own = self.last_loads(c)
        own.wait()
        slot = c % 2
        for flow in range(2):

            @pl.when(self.along[flow] > 0)
            def _():
                copies[flow].wait()
                add_rows(self.last.at[slot, 2], [self.last.at[slot, flow]], self.rows)

        self.save(c).start()

    def save(self, c):
        return pltpu.make_async_copy(
            self.last.at[c % 2, 2],
            self.total.at[pl.ds(c * self.rows, self.rows)],
            self.load_sem.at[c % 2, 1, 3],
        )

    def advance(self, time):
        while self.events and self.events[0][0] <= time:
            _, hop, rank, c = self.events.pop(0)
            self.settle()
            if hop == self.size:
                if c >= 2:
                    self.save(c - 2).wait()
                self.last_begin(c)
            else:
                self.begin(hop, rank, c)
            self.pending = (hop, rank, c)

    def settle(self):
        if self.pending is not None:
            hop, rank, c = self.pending
            self.pending = None
            if hop == self.size:
                self.last_end(c)
            else:
                self.end(hop, rank, c)

    def finish(self):
        self.advance(1e9)
        self.settle()
        for c in range(max(self.chunks - 2, 0), self.chunks):
            self.save(c).wait()
        for flow in range(2):
            for hop in range(self.size - 1):
                depth = AHEAD if hop == 0 else 2
                count = (self.size - 1 - hop) * self.chunks

                @pl.when(self.along[flow] == hop)
                def _():
                    for order in range(max(count - depth, 0), count):
                        rank, c = divmod(order, self.chunks)
                        if hop == 0:
                            source = self.chunk(self.dest(flow, rank), c)
                        else:
                            source = self.stage.at[flow, order % 2, 0]
                        self.remote(flow, rank, c, source).wait_send()


AHEAD = 100


class Clock:
    def __init__(self, sums):
        self.sums, self.time = sums, 0.0

    def start(self):
        for one in self.sums:
            one.start()

    def to(self, time):
        self.time = time
        for one in self.sums:
            one.advance(time)

    def by(self, step):
        self.to(self.time + step)

    def at(self, *times):
        left = list(times)
        return lambda: self.to(left.pop(0))

    def finish(self):
        for one in self.sums:
            one.finish()


MARGIN = 12.0


class NearChipSum:
    def __init__(self, source, base, scratch, total, first, span):
        self.source, self.base, self.total = source, base, total
        self.blocks, self.landing, self.send_sem, self.recv_sem, load_sem, self.save_sem = scratch
        self.size = lax.axis_size("dp") // 2
        self.pitch = source.shape[0] // self.size
        self.dp = lax.axis_index("dp")
        self.place = lax.div(self.dp, np.int32(2))
        self.along = (self.place, self.size - 1 - self.place)
        self.chunks = self.send_sem.shape[2]
        self.deep = self.landing.shape[2]
        self.rows = self.deep // self.chunks
        self.loads = [
            pltpu.make_async_copy(
                source.at[pl.ds(d * self.pitch + base, self.deep)], self.blocks.at[d], load_sem.at[d]
            )
            for d in range(self.size)
        ]
        self.step = span / ((self.size - 1) * self.chunks)
        events = []
        for rank in range(self.size - 1):
            due = first + self.step * self.chunks * rank - MARGIN
            events += [(due, 0, rank, c) for c in range(self.chunks)]
        for hop in range(1, self.size - 1):
            for rank in range(self.size - 1 - hop):
                for c in range(self.chunks):
                    due = first + self.step * (rank * self.chunks + c + hop) + hop
                    events.append((due, hop, rank, c))
        latest = max(events)[0]
        for c in range(self.chunks):
            due = max(first + span - self.step * (self.chunks - 1 - c) + 1.0, latest)
            events.append((due, self.size, 0, c))
        self.events = sorted(events)

    def dest(self, flow, rank):
        return self.size - 1 - rank if flow == 0 else rank

    def landed(self, flow, rank, c):
        return self.landing.at[flow, rank, pl.ds(c * self.rows, self.rows)]

    def remote(self, flow, rank, c, source=None):
        landed = self.landed(flow, rank, c)
        return pltpu.make_async_remote_copy(
            src_ref=landed if source is None else source,
            dst_ref=landed,
            send_sem=self.send_sem.at[flow, rank, c],
            recv_sem=self.recv_sem.at[flow, rank, c],
            device_id={"dp": self.dp + (2 if flow == 0 else -2)},
            device_id_type=MESH,
        )

    def outer(self, flow, rank, c):
        first = self.dest(flow, rank) * self.pitch + self.base + c * self.rows
        return self.remote(flow, rank, c, self.source.at[pl.ds(first, self.rows)])

    def start(self):
        for load in self.loads:
            load.start()

    def send(self, rank, c):
        for flow in range(2):

            @pl.when(self.along[flow] == 0)
            def _():
                self.outer(flow, rank, c).start()

    def pass_on(self, hop, rank, c):
        for flow in range(2):

            @pl.when(self.along[flow] == hop)
            def _():
                copy = self.remote(flow, rank, c)
                copy.wait_recv()
                own = self.blocks.at[self.dest(flow, rank), pl.ds(c * self.rows, self.rows)]
                add_rows(self.landed(flow, rank, c), [own], self.rows)
                copy.start()

    def own(self, c):
        return self.blocks.at[self.place, pl.ds(c * self.rows, self.rows)]

    def save(self, c):
        target = self.total.at[pl.ds(c * self.rows, self.rows)]
        return pltpu.make_async_copy(self.own(c), target, self.save_sem.at[c])

    def take(self, c):
        for flow in range(2):

            @pl.when(self.along[flow] > 0)
            def _():
                rank = self.size - 1 - self.along[flow]
                self.remote(flow, rank, c).wait_recv()
                add_rows(self.own(c), [self.landed(flow, rank, c)], self.rows)

        self.save(c).start()

    def advance(self, time):
        while self.events and self.events[0][0] <= time:
            _, hop, rank, c = self.events.pop(0)
            if hop == 0:
                self.send(rank, c)
                continue
            while self.loads:
                self.loads.pop().wait()
            if hop == self.size:
                self.take(c)
            else:
                self.pass_on(hop, rank, c)

    def finish(self):
        self.advance(1e9)
        for c in range(self.chunks):
            self.save(c).wait()
        for flow in range(2):
            for hop in range(self.size - 1):

                @pl.when(self.along[flow] == hop)
                def _():
                    for rank in range(self.size - 1 - hop):
                        for c in range(self.chunks):
                            copy = self.outer if hop == 0 else self.remote
                            copy(flow, rank, c).wait_send()


def near_chip_sum_scratch(size, deep, width):
    chunks = chip_chunks(size)
    dma = lambda *shape: pltpu.SemaphoreType.DMA(shape)
    return [
        pltpu.VMEM((size, deep, width), BF16),
        pltpu.VMEM((2, size - 1, deep, width), BF16),
        dma(2, size - 1, chunks),
        dma(2, size - 1, chunks),
        dma(size),
        dma(chunks),
    ]


def greet_chips():
    barrier = pltpu.get_barrier_semaphore()
    dp, dps = lax.axis_index("dp"), lax.axis_size("dp")
    for step in (2, dps - 2):
        device = {"dp": lax.rem(dp + np.int32(step), np.int32(dps))}
        pl.semaphore_signal(barrier, inc=1, device_id=device, device_id_type=MESH)
    return 2


def chip_chunks(size):
    return 4 if size == 4 else 1


def chip_sum_shapes(size, deep, width):
    chunks = chip_chunks(size)
    rows = deep // chunks
    dma = lambda *shape: pltpu.SemaphoreType.DMA(shape)
    return (
        jax.ShapeDtypeStruct((2, size - 1, deep, width), BF16),
        [
            pltpu.VMEM((2, 2, 2, rows, width), BF16),
            pltpu.VMEM((2, 3, rows, width), BF16),
            dma(2, size - 1, chunks),
            dma(2, size - 1, chunks),
            dma(2, 2, 4),
        ],
    )


def front_kernel(
    lengths, tokens, gain, gain_two, cos_place, sin_place, w_query, w_key, w_value, w_out, cotangent,
    gathered_out, query_out, key_out, value_out, cos_out, sin_out,
    attended_out, log_out, state_out, normed_out, cot_minor, cot_major,
    gathered, weights, raw_key, raw_value, query, key, value, w_buf, attended, log_total, part, slots,
    send_sem, recv_sem, sums_send, sums_recv, cot_send, cot_recv, local_sem,
):
    peers = Peers()
    rows, depth = tokens.shape
    group = gathered.shape[0]
    q_width, kv_heads = w_query.shape[1], w_key.shape[1] // HD
    kv_width = kv_heads * LANES
    local = Local(local_sem)
    load_out = local.copy(w_out, w_buf)
    loads = [
        local.copy(w_key, raw_key),
        local.copy(w_value, raw_value),
        local.copy(w_query, weights.at[:, pl.ds(0, q_width)]),
    ]
    me = peers.at(0, 0)
    gain_row = gain[...]

    def normalize(k, carry):
        values = tokens[pl.ds(pl.multiple_of(k * 16, 16), 16), :].astype(F32)
        scale = lax.rsqrt(jnp.mean(values * values, axis=-1, keepdims=True) + EPSILON)
        gathered[pl.ds(pl.multiple_of(me * rows + k * 16, 16), 16), :] = (
            values * scale * gain_row
        ).astype(BF16)
        return carry

    lax.fori_loop(0, rows // 16, normalize, 0)
    greet(peers)

    def prepare():
        ends = ends_of(lengths)

        def turn(k, carry):
            first = pl.multiple_of(k * 128, 128)
            cos, sin = turn_tables(ends, first, 128, cos_place, sin_place)
            cos_out[pl.ds(first, 128), :] = cos
            sin_out[pl.ds(first, 128), :] = sin
            return carry

        lax.fori_loop(0, group // 128, turn, 0)
        for load in loads:
            load.wait()

        def some(k, carry):
            at = pl.ds(pl.multiple_of(k * 128, 128), 128)
            for raw, base in ((raw_key, q_width), (raw_value, q_width + kv_width)):
                for j, twice in enumerate(doubled(raw[at, :].astype(F32), kv_heads)):
                    weights[at, base + j * LANES : base + (j + 1) * LANES] = twice.astype(BF16)
            return carry

        lax.fori_loop(0, depth // 128, some, 0)

    cot_wire = Wire(cot_send, cot_recv)

    def send_cotangent():
        part = lambda half: half_block(cotangent, 0, rows, half)
        landed = lambda ref, half: half_block(ref, 0, rows, half)
        for k, j in enumerate(peers.steps()):
            cot_wire.copy(part(0), landed(cot_minor.at[k], 0), peers.minor(j))
        cot_wire.copy(part(1), landed(cot_major, 1), peers.major())
        for k, j in enumerate(peers.steps()):
            cot_wire.copy(part(1), landed(cot_minor.at[k], 1), peers.minor(j))
        cot_wire.copy(part(0), landed(cot_major, 0), peers.major())

    gather_wire = Wire(send_sem, recv_sem)
    for step, spans in enumerate(gather(peers, gather_wire, gathered, rows)):
        if step == 0:
            prepare()
        if step == 3:
            saves = [local.copy(gathered, gathered_out)]
            send_cotangent()
        cos, sin = load_rows(cos_out, spans), load_rows(sin_out, spans)
        normed = load_rows(gathered, spans)
        for base, width, out, turned in (
            (0, q_width, query, True),
            (q_width, kv_width, key, True),
            (q_width + kv_width, kv_width, value, False),
        ):
            raw = dot_nn(normed, weights[:, base : base + width])
            for c in range(0, width, LANES):
                piece = raw[:, c : c + LANES]
                if turned:
                    piece = piece * cos + swap_halves(piece) * sin
                store_rows(out, spans, slice(c, c + LANES), piece.astype(BF16))
    saves += [local.copy(query, query_out), local.copy(key, key_out), local.copy(value, value_out)]
    ends = ends_of(lengths)
    pairs_per_kv = q_width // LANES // kv_heads
    log_total[...] = jnp.zeros_like(log_total)
    tile = 256
    for i in range(group // tile):
        keys = (i + 1) * tile

        def one_pair(pair, carry, i=i, keys=keys):
            at = pl.ds(i * tile, tile)
            lanes = pl.ds(pl.multiple_of(pair * LANES, LANES), LANES)
            kv_lanes = pl.ds(
                pl.multiple_of(lax.div(pair, np.int32(pairs_per_kv)) * LANES, LANES), LANES
            )
            both = query[at, lanes]
            key_rows, value_rows = key[0:keys, kv_lanes], value[0:keys, kv_lanes]
            first = first_head(tile)
            column = lax.broadcasted_iota(jnp.int32, (tile, keys), 1)
            row = lax.broadcasted_iota(jnp.int32, (tile, keys), 0) + i * tile
            start = starts_of(lax.broadcasted_iota(jnp.int32, (tile, 1), 0) + i * tile, ends)
            allowed = (column >= start) & (column <= row)
            logs = log_total[at, :]
            outs = []
            for h in range(2):
                own = first if h == 0 else jnp.logical_not(first)
                scores = dot_nt(jnp.where(own, both, jnp.zeros_like(both)), key_rows)
                scores = jnp.where(allowed, scores, MASKED)
                row_max = jnp.max(scores, axis=-1, keepdims=True)
                weights = jnp.exp2((scores - row_max) * SCALE2)
                row_sum = jnp.sum(weights, axis=-1, keepdims=True)
                outs.append(dot_nn(weights.astype(BF16), value_rows) / row_sum)
                logs = jnp.where(
                    lane_of(tile) == pair * 2 + h, row_max * SCALE2 + jnp.log2(row_sum), logs
                )
            log_total[at, :] = logs
            attended[at, lanes] = jnp.where(first, outs[0], outs[1]).astype(BF16)
            return carry

        lax.fori_loop(0, q_width // LANES, one_pair, 0)

    saves += [local.copy(attended, attended_out), local.copy(log_total, log_out)]
    load_out.wait()

    def make(first, count):
        at = pl.ds(pl.multiple_of(first * rows, rows), count * rows)
        heads = attended[at, :]
        for c in range(0, depth, 1024):
            part[at, c : c + 1024] = dot_nn(heads, w_buf[:, c : c + 1024]).astype(BF16)

    wire = Wire(sums_send, sums_recv)
    sums = scatter(peers, wire, part, slots, rows, make)
    gain_row = gain_two[...]
    half = rows // 2
    for h in range(2):

        def finish(k, carry, h=h):
            inner = pl.ds(pl.multiple_of(k * 16, 16), 16)
            outer = pl.ds(pl.multiple_of(h * half + k * 16, 16), 16)
            mixed = sums[h][0][inner, :].astype(F32)
            for other in sums[h][1:]:
                mixed = mixed + other[inner, :].astype(F32)
            state = tokens[outer, :].astype(F32) + mixed
            scale = lax.rsqrt(jnp.mean(state * state, axis=-1, keepdims=True) + EPSILON)
            state_out[outer, :] = state
            normed_out[outer, :] = (state * scale * gain_row).astype(BF16)
            return carry

        lax.fori_loop(0, half // 16, finish, 0)
    gather_wire.wait_sends()
    wire.wait_sends()
    for copy in (*cot_wire.copies, *saves):
        copy.wait()


def any_spec():
    return pl.BlockSpec(memory_space=pl.ANY)


def vmem_spec():
    return pl.BlockSpec(memory_space=pltpu.VMEM)


def params(collective_id):
    return pltpu.CompilerParams(
        collective_id=collective_id, has_side_effects=True, vmem_limit_bytes=VMEM_LIMIT
    )


def smem_spec():
    return pl.BlockSpec(memory_space=pltpu.SMEM)


def front(lengths, tokens, gain, gain_two, w_query, w_key, w_value, w_out, cotangent):
    n = lax.axis_size("tensor")
    m = n // 2
    rows, depth = tokens.shape
    group = rows * n
    q_width, kv_raw = w_query.shape[1], w_key.shape[1]
    kv_width = kv_raw // HD * LANES
    heads = [(group, q_width), (group, kv_width), (group, kv_width)]
    low = lambda *shape: jax.ShapeDtypeStruct(shape, BF16)
    return pl.pallas_call(
        front_kernel,
        out_shape=(
            low(group, depth),
            *[low(*shape) for shape in heads],
            jax.ShapeDtypeStruct((group, LANES), F32),
            jax.ShapeDtypeStruct((group, LANES), F32),
            low(group, q_width),
            jax.ShapeDtypeStruct((group, LANES), F32),
            jax.ShapeDtypeStruct((rows, depth), F32),
            low(rows, depth),
            low(m - 1, rows, depth),
            low(rows, depth),
        ),
        in_specs=[smem_spec()] + [vmem_spec()] * 5 + [any_spec()] * 5,
        out_specs=(
            *[any_spec()] * 4, vmem_spec(), vmem_spec(), any_spec(), any_spec(),
            vmem_spec(), vmem_spec(), any_spec(), any_spec(),
        ),
        scratch_shapes=[
            pltpu.VMEM((group, depth), BF16),
            pltpu.VMEM((depth, q_width + 2 * kv_width), BF16),
            pltpu.VMEM((depth, kv_raw), BF16),
            pltpu.VMEM((depth, kv_raw), BF16),
            *[pltpu.VMEM(shape, BF16) for shape in heads],
            pltpu.VMEM(w_out.shape, BF16),
            pltpu.VMEM((group, q_width), BF16),
            pltpu.VMEM((group, LANES), F32),
            pltpu.VMEM((group, depth), BF16),
            slots_for(n, rows, depth),
            *wires(n),
            *wires(n),
            pltpu.SemaphoreType.DMA((2 * m,)),
            pltpu.SemaphoreType.DMA((2 * m,)),
            pltpu.SemaphoreType.DMA((10,)),
        ],
        cost_estimate=pl.CostEstimate(
            flops=2 * group * depth * (2 * q_width + 2 * kv_width),
            bytes_accessed=60 * 2**20,
            transcendentals=0,
        ),
        compiler_params=params(1),
    )(
        lengths, tokens, gain, gain_two, *place_tables(group), w_query, w_key, w_value, w_out,
        cotangent,
    )


class Exchange:
    def __init__(self, wire, stage, received):
        self.wire, self.stage, self.received, self.sent = wire, stage, received, []

    def run(self, jobs, tick=lambda: None):
        mine = core_of()
        copies = []
        for k in range(len(jobs) + 1):
            if k < len(jobs):
                tile, save, pair = jobs[k]
                slot = self.stage.at[k % 2]
                if k >= 2:
                    copies[k - 2].wait_send()
                tile(2 * pair + 1 - mine, slot, False)
                copies.append(self.wire.copy(slot, self.received.at[k], other_core()))
                tick()
            if k >= 1:
                tile, save, pair = jobs[k - 1]
                copies[k - 1].wait_recv()
                tile(2 * pair + mine, self.received.at[k - 1], True)
                save(pair, self.received.at[k - 1])
                tick()
        for copy in copies[-2:]:
            copy.wait_send()


def put(target, at, value, add):
    if add:
        value = value + target[at].astype(F32)
    target[at] = value.astype(BF16)


def hidden_kernel(
    normed, cotangent, cot_minor, cot_major, w_gate, w_up,
    gathered_out, hidden_out, slope_gate_out, slope_up_out, cot_out, grad_down_out,
    gathered, gate_buf, up_buf, hidden, slope_gate, slope_up, cot, stage, received,
    send_sem, recv_sem, cot_send, cot_recv, core_send, core_recv, local_sem,
):
    peers = Peers()
    rows, depth = normed.shape
    units = w_gate.shape[1]
    me, major = peers.at(0, 0), peers.at(1, 0)
    local = Local(local_sem)
    first_load = local.copy(normed, block(gathered, me, rows))
    loads = [local.copy(w_gate, gate_buf), local.copy(w_up, up_buf)]
    cot_loads = [local.copy(cotangent, block(cot, me, rows))]
    for k, j in enumerate(peers.steps()):
        cot_loads.append(local.copy(cot_minor.at[k], block(cot, peers.at(0, -j), rows)))
    cot_loads.append(local.copy(cot_major, block(cot, major, rows)))
    greet(peers, core=True)
    first_load.wait()

    def use(spans):
        tile = 512

        def some(k, carry):
            lanes = pl.ds(pl.multiple_of(k * tile, tile), tile)
            x = load_rows(gathered, spans)
            gate = dot_nn(x, gate_buf[:, lanes])
            up = dot_nn(x, up_buf[:, lanes])
            sigmoid = jax.nn.sigmoid(gate)
            silu = gate * sigmoid
            slope = up * sigmoid * (1.0 + gate * (1.0 - sigmoid))
            store_rows(hidden, spans, lanes, (silu * up).astype(BF16))
            store_rows(slope_up, spans, lanes, silu.astype(BF16))
            store_rows(slope_gate, spans, lanes, slope.astype(BF16))
            return carry

        lax.fori_loop(0, units // tile, some, 0)

    cot_wire = Wire(cot_send, cot_recv)
    rest = ([], [])
    width = depth // 2

    def send_rest():
        for load in cot_loads:
            load.wait()
        for side in range(2):
            lanes = pl.ds(side * width, width)

            def send(index, half, device):
                ref = half_block(cot, index, rows, half).at[:, lanes]
                rest[side].append(cot_wire.copy(ref, ref, device))

            for j in peers.steps():
                send(major, 1, peers.minor(j))
            for j in peers.steps():
                send(peers.at(0, -j), 0, peers.major())

    wire = Wire(send_sem, recv_sem)
    for step, spans in enumerate(gather(peers, wire, gathered, rows)):
        if step == 0:
            for load in loads:
                load.wait()
        if step == 3:
            send_rest()
        use(spans)
    saves = [
        local.copy(gathered, gathered_out),
        local.copy(hidden, hidden_out),
        local.copy(slope_gate, slope_gate_out),
        local.copy(slope_up, slope_up_out),
    ]
    columns = stage.shape[2]
    pairs = received.shape[0]
    arrived = set()

    def tile_of(side):
        def tile(index, target, add):
            if side not in arrived:
                arrived.add(side)
                for copy in rest[side]:
                    copy.wait_recv()
            lanes = pl.ds(pl.multiple_of(index * columns, columns), columns)
            step = 512

            def some(k, carry):
                at = pl.ds(pl.multiple_of(k * step, step), step)
                put(target, (at, slice(None)), dot_tn(hidden[:, at], cot[:, lanes]), add)
                return carry

            lax.fori_loop(0, units // step, some, 0)

        return tile

    def save(k, ref):
        saves.append(local.copy(ref, grad_down_out.at[pl.ds(k * units, units)]))

    Exchange(Wire(core_send, core_recv), stage, received).run(
        [(tile_of(2 * k // pairs), save, k) for k in range(pairs)]
    )
    saves.append(local.copy(cot, cot_out))
    wire.wait_sends()
    cot_wire.wait_sends()
    for copy in saves:
        copy.wait()


def hidden_units(normed, cotangent, cot_minor, cot_major, w_gate, w_up):
    n = lax.axis_size("tensor")
    pairs = lax.axis_size("dp") // 2
    rows, depth = normed.shape
    group, units, columns = rows * n, w_gate.shape[1], depth // (2 * pairs)
    wide = lambda width: jax.ShapeDtypeStruct((group, width), BF16)
    return pl.pallas_call(
        hidden_kernel,
        out_shape=(
            wide(depth), wide(units), wide(units), wide(units), wide(depth),
            jax.ShapeDtypeStruct((pairs * units, columns), BF16),
        ),
        in_specs=[any_spec()] * 6,
        out_specs=(any_spec(),) * 6,
        scratch_shapes=[
            pltpu.VMEM((group, depth), BF16),
            pltpu.VMEM((depth, units), BF16),
            pltpu.VMEM((depth, units), BF16),
            pltpu.VMEM((group, units), BF16),
            pltpu.VMEM((group, units), BF16),
            pltpu.VMEM((group, units), BF16),
            pltpu.VMEM((group, depth), BF16),
            pltpu.VMEM((2, units, columns), BF16),
            pltpu.VMEM((pairs, units, columns), BF16),
            *wires(n),
            pltpu.SemaphoreType.DMA((2 * wire_count(n),)),
            pltpu.SemaphoreType.DMA((2 * wire_count(n),)),
            pltpu.SemaphoreType.DMA((pairs,)),
            pltpu.SemaphoreType.DMA((pairs,)),
            pltpu.SemaphoreType.DMA((3 + n // 2 + 1 + 5 + pairs,)),
        ],
        cost_estimate=pl.CostEstimate(
            flops=6 * group * depth * units, bytes_accessed=60 * 2**20, transcendentals=0
        ),
        compiler_params=params(3),
    )(normed, cotangent, cot_minor, cot_major, w_gate, w_up)


def norm_back(values, gain_row, grad_normed):
    scale = lax.rsqrt(jnp.mean(values * values, axis=-1, keepdims=True) + EPSILON)
    unit = values * scale
    scaled = grad_normed * gain_row
    grad = scale * (scaled - unit * jnp.mean(scaled * unit, axis=-1, keepdims=True))
    return grad, grad_normed * unit


def fold_rows(values):
    return values[:8] + values[8:]


def hidden_back_kernel(
    slope_gate, slope_up, cot_all, gathered_in, state, cotangent, gain, w_down, w_gate, w_up, grad_down,
    grad_state_out, grad_mixed_out, gain_out, grad_gate_up_out, landing, total_down,
    gate_buf, up_buf, down_buf, grad_gate, grad_up, cot, part, slots, stage, received,
    send_sem, recv_sem, core_send, core_recv, local_sem, *chip_scratch,
):
    peers = Peers()
    rows, depth = state.shape
    group, units = slope_gate.shape
    chunk = down_buf.shape[1]
    chunks = units // chunk
    local = Local(local_sem)
    load_cot = local.copy(cot_all, cot)

    def load_down(k):
        source = w_down.at[pl.ds(k % chunks * chunk, chunk)]
        return local.copy(source, down_buf.at[k % 2])

    downs = [load_down(0)]
    slopes = [local.copy(slope_gate, grad_gate), local.copy(slope_up, grad_up)]
    downs.append(load_down(1))
    greet(peers, core=True, chips=True)
    clock = Clock([ChipSum(grad_down, 0, chip_scratch, landing, total_down, 4.0, 72.0)])
    clock.to(1.0)
    later = []

    def make(first, count):
        at = pl.ds(pl.multiple_of(first * rows, rows), count * rows)
        base = chunks if later else 0
        for c in range(chunks):
            downs[base + c].wait()
            if not later:
                load_cot.wait()
                for load in slopes:
                    load.wait()
                later.extend(
                    [
                        local.copy(w_gate, gate_buf),
                        local.copy(w_up, up_buf),
                        local.copy(state, grad_state_out),
                    ]
                )
            lanes = slice(c * chunk, (c + 1) * chunk)
            grad_hidden = dot_nt(cot[at, :], down_buf[c % 2])
            grad_gate[at, lanes] = (grad_hidden * grad_gate[at, lanes].astype(F32)).astype(BF16)
            grad_up[at, lanes] = (grad_hidden * grad_up[at, lanes].astype(F32)).astype(BF16)
            if base + c + 2 < 2 * chunks:
                downs.append(load_down(base + c + 2))
            clock.by(7.0 if base + c == 0 else 1.5)
        if base == 0:
            for load in later[:2]:
                load.wait()
        else:
            later.append(local.copy(gathered_in, cot))
        step = 512

        for k in range(depth // step):
            inner = slice(k * step, (k + 1) * step)
            total = dot_nt(grad_gate[at, :], gate_buf[inner, :])
            total = total + dot_nt(grad_up[at, :], up_buf[inner, :])
            part[at, inner] = total.astype(BF16)
            clock.by(2.7)

    deep = stage.shape[1]
    saves = []

    def tile_of(grad):
        def tile(index, target, add):
            lanes = pl.ds(pl.multiple_of(index * deep, deep), deep)
            step = min(1024, units)

            def some(k, carry):
                inner = pl.ds(pl.multiple_of(k * step, step), step)
                put(target, (slice(None), inner), dot_tn(cot[:, lanes], grad[:, inner]), add)
                return carry

            lax.fori_loop(0, units // step, some, 0)

        return tile

    def save_at(base):
        def save(k, ref):
            target = grad_gate_up_out.at[pl.ds(k * deep, deep), pl.ds(base, units)]
            saves.append(local.copy(ref, target))

        return save

    def weight_grads():
        later[3].wait()
        pairs = received.shape[0] // 2
        Exchange(Wire(core_send, core_recv), stage, received).run(
            [(tile_of(grad_gate), save_at(0), k) for k in range(pairs)]
            + [(tile_of(grad_up), save_at(units), k) for k in range(pairs)],
            lambda: clock.by(1.6),
        )

    wire = Wire(send_sem, recv_sem)
    sums = scatter(peers, wire, part, slots, rows, make, weight_grads, lambda: clock.by(0.5))
    later[2].wait()
    gain_row = gain[...]
    half = rows // 2
    gain_out[...] = jnp.zeros_like(gain_out)
    for h in range(2):

        def finish(k, carry, h=h):
            inner = pl.ds(pl.multiple_of(k * 16, 16), 16)
            outer = pl.ds(pl.multiple_of(h * half + k * 16, 16), 16)
            grad_normed = sums[h][0][inner, :].astype(F32)
            for other in sums[h][1:]:
                grad_normed = grad_normed + other[inner, :].astype(F32)
            grad, gain_part = norm_back(grad_state_out[outer, :], gain_row, grad_normed)
            grad = grad + cotangent[outer, :].astype(F32)
            gain_out[...] += fold_rows(gain_part)
            grad_state_out[outer, :] = grad
            grad_mixed_out[outer, :] = grad.astype(BF16)
            return carry

        lax.fori_loop(0, half // 16, finish, 0)
    clock.finish()
    wire.wait_sends()
    for copy in saves:
        copy.wait()


def hidden_back(
    slope_gate, slope_up, cot_all, gathered, state, cotangent, gain, w_down, w_gate, w_up, grad_down
):
    n = lax.axis_size("tensor")
    pairs = lax.axis_size("dp") // 2
    rows, depth = state.shape
    group, units = slope_gate.shape
    deep = depth // (2 * pairs)
    chunk = 512
    landing, chip_scratch = chip_sum_shapes(pairs, units, grad_down.shape[1])
    return pl.pallas_call(
        hidden_back_kernel,
        out_shape=(
            jax.ShapeDtypeStruct((rows, depth), F32),
            jax.ShapeDtypeStruct((rows, depth), BF16),
            jax.ShapeDtypeStruct((8, depth), F32),
            jax.ShapeDtypeStruct((pairs * deep, 2 * units), BF16),
            landing,
            jax.ShapeDtypeStruct((units, grad_down.shape[1]), BF16),
        ),
        in_specs=[any_spec()] * 5 + [vmem_spec()] * 2 + [any_spec()] * 4,
        out_specs=(vmem_spec(), vmem_spec(), vmem_spec(), any_spec(), any_spec(), any_spec()),
        scratch_shapes=[
            pltpu.VMEM((depth, units), BF16),
            pltpu.VMEM((depth, units), BF16),
            pltpu.VMEM((2, chunk, depth), BF16),
            pltpu.VMEM((group, units), BF16),
            pltpu.VMEM((group, units), BF16),
            pltpu.VMEM((group, depth), BF16),
            pltpu.VMEM((group, depth), BF16),
            slots_for(n, rows, depth),
            pltpu.VMEM((2, deep, units), BF16),
            pltpu.VMEM((2 * pairs, deep, units), BF16),
            *wires(n),
            pltpu.SemaphoreType.DMA((2 * pairs,)),
            pltpu.SemaphoreType.DMA((2 * pairs,)),
            pltpu.SemaphoreType.DMA((7 + 2 * (units // chunk) + 2 * pairs,)),
            *chip_scratch,
        ],
        cost_estimate=pl.CostEstimate(
            flops=10 * group * depth * units, bytes_accessed=80 * 2**20, transcendentals=0
        ),
        compiler_params=params(4),
    )(
        slope_gate, slope_up, cot_all, gathered, state, cotangent, gain, w_down, w_gate, w_up,
        grad_down,
    )


def attend_back_kernel(
    lengths, gain, grad_mixed, query_in, key_in, value_in, attended_in, log_in, cos_in, sin_in,
    tokens_in, state_in, gathered_in, w_out, w_query, w_key, w_value, grad_gate_up,
    grad_tokens_out, gain_out, grads_out, total_gate_up,
    query, key, value, attended, log_total, cos_table, sin_table, tokens, grad_state,
    mixed, out_buf, query_buf, key_buf, value_buf, gathered, grad_att, key_acc, value_acc, grads, part, slots,
    stage_out, got_out, stage_qkv, got_qkv,
    send_sem, recv_sem, sums_send, sums_recv, out_send, out_recv, qkv_send, qkv_recv, local_sem, *chip_scratch,
):
    peers = Peers()
    rows, depth = tokens.shape
    group, q_width = query.shape
    kv_heads = w_key.shape[1] // HD
    kv_raw = kv_heads * HD
    pairs_per_kv = q_width // LANES // kv_heads
    me = peers.at(0, 0)
    local = Local(local_sem)
    first_load = local.copy(grad_mixed, block(mixed, me, rows))
    load_out = local.copy(w_out, out_buf)
    sources = (
        query_in, key_in, value_in, attended_in, log_in, cos_in, sin_in, tokens_in, state_in
    )
    buffers = (query, key, value, attended, log_total, cos_table, sin_table, tokens, grad_state)
    loads = [local.copy(source, buffer) for source, buffer in zip(sources, buffers)]
    loads += [
        local.copy(w_query, query_buf),
        local.copy(w_key, key_buf),
        local.copy(w_value, value_buf),
        local.copy(gathered_in, gathered),
    ]
    greet(peers, core=True, chips=True)
    clock = Clock([NearChipSum(grad_gate_up, 0, chip_scratch, total_gate_up, 0.0, 108.0)])
    clock.start()
    clock.to(0.5)
    first_load.wait()
    ends, saves = ends_of(lengths), []
    gather_wire = Wire(send_sem, recv_sem)
    for step, spans in enumerate(gather(peers, gather_wire, mixed, rows)):
        if step == 0:
            load_out.wait()
        grad_rows = dot_nt(load_rows(mixed, spans), out_buf[...]).astype(BF16)
        store_rows(grad_att, spans, slice(None), grad_rows)
        clock.to(1.0 + 12.0 * step)

    for load in loads:
        load.wait()
    columns = stage_out.shape[2]

    def out_tile(index, target, add):
        lanes = pl.ds(pl.multiple_of(index * columns, columns), columns)
        put(target, (slice(None), slice(None)), dot_tn(attended[...], mixed[:, lanes]), add)

    pairs = got_out.shape[0]
    width = grads.shape[1]

    def out_save(k, ref):
        for c in range(q_width // columns):
            target = grads_out.at[
                pl.ds(k * columns, columns), pl.ds(width + c * columns, columns)
            ]
            saves.append(local.copy(ref.at[pl.ds(c * columns, columns)], target))

    key_acc[...] = jnp.zeros_like(key_acc)
    value_acc[...] = jnp.zeros_like(value_acc)
    tile = 256
    for i in range(group // tile):
        keys = (i + 1) * tile

        def one_pair(pair, carry, i=i, keys=keys):
            at = pl.ds(i * tile, tile)
            lanes = pl.ds(pl.multiple_of(pair * LANES, LANES), LANES)
            kv_lanes = pl.ds(
                pl.multiple_of(lax.div(pair, np.int32(pairs_per_kv)) * LANES, LANES), LANES
            )
            both, grad_both = query[at, lanes], grad_att[at, lanes]
            key_rows, value_rows = key[0:keys, kv_lanes], value[0:keys, kv_lanes]
            first = first_head(tile)
            dots = grad_both.astype(F32) * attended[at, lanes].astype(F32)
            column = lax.broadcasted_iota(jnp.int32, (tile, keys), 1)
            row = lax.broadcasted_iota(jnp.int32, (tile, keys), 0) + i * tile
            start = starts_of(lax.broadcasted_iota(jnp.int32, (tile, 1), 0) + i * tile, ends)
            allowed = (column >= start) & (column <= row)
            logs = log_total[at, :]
            grad_queries, grad_keys, grad_values = [], 0.0, 0.0
            for h in range(2):
                own = first if h == 0 else jnp.logical_not(first)
                own_query = jnp.where(own, both, jnp.zeros_like(both))
                own_grad = jnp.where(own, grad_both, jnp.zeros_like(grad_both))
                row_dot = jnp.sum(jnp.where(own, dots, 0.0), axis=-1, keepdims=True)
                scores = dot_nt(own_query, key_rows)
                log_row = jnp.sum(
                    jnp.where(lane_of(tile) == pair * 2 + h, logs, 0.0), axis=-1, keepdims=True
                )
                probs = jnp.exp2(scores * SCALE2 - log_row)
                probs = jnp.where(allowed, probs, 0.0)
                grad_probs = dot_nt(own_grad, value_rows)
                grad_scores = (probs * (grad_probs - row_dot)).astype(BF16)
                grad_queries.append(dot_nn(grad_scores, key_rows))
                grad_keys = grad_keys + dot_tn(grad_scores, own_query)
                grad_values = grad_values + dot_tn(probs.astype(BF16), own_grad)
            key_acc[0:keys, kv_lanes] += grad_keys
            value_acc[0:keys, kv_lanes] += grad_values
            turned = jnp.where(first, grad_queries[0], grad_queries[1]) * 0.125
            turned = turned * cos_table[at, :] - swap_halves(turned) * sin_table[at, :]
            grads[at, lanes] = turned.astype(BF16)
            return carry

        lax.fori_loop(0, q_width // LANES, one_pair, 0)
        clock.by(2.1 * (i + 1))

    def fold(k, carry):
        at = pl.ds(pl.multiple_of(k * 128, 128), 128)
        cos, sin = cos_table[at, :], sin_table[at, :]
        key_heads, value_heads = [], []
        for j in range(kv_heads):
            lanes = slice(j * LANES, (j + 1) * LANES)
            both = key_acc[at, lanes] * 0.125
            both = both + pltpu.roll(both, HD, 1)
            key_heads.append(both * cos - swap_halves(both) * sin)
            both = value_acc[at, lanes]
            value_heads.append(both + pltpu.roll(both, HD, 1))
        for heads, base in ((key_heads, q_width), (value_heads, q_width + kv_raw)):
            if kv_heads == 1:
                grads[at, base : base + HD] = heads[0][:, :HD].astype(BF16)
            for j in range(0, kv_heads - 1, 2):
                pair = jnp.where(first_head(128), heads[j], heads[j + 1])
                grads[at, base + j * HD : base + (j + 2) * HD] = pair.astype(BF16)
        return carry

    lax.fori_loop(0, group // 128, fold, 0)

    def make(first, count):
        at = pl.ds(pl.multiple_of(first * rows, rows), count * rows)
        step = 1024
        for c in range(0, depth, step):
            inner = slice(c, c + step)
            total = dot_nt(grads[at, 0:q_width], query_buf[inner, :])
            total = total + dot_nt(grads[at, q_width : q_width + kv_raw], key_buf[inner, :])
            total = total + dot_nt(grads[at, q_width + kv_raw :], value_buf[inner, :])
            part[at, inner] = total.astype(BF16)
            clock.by(1.2)

    deep = stage_qkv.shape[1]

    def qkv_tile(index, target, add):
        lanes = pl.ds(pl.multiple_of(index * deep, deep), deep)
        put(target, (slice(None), slice(None)), dot_tn(gathered[:, lanes], grads[...]), add)

    def qkv_save(k, ref):
        target = grads_out.at[pl.ds(k * deep, deep), pl.ds(0, width)]
        saves.append(local.copy(ref, target))

    def weight_grads():
        Exchange(Wire(out_send, out_recv), stage_out, got_out).run(
            [(out_tile, out_save, k) for k in range(pairs)], lambda: clock.by(0.5)
        )
        Exchange(Wire(qkv_send, qkv_recv), stage_qkv, got_qkv).run(
            [(qkv_tile, qkv_save, k) for k in range(pairs)], lambda: clock.by(0.9)
        )

    wire = Wire(sums_send, sums_recv)
    sums = scatter(
        peers, wire, part, slots, rows, make, tick=clock.at(66.0, 80.0, 90.0, 101.0), early=weight_grads
    )
    gain_row = gain[...]
    half = rows // 2
    gain_out[...] = jnp.zeros_like(gain_out)
    for h in range(2):

        def finish(k, carry, h=h):
            inner = pl.ds(pl.multiple_of(k * 16, 16), 16)
            outer = pl.ds(pl.multiple_of(h * half + k * 16, 16), 16)
            grad_normed = sums[h][0][inner, :].astype(F32)
            for other in sums[h][1:]:
                grad_normed = grad_normed + other[inner, :].astype(F32)
            grad, gain_part = norm_back(tokens[outer, :].astype(F32), gain_row, grad_normed)
            gain_out[...] += fold_rows(gain_part)
            grad_tokens_out[outer, :] = (grad + grad_state[outer, :]).astype(BF16)
            return carry

        lax.fori_loop(0, half // 16, finish, 0)
    clock.finish()
    gather_wire.wait_sends()
    wire.wait_sends()
    for copy in saves:
        copy.wait()


def attend_back(
    lengths, grad_mixed, query, key, value, attended, log_total, cos_table, sin_table,
    tokens, gain, grad_state, gathered, w_out, w_query, w_key, w_value, grad_gate_up,
):
    n = lax.axis_size("tensor")
    pairs = lax.axis_size("dp") // 2
    rows, depth = tokens.shape
    group, q_width = query.shape
    kv_width, kv_raw = key.shape[1], w_key.shape[1]
    width = q_width + 2 * kv_raw
    deep = depth // (2 * pairs)
    dma = lambda count: pltpu.SemaphoreType.DMA((count,))
    early = deep - deep // 4
    chip_scratch = near_chip_sum_scratch(pairs, early, grad_gate_up.shape[1])
    return pl.pallas_call(
        attend_back_kernel,
        out_shape=(
            jax.ShapeDtypeStruct((rows, depth), BF16),
            jax.ShapeDtypeStruct((8, depth), F32),
            jax.ShapeDtypeStruct((pairs * deep, width + q_width), BF16),
            jax.ShapeDtypeStruct((early, grad_gate_up.shape[1]), BF16),
        ),
        in_specs=[smem_spec(), vmem_spec()] + [any_spec()] * 16,
        out_specs=(vmem_spec(), vmem_spec(), any_spec(), any_spec()),
        scratch_shapes=[
            *[
                pltpu.VMEM(source.shape, source.dtype)
                for source in (
                    query, key, value, attended, log_total, cos_table, sin_table, tokens, grad_state
                )
            ],
            pltpu.VMEM((group, depth), BF16),
            pltpu.VMEM(w_out.shape, BF16),
            pltpu.VMEM(w_query.shape, BF16),
            pltpu.VMEM(w_key.shape, BF16),
            pltpu.VMEM(w_value.shape, BF16),
            pltpu.VMEM((group, depth), BF16),
            pltpu.VMEM((group, q_width), BF16),
            pltpu.VMEM((group, kv_width), F32),
            pltpu.VMEM((group, kv_width), F32),
            pltpu.VMEM((group, width), BF16),
            pltpu.VMEM((group, depth), BF16),
            slots_for(n, rows, depth),
            pltpu.VMEM((2, q_width, deep), BF16),
            pltpu.VMEM((pairs, q_width, deep), BF16),
            pltpu.VMEM((2, deep, width), BF16),
            pltpu.VMEM((pairs, deep, width), BF16),
            *wires(n),
            *wires(n),
            dma(pairs), dma(pairs), dma(pairs), dma(pairs), dma(15 + pairs * (1 + q_width // deep)),
            *chip_scratch,
        ],
        cost_estimate=pl.CostEstimate(
            flops=2 * group * depth * q_width * 12, bytes_accessed=60 * 2**20, transcendentals=0
        ),
        compiler_params=params(5),
    )(lengths, gain, grad_mixed, query, key, value, attended, log_total, cos_table, sin_table,
      tokens, grad_state, gathered, w_out, w_query, w_key, w_value, grad_gate_up)


class GainSums:
    def __init__(self, gains, tiles, from_tensor, from_dp, wire, chunk):
        self.gains, self.tiles, self.from_tensor, self.from_dp = gains, tiles, from_tensor, from_dp
        self.wire, self.n, self.dps = wire, lax.axis_size("tensor"), lax.axis_size("dp")
        self.chunk = chunk
        self.me, self.dp = lax.axis_index("tensor"), lax.axis_index("dp")

    def tensor(self, step):
        return lax.rem(self.me + np.int32(step), np.int32(self.n))

    def data(self, step):
        return lax.rem(self.dp + np.int32(step), np.int32(self.dps))

    def greet(self):
        barrier = pltpu.get_barrier_semaphore()
        for step in range(1, self.n):
            device = {"tensor": self.tensor(step)}
            pl.semaphore_signal(barrier, inc=1, device_id=device, device_id_type=MESH)
        for step in range(1, self.dps):
            device = {"dp": self.data(step)}
            pl.semaphore_signal(barrier, inc=1, device_id=device, device_id_type=MESH)
        pl.semaphore_wait(barrier, self.n + self.dps - 2)

    def start(self):
        for t in range(self.n):
            for d in range(self.dps):
                lane = (d * self.n + t) * self.chunk // LANES * LANES
                for k, gain in enumerate(self.gains):
                    self.tiles[t, d, k] = gain[:, lane : lane + LANES]
        self.first = [
            self.wire.copy(
                self.tiles.at[self.tensor(step)],
                self.from_tensor.at[step - 1],
                {"tensor": self.tensor(step)},
            )
            for step in range(1, self.n)
        ]

    def forward(self):
        for copy in self.first:
            copy.wait_recv()
        total = self.tiles[self.me]
        for step in range(1, self.n):
            total = total + self.from_tensor[step - 1]
        self.from_tensor[0] = total
        self.second = [
            self.wire.copy(
                self.from_tensor.at[0, self.data(step)],
                self.from_dp.at[step - 1],
                {"dp": self.data(step)},
            )
            for step in range(1, self.dps)
        ]

    def finish(self, out):
        for copy in self.second:
            copy.wait_recv()
        total = self.from_tensor[0, self.dp]
        for step in range(1, self.dps):
            total = total + self.from_dp[step - 1]
        out[...] = total


def output_kernel(
    hidden_in, w_down, state, gain_one, gain_two, grad_gate_up, grads,
    output, gains_out, total_gate_up, total_grads,
    hidden, down_buf, part, slots, tiles, from_tensor, from_dp,
    send_sem, recv_sem, gain_send, gain_recv, local_sem, *chip_scratch,
):
    peers = Peers()
    rows, depth = state.shape
    local = Local(local_sem)
    loads = [local.copy(hidden_in, hidden), local.copy(w_down, down_buf)]
    chunk = depth // (lax.axis_size("tensor") * lax.axis_size("dp"))
    gains = GainSums(
        (gain_one, gain_two), tiles, from_tensor, from_dp, Wire(gain_send, gain_recv), chunk
    )
    gains.greet()
    base = grad_gate_up.shape[0] // (lax.axis_size("dp") // 2) - total_gate_up.shape[0]
    half = len(chip_scratch) // 2
    clock = Clock(
        [
            NearChipSum(grad_gate_up, base, chip_scratch[:half], total_gate_up, 0.0, 36.0),
            NearChipSum(grads, 0, chip_scratch[half:], total_grads, 36.0, 45.0),
        ]
    )
    clock.start()
    clock.to(0.5)
    gains.start()
    for load in loads:
        load.wait()

    def make(first, count):
        at = pl.ds(pl.multiple_of(first * rows, rows), count * rows)
        step = 512

        for k in range(depth // step):
            lanes = slice(k * step, (k + 1) * step)
            part[at, lanes] = dot_nn(hidden[at, :], down_buf[:, lanes]).astype(BF16)
            clock.by(1.6)

    wire = Wire(send_sem, recv_sem)
    ticks = clock.at(17.0, 29.0, 35.0, 47.0)
    sums = scatter(peers, wire, part, slots, rows, make, gains.forward, ticks)
    half = rows // 2
    for h in range(2):

        def finish(k, carry, h=h):
            inner = pl.ds(pl.multiple_of(k * 16, 16), 16)
            outer = pl.ds(pl.multiple_of(h * half + k * 16, 16), 16)
            total = sums[h][0][inner, :].astype(F32)
            for other in sums[h][1:]:
                total = total + other[inner, :].astype(F32)
            output[outer, :] = (state[outer, :] + total).astype(BF16)
            return carry

        lax.fori_loop(0, half // 16, finish, 0)
    gains.finish(gains_out)
    clock.finish()
    wire.wait_sends()
    gains.wire.wait_sends()


def layer_output(hidden, w_down, state, gain_one, gain_two, grad_gate_up, grads):
    n, dps = lax.axis_size("tensor"), lax.axis_size("dp")
    rows, depth = state.shape
    dma = lambda count: pltpu.SemaphoreType.DMA((count,))
    pairs = dps // 2
    deep = grads.shape[0] // pairs
    scratch_a = near_chip_sum_scratch(pairs, deep // 4, grad_gate_up.shape[1])
    scratch_b = near_chip_sum_scratch(pairs, deep, grads.shape[1])
    return pl.pallas_call(
        output_kernel,
        out_shape=(
            jax.ShapeDtypeStruct((rows, depth), BF16),
            jax.ShapeDtypeStruct((2, 8, LANES), F32),
            jax.ShapeDtypeStruct((deep // 4, grad_gate_up.shape[1]), BF16),
            jax.ShapeDtypeStruct((deep, grads.shape[1]), BF16),
        ),
        in_specs=[any_spec()] * 2 + [vmem_spec()] * 3 + [any_spec()] * 2,
        out_specs=(vmem_spec(), vmem_spec()) + (any_spec(),) * 2,
        scratch_shapes=[
            pltpu.VMEM(hidden.shape, BF16),
            pltpu.VMEM(w_down.shape, BF16),
            pltpu.VMEM((hidden.shape[0], depth), BF16),
            slots_for(n, rows, depth),
            pltpu.VMEM((n, dps, 2, 8, LANES), F32),
            pltpu.VMEM((n - 1, dps, 2, 8, LANES), F32),
            pltpu.VMEM((dps - 1, 2, 8, LANES), F32),
            *wires(n),
            dma(n + dps - 2), dma(n + dps - 2), dma(2),
            *scratch_a,
            *scratch_b,
        ],
        cost_estimate=pl.CostEstimate(
            flops=2 * hidden.shape[0] * depth * hidden.shape[1],
            bytes_accessed=20 * 2**20,
            transcendentals=0,
        ),
        compiler_params=params(6),
    )(hidden, w_down, state, gain_one, gain_two, grad_gate_up, grads)


def unpack_kernel(
    down, gate_up_a, gate_up_b, packed, output_in, tokens_in,
    grad_down, grad_gate, grad_up, grad_query, grad_key, grad_value, grad_out, output, grad_tokens,
):
    output[...] = output_in[...]
    grad_tokens[...] = tokens_in[...]
    grad_down[...] = down[...].astype(F32)
    units = grad_gate.shape[1]
    last = pl.num_programs(0) - 1

    @pl.when(pl.program_id(0) < last)
    def _():
        grad_gate[...] = gate_up_a[:, :units].astype(F32)
        grad_up[...] = gate_up_a[:, units:].astype(F32)

    @pl.when(pl.program_id(0) == last)
    def _():
        grad_gate[...] = gate_up_b[:, :units].astype(F32)
        grad_up[...] = gate_up_b[:, units:].astype(F32)

    first = 0
    for target in (grad_query, grad_key, grad_value):
        width = target.shape[1]
        target[...] = packed[:, first : first + width].astype(F32)
        first += width
    deep = grad_out.shape[2]
    for c in range(grad_out.shape[0]):
        grad_out[c] = packed[:, first + c * deep : first + (c + 1) * deep].astype(F32)


def unpack(down, gate_up_a, gate_up_b, packed, output, tokens, q_width, kv_raw):
    deep, units = packed.shape[0], gate_up_a.shape[1] // 2
    steps = 4
    rows = lambda array: (array[0] // steps, array[1])
    spec = lambda array: pl.BlockSpec(rows(array), lambda i: (i, 0))
    early = pl.BlockSpec((deep // steps, 2 * units), lambda i: (jnp.minimum(i, steps - 2), 0))
    late = pl.BlockSpec((deep // steps, 2 * units), lambda i: (0, 0))
    flat = (
        (down.shape, F32), ((deep, units), F32), ((deep, units), F32),
        ((deep, q_width), F32), ((deep, kv_raw), F32), ((deep, kv_raw), F32),
    )
    pieces = q_width // deep
    *grads, grad_out, output, tokens = pl.pallas_call(
        unpack_kernel,
        grid=(steps,),
        out_shape=(
            *[jax.ShapeDtypeStruct(shape, kind) for shape, kind in flat],
            jax.ShapeDtypeStruct((pieces, deep, deep), F32),
            jax.ShapeDtypeStruct(output.shape, BF16),
            jax.ShapeDtypeStruct(tokens.shape, BF16),
        ),
        in_specs=[
            spec(down.shape), early, late, spec(packed.shape), spec(output.shape),
            spec(tokens.shape),
        ],
        out_specs=(
            *[spec(shape) for shape, _ in flat],
            pl.BlockSpec((pieces, deep // steps, deep), lambda i: (0, i, 0)),
            spec(output.shape),
            spec(tokens.shape),
        ),
    )(down, gate_up_a, gate_up_b, packed, output, tokens)
    return *grads, grad_out.reshape(q_width, deep), output, tokens


def local(
    tokens, lengths, gain_one, w_query, w_key, w_value, w_out, gain_two, w_gate, w_up, w_down,
    cotangent,
):
    depth = tokens.shape[1]
    gain_one, gain_two = gain_one[None], gain_two[None]
    (
        gathered_one, query, key, value, cos_table, sin_table, attended, log_total, state, normed_two,
        cot_minor, cot_major,
    ) = front(
        lengths, tokens, gain_one, gain_two, w_query, w_key, w_value, w_out, cotangent
    )
    gathered_two, hidden, slope_gate, slope_up, cot_all, grad_down = hidden_units(
        normed_two, cotangent, cot_minor, cot_major, w_gate, w_up
    )
    grad_state, grad_mixed, gain_two_part, grad_gate_up, _, total_down = hidden_back(
        slope_gate, slope_up, cot_all, gathered_two, state, cotangent, gain_two,
        w_down, w_gate, w_up, grad_down,
    )
    grad_tokens, gain_one_part, grads, gate_up_a = attend_back(
        lengths, grad_mixed, query, key, value, attended, log_total, cos_table, sin_table,
        tokens, gain_one, grad_state, gathered_one, w_out, w_query, w_key, w_value, grad_gate_up,
    )
    output, gains, gate_up_b, packed = layer_output(
        hidden, w_down, state, gain_one_part, gain_two_part, grad_gate_up, grads
    )
    share = depth // (lax.axis_size("tensor") * lax.axis_size("dp"))
    place = lax.rem(
        (lax.axis_index("dp") * lax.axis_size("tensor") + lax.axis_index("tensor")) * share, LANES
    )
    gains = lax.dynamic_slice_in_dim(jnp.sum(gains, axis=1), place, share, axis=1)
    (
        grad_w_down, grad_w_gate, grad_w_up, grad_w_query, grad_w_key, grad_w_value, grad_w_out,
        output, grad_tokens,
    ) = unpack(
        total_down, gate_up_a, gate_up_b, packed, output, grad_tokens,
        w_query.shape[1], w_key.shape[1],
    )
    return (
        output, grad_tokens, gains[0], grad_w_query, grad_w_key, grad_w_value, grad_w_out,
        gains[1], grad_w_gate, grad_w_up, grad_w_down,
    )


def solution(mesh):
    return jax.shard_map(
        local,
        mesh=mesh,
        in_specs=(
            P(("dp", "tensor"), None),
            P("dp", None),
            P(),
            P(None, "tensor"),
            P(None, "tensor"),
            P(None, "tensor"),
            P("tensor", None),
            P(),
            P(None, "tensor"),
            P(None, "tensor"),
            P("tensor", None),
            P(("dp", "tensor"), None),
        ),
        out_specs=(
            P(("dp", "tensor"), None),
            P(("dp", "tensor"), None),
            P(("dp", "tensor")),
            P("dp", "tensor"),
            P("dp", "tensor"),
            P("dp", "tensor"),
            P("tensor", "dp"),
            P(("dp", "tensor")),
            P("dp", "tensor"),
            P("dp", "tensor"),
            P("tensor", "dp"),
        ),
        check_vma=False,
    )
```

```python
import functools
import math

import jax
import jax.numpy as jnp
import numpy as np
from jax import lax
from jax.experimental import pallas as pl
from jax.experimental.pallas import tpu as pltpu
from jax.sharding import PartitionSpec as P

HD = 64
LANES = 128
EPSILON = 1e-05
MASKED = -1e30
LOG2E = math.log2(math.e)
SCALE2 = 0.125 * LOG2E
BF16 = jnp.bfloat16
F32 = jnp.float32
MESH = pl.DeviceIdType.MESH
VMEM_LIMIT = 60 * 2**20


def dot_nn(a, b):
    return jnp.dot(a, b, preferred_element_type=F32)


def dot_nt(a, b):
    return lax.dot_general(a, b, (((1,), (1,)), ((), ())), preferred_element_type=F32)


def dot_tn(a, b):
    return lax.dot_general(a, b, (((0,), (0,)), ((), ())), preferred_element_type=F32)


def place_tables(group):
    index = np.arange(HD // 2, dtype=np.float64)
    base = np.exp(-math.log(500000.0) * 2.0 * index / HD)
    wavelength = 2.0 * math.pi / base
    smooth = (8192.0 / wavelength - 1.0) / 3.0
    blended = (1.0 - smooth) * base / 32.0 + smooth * base
    frequency = np.where(
        wavelength < 2048.0, base, np.where(wavelength > 8192.0, base / 32.0, blended)
    )
    angles = np.arange(group, dtype=np.float64)[:, None] * frequency[None, :]
    cos_half, sin_half = np.cos(angles), np.sin(angles)
    return (
        np.concatenate([cos_half] * 4, axis=1).astype(np.float32),
        np.concatenate([-sin_half, sin_half, -sin_half, sin_half], axis=1).astype(np.float32),
    )


def ends_of(lengths):
    ends, end = [], 0
    for k in range(lengths.shape[1]):
        end = end + lengths[0, k]
        ends.append(end)
    return ends


def starts_of(places, ends):
    start = jnp.zeros_like(places)
    for end in ends:
        start = jnp.where(places >= end, end, start)
    return start


def turn_tables(ends, first, count, cos_place, sin_place):
    places = lax.broadcasted_iota(jnp.int32, (count, LANES), 0) + first
    cos_start, sin_start = jnp.ones((count, LANES), F32), jnp.zeros((count, LANES), F32)
    for end in ends:
        at = pl.ds(jnp.minimum(end, cos_place.shape[0] - 1), 1)
        cos_start = jnp.where(places >= end, cos_place[at, :], cos_start)
        sin_start = jnp.where(places >= end, sin_place[at, :], sin_start)
    rows = pl.ds(first, count)
    cos, sin = cos_place[rows, :], sin_place[rows, :]
    return cos * cos_start + sin * sin_start, sin * cos_start - cos * sin_start


class Peers:
    def __init__(self):
        self.n = lax.axis_size("tensor")
        self.m = self.n // 2
        index = lax.axis_index("tensor")
        self.y = lax.div(index, np.int32(self.m))
        self.x = lax.rem(index, np.int32(self.m))

    def at(self, flip, step):
        row = 1 - self.y if flip else self.y
        return row * self.m + lax.rem(self.x + np.int32(step + self.m), np.int32(self.m))

    def minor(self, step):
        return {"tensor": self.at(0, step)}

    def major(self):
        return {"tensor": self.at(1, 0)}

    def steps(self):
        return range(1, self.m)


def core_of():
    return lax.rem(lax.axis_index("dp"), np.int32(2))


def other_core():
    return {"dp": lax.axis_index("dp") + 1 - 2 * core_of()}


def greet(peers, core=False, chips=False):
    barrier = pltpu.get_barrier_semaphore()
    for step in peers.steps():
        pl.semaphore_signal(barrier, inc=1, device_id=peers.minor(step), device_id_type=MESH)
    pl.semaphore_signal(barrier, inc=1, device_id=peers.major(), device_id_type=MESH)
    if core:
        pl.semaphore_signal(barrier, inc=1, device_id=other_core(), device_id_type=MESH)
    more = greet_chips() if chips else 0
    pl.semaphore_wait(barrier, peers.m + (1 if core else 0) + more)


class Wire:
    def __init__(self, send_sem, recv_sem):
        self.send_sem, self.recv_sem, self.copies = send_sem, recv_sem, []

    def copy(self, source, target, device):
        k = len(self.copies)
        copy = pltpu.make_async_remote_copy(
            src_ref=source,
            dst_ref=target,
            send_sem=self.send_sem.at[k],
            recv_sem=self.recv_sem.at[k],
            device_id=device,
            device_id_type=MESH,
        )
        copy.start()
        self.copies.append(copy)
        return copy

    def wait_sends(self):
        for copy in self.copies:
            copy.wait_send()


def wire_count(n):
    return 4 * (n // 2 - 1) + 2


def wires(n):
    return [pltpu.SemaphoreType.DMA((wire_count(n),))] * 2


class Local:
    def __init__(self, sem):
        self.sem, self.copies = sem, []

    def copy(self, source, target):
        copy = pltpu.make_async_copy(source, target, self.sem.at[len(self.copies)])
        copy.start()
        self.copies.append(copy)
        return copy


def block(ref, index, rows):
    return ref.at[pl.ds(pl.multiple_of(index * rows, rows), rows)]


def half_block(ref, index, rows, half):
    size = rows // 2
    return ref.at[pl.ds(pl.multiple_of(index * rows + half * size, size), size)]


def gather(peers, wire, buf, rows):
    steps, half = list(peers.steps()), rows // 2
    part = lambda index, side: half_block(buf, index, rows, side)
    span = lambda index, side: (pl.multiple_of(index * rows + side * half, half), half)
    me, major = peers.at(0, 0), peers.at(1, 0)
    send = lambda ref, device: wire.copy(ref, ref, device)
    minor_a = [send(part(me, 0), peers.minor(j)) for j in steps]
    major_b = send(part(me, 1), peers.major())
    minor_b = [send(part(me, 1), peers.minor(j)) for j in steps]
    major_a = send(part(me, 0), peers.major())
    yield [(pl.multiple_of(me * rows, rows), rows)]
    forward = []
    for j, copy in zip(steps, minor_a):
        copy.wait_recv()
        forward.append(send(part(peers.at(0, -j), 0), peers.major()))
    major_b.wait_recv()
    forward += [send(part(major, 1), peers.minor(j)) for j in steps]
    yield [span(peers.at(0, -j), 0) for j in steps] + [span(major, 1)]
    for copy in (*minor_b, major_a):
        copy.wait_recv()
    yield [span(peers.at(0, -j), 1) for j in steps] + [span(major, 0)]
    for copy in forward:
        copy.wait_recv()
    yield [(pl.multiple_of(peers.at(1, -j) * rows, rows), rows) for j in steps]


def load_rows(ref, spans):
    return jnp.concatenate([ref[pl.ds(first, count), :] for first, count in spans], axis=0)


def store_rows(ref, spans, lanes, value):
    at = 0
    for first, count in spans:
        ref[pl.ds(first, count), lanes] = value[at : at + count]
        at += count


def add_rows(target, others, size):
    step = 16
    while step * target.shape[1] < 32768 and size % (2 * step) == 0:
        step *= 2

    def some(k, carry):
        at = pl.ds(pl.multiple_of(k * step, step), step)
        total = target[at, :].astype(F32)
        for other in others:
            total = total + other[at, :].astype(F32)
        target[at, :] = total.astype(target.dtype)
        return carry

    lax.fori_loop(0, size // step, some, 0)


def scatter(peers, wire, part_ref, slots, rows, make, meanwhile=None, tick=lambda: None, early=None):
    steps = list(peers.steps())
    part = lambda index, half: half_block(part_ref, index, rows, half)
    me, major = peers.at(0, 0), peers.at(1, 0)
    count = len(steps)
    via_a, via_b, direct_b, sum_a = (
        [slots.at[group * count + k] for k in range(count)] for group in range(4)
    )
    direct_a, sum_b = slots.at[4 * count], slots.at[4 * count + 1]
    make((1 - peers.y) * peers.m, peers.m)
    first_a, first_b = [], []
    for k, j in enumerate(steps):
        index = peers.at(1, j)
        first_a.append(wire.copy(part(index, 0), via_a[k], peers.major()))
        first_b.append(wire.copy(part(index, 1), via_b[k], peers.minor(j)))
    plain_a = wire.copy(part(major, 0), direct_a, peers.major())
    make(peers.y * peers.m, peers.m)
    plain_b = [
        wire.copy(part(peers.at(0, j), 1), direct_b[k], peers.minor(j))
        for k, j in enumerate(steps)
    ]
    tick()
    if early is not None:
        early()
    done_a = []
    for k, j in enumerate(steps):
        first_a[k].wait_recv()
        target = part(peers.at(0, j), 0)
        add_rows(target, [via_a[k]], rows // 2)
        done_a.append(wire.copy(target, sum_a[k], peers.minor(j)))
    for copy in first_b:
        copy.wait_recv()
    target = part(major, 1)
    add_rows(target, via_b, rows // 2)
    done_b = wire.copy(target, sum_b, peers.major())
    tick()
    if meanwhile is not None:
        meanwhile()
    for copy in (plain_a, *plain_b):
        copy.wait_recv()
    tick()
    for copy in (*done_a, done_b):
        copy.wait_recv()
    tick()
    return (
        (part(me, 0), direct_a, *sum_a),
        (part(me, 1), sum_b, *direct_b),
    )


def slots_for(n, rows, width):
    return pltpu.VMEM((wire_count(n), rows // 2, width), BF16)


def lane_of(rows, width=LANES):
    return lax.broadcasted_iota(jnp.int32, (rows, width), 1)


def first_head(rows):
    return lane_of(rows) < HD


def swap_halves(values):
    first = lax.rem(lane_of(values.shape[0]), np.int32(HD)) < HD // 2
    return jnp.where(first, pltpu.roll(values, LANES - HD // 2, 1), pltpu.roll(values, HD // 2, 1))


def doubled(pair, heads):
    if heads == 1:
        return [jnp.concatenate([pair, pair], axis=1)]
    out = []
    for k in range(heads // 2):
        both = pair[:, k * LANES : (k + 1) * LANES]
        swapped = pltpu.roll(both, HD, 1)
        first = first_head(both.shape[0])
        out += [jnp.where(first, both, swapped), jnp.where(first, swapped, both)]
    return out


class ChipSum:
    def __init__(self, source, base, scratch, landing, total, first, span):
        self.source, self.base, self.landing, self.total = source, base, landing, total
        self.stage, self.last, *sems = scratch
        self.send_sem, self.recv_sem, self.load_sem = sems
        self.size = lax.axis_size("dp") // 2
        self.pitch = source.shape[0] // self.size
        self.dp = lax.axis_index("dp")
        place = lax.div(self.dp, np.int32(2))
        self.place, self.along = place, (place, self.size - 1 - place)
        self.chunks = self.send_sem.shape[2]
        self.deep = landing.shape[2]
        self.rows = self.deep // self.chunks
        self.pending = None
        events = []
        step = span / ((self.size - 1) * self.chunks)
        for hop in range(self.size - 1):
            for rank in range(self.size - 1 - hop):
                for c in range(self.chunks):
                    order = rank * self.chunks + c
                    due = first + step * (order + hop) + 3.0 * hop
                    if hop == 0:
                        due = first + step * self.chunks * rank - MARGIN
                    events.append((due, hop, rank, c))
        for c in range(self.chunks):
            due = first + span - step * (self.chunks - 1 - c) + 3.0
            events.append((max(due, max(events)[0]), self.size, 0, c))
        self.events = sorted(events)

    def dest(self, flow, rank):
        return self.size - 1 - rank if flow == 0 else rank

    def chunk(self, d, c):
        return self.source.at[pl.ds(pl.multiple_of(d * self.pitch + self.base + c * self.rows, 16), self.rows)]

    def landed(self, flow, rank, c):
        return self.landing.at[flow, rank, pl.ds(c * self.rows, self.rows)]

    def remote(self, flow, rank, c, source):
        return pltpu.make_async_remote_copy(
            src_ref=source,
            dst_ref=self.landed(flow, rank, c),
            send_sem=self.send_sem.at[flow, rank, c],
            recv_sem=self.recv_sem.at[flow, rank, c],
            device_id={"dp": self.dp + (2 if flow == 0 else -2)},
            device_id_type=MESH,
        )

    def loads(self, flow, slot, sources):
        return [
            pltpu.make_async_copy(ref, self.stage.at[flow, slot, k], self.load_sem.at[flow, slot, k])
            for k, ref in enumerate(sources)
        ]

    def sources(self, flow, rank, c):
        return (self.landed(flow, rank, c), self.chunk(self.dest(flow, rank), c))

    def begin(self, hop, rank, c):
        order = rank * self.chunks + c
        for flow in range(2):
            if hop == 0:

                @pl.when(self.along[flow] == 0)
                def _():
                    if order >= AHEAD:
                        before = divmod(order - AHEAD, self.chunks)
                        self.remote(flow, *before, self.chunk(self.dest(flow, before[0]), before[1])).wait_send()
                    self.remote(flow, rank, c, self.chunk(self.dest(flow, rank), c)).start()

            else:

                @pl.when(self.along[flow] == hop)
                def _():
                    slot = order % 2
                    if order >= 2:
                        before = divmod(order - 2, self.chunks)
                        self.remote(flow, *before, self.stage.at[flow, slot, 0]).wait_send()
                    self.remote(flow, rank, c, self.stage.at[flow, slot, 0]).wait_recv()
                    for load in self.loads(flow, slot, self.sources(flow, rank, c)):
                        load.start()

    def end(self, hop, rank, c):
        order = rank * self.chunks + c
        if hop == 0:
            return
        for flow in range(2):

            @pl.when(self.along[flow] == hop)
            def _():
                slot = order % 2
                for load in self.loads(flow, slot, self.sources(flow, rank, c)):
                    load.wait()
                target = self.stage.at[flow, slot, 0]
                add_rows(target, [self.stage.at[flow, slot, 1]], self.rows)
                self.remote(flow, rank, c, target).start()

    def last_loads(self, c):
        slot = c % 2
        copies = [
            pltpu.make_async_copy(
                self.landing.at[flow, self.size - 1 - self.along[flow], pl.ds(c * self.rows, self.rows)],
                self.last.at[slot, flow],
                self.load_sem.at[flow, slot, 2],
            )
            for flow in range(2)
        ]
        own = pltpu.make_async_copy(
            self.chunk(self.place, c), self.last.at[slot, 2], self.load_sem.at[slot, 0, 3]
        )
        return copies, own

    def last_begin(self, c):
        copies, own = self.last_loads(c)
        own.start()
        for flow in range(2):

            @pl.when(self.along[flow] > 0)
            def _():
                rank = self.size - 1 - self.along[flow]
                landed = self.landing.at[flow, rank, pl.ds(c * self.rows, self.rows)]
                pltpu.make_async_remote_copy(
                    src_ref=landed,
                    dst_ref=landed,
                    send_sem=self.send_sem.at[flow, rank, c],
                    recv_sem=self.recv_sem.at[flow, rank, c],
                    device_id={"dp": self.dp},
                    device_id_type=MESH,
                ).wait_recv()
                copies[flow].start()

    def last_end(self, c):
        copies, own = self.last_loads(c)
        own.wait()
        slot = c % 2
        for flow in range(2):

            @pl.when(self.along[flow] > 0)
            def _():
                copies[flow].wait()
                add_rows(self.last.at[slot, 2], [self.last.at[slot, flow]], self.rows)

        self.save(c).start()

    def save(self, c):
        return pltpu.make_async_copy(
            self.last.at[c % 2, 2],
            self.total.at[pl.ds(c * self.rows, self.rows)],
            self.load_sem.at[c % 2, 1, 3],
        )

    def advance(self, time):
        while self.events and self.events[0][0] <= time:
            _, hop, rank, c = self.events.pop(0)
            self.settle()
            if hop == self.size:
                if c >= 2:
                    self.save(c - 2).wait()
                self.last_begin(c)
            else:
                self.begin(hop, rank, c)
            self.pending = (hop, rank, c)

    def settle(self):
        if self.pending is not None:
            hop, rank, c = self.pending
            self.pending = None
            if hop == self.size:
                self.last_end(c)
            else:
                self.end(hop, rank, c)

    def finish(self):
        self.advance(1e9)
        self.settle()
        for c in range(max(self.chunks - 2, 0), self.chunks):
            self.save(c).wait()
        for flow in range(2):
            for hop in range(self.size - 1):
                depth = AHEAD if hop == 0 else 2
                count = (self.size - 1 - hop) * self.chunks

                @pl.when(self.along[flow] == hop)
                def _():
                    for order in range(max(count - depth, 0), count):
                        rank, c = divmod(order, self.chunks)
                        if hop == 0:
                            source = self.chunk(self.dest(flow, rank), c)
                        else:
                            source = self.stage.at[flow, order % 2, 0]
                        self.remote(flow, rank, c, source).wait_send()


AHEAD = 100


class Clock:
    def __init__(self, sums):
        self.sums, self.time = sums, 0.0

    def start(self):
        for one in self.sums:
            one.start()

    def to(self, time):
        self.time = time
        for one in self.sums:
            one.advance(time)

    def by(self, step):
        self.to(self.time + step)

    def at(self, *times):
        left = list(times)
        return lambda: self.to(left.pop(0))

    def finish(self):
        for one in self.sums:
            one.finish()


MARGIN = 12.0


class NearChipSum:
    def __init__(self, source, base, scratch, total, first, span):
        self.source, self.base, self.total = source, base, total
        self.blocks, self.landing, self.send_sem, self.recv_sem, load_sem, self.save_sem = scratch
        self.size = lax.axis_size("dp") // 2
        self.pitch = source.shape[0] // self.size
        self.dp = lax.axis_index("dp")
        self.place = lax.div(self.dp, np.int32(2))
        self.along = (self.place, self.size - 1 - self.place)
        self.chunks = self.send_sem.shape[2]
        self.deep = self.landing.shape[2]
        self.rows = self.deep // self.chunks
        self.loads = [
            pltpu.make_async_copy(
                source.at[pl.ds(d * self.pitch + base, self.deep)], self.blocks.at[d], load_sem.at[d]
            )
            for d in range(self.size)
        ]
        self.step = span / ((self.size - 1) * self.chunks)
        events = []
        for rank in range(self.size - 1):
            due = first + self.step * self.chunks * rank - MARGIN
            events += [(due, 0, rank, c) for c in range(self.chunks)]
        for hop in range(1, self.size - 1):
            for rank in range(self.size - 1 - hop):
                for c in range(self.chunks):
                    due = first + self.step * (rank * self.chunks + c + hop) + hop
                    events.append((due, hop, rank, c))
        latest = max(events)[0]
        for c in range(self.chunks):
            due = max(first + span - self.step * (self.chunks - 1 - c) + 1.0, latest)
            events.append((due, self.size, 0, c))
        self.events = sorted(events)

    def dest(self, flow, rank):
        return self.size - 1 - rank if flow == 0 else rank

    def landed(self, flow, rank, c):
        return self.landing.at[flow, rank, pl.ds(c * self.rows, self.rows)]

    def remote(self, flow, rank, c, source=None):
        landed = self.landed(flow, rank, c)
        return pltpu.make_async_remote_copy(
            src_ref=landed if source is None else source,
            dst_ref=landed,
            send_sem=self.send_sem.at[flow, rank, c],
            recv_sem=self.recv_sem.at[flow, rank, c],
            device_id={"dp": self.dp + (2 if flow == 0 else -2)},
            device_id_type=MESH,
        )

    def outer(self, flow, rank, c):
        first = self.dest(flow, rank) * self.pitch + self.base + c * self.rows
        return self.remote(flow, rank, c, self.source.at[pl.ds(first, self.rows)])

    def start(self):
        for load in self.loads:
            load.start()

    def send(self, rank, c):
        for flow in range(2):

            @pl.when(self.along[flow] == 0)
            def _():
                self.outer(flow, rank, c).start()

    def pass_on(self, hop, rank, c):
        for flow in range(2):

            @pl.when(self.along[flow] == hop)
            def _():
                copy = self.remote(flow, rank, c)
                copy.wait_recv()
                own = self.blocks.at[self.dest(flow, rank), pl.ds(c * self.rows, self.rows)]
                add_rows(self.landed(flow, rank, c), [own], self.rows)
                copy.start()

    def own(self, c):
        return self.blocks.at[self.place, pl.ds(c * self.rows, self.rows)]

    def save(self, c):
        target = self.total.at[pl.ds(c * self.rows, self.rows)]
        return pltpu.make_async_copy(self.own(c), target, self.save_sem.at[c])

    def take(self, c):
        for flow in range(2):

            @pl.when(self.along[flow] > 0)
            def _():
                rank = self.size - 1 - self.along[flow]
                self.remote(flow, rank, c).wait_recv()
                add_rows(self.own(c), [self.landed(flow, rank, c)], self.rows)

        self.save(c).start()

    def advance(self, time):
        while self.events and self.events[0][0] <= time:
            _, hop, rank, c = self.events.pop(0)
            if hop == 0:
                self.send(rank, c)
                continue
            while self.loads:
                self.loads.pop().wait()
            if hop == self.size:
                self.take(c)
            else:
                self.pass_on(hop, rank, c)

    def finish(self):
        self.advance(1e9)
        for c in range(self.chunks):
            self.save(c).wait()
        for flow in range(2):
            for hop in range(self.size - 1):

                @pl.when(self.along[flow] == hop)
                def _():
                    for rank in range(self.size - 1 - hop):
                        for c in range(self.chunks):
                            copy = self.outer if hop == 0 else self.remote
                            copy(flow, rank, c).wait_send()


def near_chip_sum_scratch(size, deep, width):
    chunks = chip_chunks(size)
    dma = lambda *shape: pltpu.SemaphoreType.DMA(shape)
    return [
        pltpu.VMEM((size, deep, width), BF16),
        pltpu.VMEM((2, size - 1, deep, width), BF16),
        dma(2, size - 1, chunks),
        dma(2, size - 1, chunks),
        dma(size),
        dma(chunks),
    ]


def greet_chips():
    barrier = pltpu.get_barrier_semaphore()
    dp, dps = lax.axis_index("dp"), lax.axis_size("dp")
    for step in (2, dps - 2):
        device = {"dp": lax.rem(dp + np.int32(step), np.int32(dps))}
        pl.semaphore_signal(barrier, inc=1, device_id=device, device_id_type=MESH)
    return 2


def chip_chunks(size):
    return 4 if size == 4 else 1


def chip_sum_shapes(size, deep, width):
    chunks = chip_chunks(size)
    rows = deep // chunks
    dma = lambda *shape: pltpu.SemaphoreType.DMA(shape)
    return (
        jax.ShapeDtypeStruct((2, size - 1, deep, width), BF16),
        [
            pltpu.VMEM((2, 2, 2, rows, width), BF16),
            pltpu.VMEM((2, 3, rows, width), BF16),
            dma(2, size - 1, chunks),
            dma(2, size - 1, chunks),
            dma(2, 2, 4),
        ],
    )


def front_kernel(
    lengths, tokens, gain, gain_two, cos_place, sin_place, w_query, w_key, w_value, w_out, cotangent,
    gathered_out, query_out, key_out, value_out, cos_out, sin_out,
    attended_out, log_out, state_out, normed_out, cot_minor, cot_major,
    gathered, weights, raw_key, raw_value, query, key, value, w_buf, attended, log_total, part, slots,
    send_sem, recv_sem, sums_send, sums_recv, cot_send, cot_recv, local_sem,
):
    peers = Peers()
    rows, depth = tokens.shape
    group = gathered.shape[0]
    q_width, kv_heads = w_query.shape[1], w_key.shape[1] // HD
    kv_width = kv_heads * LANES
    local = Local(local_sem)
    load_out = local.copy(w_out, w_buf)
    loads = [
        local.copy(w_key, raw_key),
        local.copy(w_value, raw_value),
        local.copy(w_query, weights.at[:, pl.ds(0, q_width)]),
    ]
    me = peers.at(0, 0)
    gain_row = gain[...]

    def normalize(k, carry):
        values = tokens[pl.ds(pl.multiple_of(k * 16, 16), 16), :].astype(F32)
        scale = lax.rsqrt(jnp.mean(values * values, axis=-1, keepdims=True) + EPSILON)
        gathered[pl.ds(pl.multiple_of(me * rows + k * 16, 16), 16), :] = (
            values * scale * gain_row
        ).astype(BF16)
        return carry

    lax.fori_loop(0, rows // 16, normalize, 0)
    greet(peers)

    def prepare():
        ends = ends_of(lengths)

        def turn(k, carry):
            first = pl.multiple_of(k * 128, 128)
            cos, sin = turn_tables(ends, first, 128, cos_place, sin_place)
            cos_out[pl.ds(first, 128), :] = cos
            sin_out[pl.ds(first, 128), :] = sin
            return carry

        lax.fori_loop(0, group // 128, turn, 0)
        for load in loads:
            load.wait()

        def some(k, carry):
            at = pl.ds(pl.multiple_of(k * 128, 128), 128)
            for raw, base in ((raw_key, q_width), (raw_value, q_width + kv_width)):
                for j, twice in enumerate(doubled(raw[at, :].astype(F32), kv_heads)):
                    weights[at, base + j * LANES : base + (j + 1) * LANES] = twice.astype(BF16)
            return carry

        lax.fori_loop(0, depth // 128, some, 0)

    cot_wire = Wire(cot_send, cot_recv)

    def send_cotangent():
        part = lambda half: half_block(cotangent, 0, rows, half)
        landed = lambda ref, half: half_block(ref, 0, rows, half)
        for k, j in enumerate(peers.steps()):
            cot_wire.copy(part(0), landed(cot_minor.at[k], 0), peers.minor(j))
        cot_wire.copy(part(1), landed(cot_major, 1), peers.major())
        for k, j in enumerate(peers.steps()):
            cot_wire.copy(part(1), landed(cot_minor.at[k], 1), peers.minor(j))
        cot_wire.copy(part(0), landed(cot_major, 0), peers.major())

    gather_wire = Wire(send_sem, recv_sem)
    for step, spans in enumerate(gather(peers, gather_wire, gathered, rows)):
        if step == 0:
            prepare()
        if step == 3:
            saves = [local.copy(gathered, gathered_out)]
            send_cotangent()
        cos, sin = load_rows(cos_out, spans), load_rows(sin_out, spans)
        normed = load_rows(gathered, spans)
        for base, width, out, turned in (
            (0, q_width, query, True),
            (q_width, kv_width, key, True),
            (q_width + kv_width, kv_width, value, False),
        ):
            raw = dot_nn(normed, weights[:, base : base + width])
            for c in range(0, width, LANES):
                piece = raw[:, c : c + LANES]
                if turned:
                    piece = piece * cos + swap_halves(piece) * sin
                store_rows(out, spans, slice(c, c + LANES), piece.astype(BF16))
    saves += [local.copy(query, query_out), local.copy(key, key_out), local.copy(value, value_out)]
    ends = ends_of(lengths)
    pairs_per_kv = q_width // LANES // kv_heads
    log_total[...] = jnp.zeros_like(log_total)
    tile = 256
    for i in range(group // tile):
        keys = (i + 1) * tile

        def one_pair(pair, carry, i=i, keys=keys):
            at = pl.ds(i * tile, tile)
            lanes = pl.ds(pl.multiple_of(pair * LANES, LANES), LANES)
            kv_lanes = pl.ds(
                pl.multiple_of(lax.div(pair, np.int32(pairs_per_kv)) * LANES, LANES), LANES
            )
            both = query[at, lanes]
            key_rows, value_rows = key[0:keys, kv_lanes], value[0:keys, kv_lanes]
            first = first_head(tile)
            column = lax.broadcasted_iota(jnp.int32, (tile, keys), 1)
            row = lax.broadcasted_iota(jnp.int32, (tile, keys), 0) + i * tile
            start = starts_of(lax.broadcasted_iota(jnp.int32, (tile, 1), 0) + i * tile, ends)
            allowed = (column >= start) & (column <= row)
            logs = log_total[at, :]
            outs = []
            for h in range(2):
                own = first if h == 0 else jnp.logical_not(first)
                scores = dot_nt(jnp.where(own, both, jnp.zeros_like(both)), key_rows)
                scores = jnp.where(allowed, scores, MASKED)
                row_max = jnp.max(scores, axis=-1, keepdims=True)
                weights = jnp.exp2((scores - row_max) * SCALE2)
                row_sum = jnp.sum(weights, axis=-1, keepdims=True)
                outs.append(dot_nn(weights.astype(BF16), value_rows) / row_sum)
                logs = jnp.where(
                    lane_of(tile) == pair * 2 + h, row_max * SCALE2 + jnp.log2(row_sum), logs
                )
            log_total[at, :] = logs
            attended[at, lanes] = jnp.where(first, outs[0], outs[1]).astype(BF16)
            return carry

        lax.fori_loop(0, q_width // LANES, one_pair, 0)

    saves += [local.copy(attended, attended_out), local.copy(log_total, log_out)]
    load_out.wait()

    def make(first, count):
        at = pl.ds(pl.multiple_of(first * rows, rows), count * rows)
        heads = attended[at, :]
        for c in range(0, depth, 1024):
            part[at, c : c + 1024] = dot_nn(heads, w_buf[:, c : c + 1024]).astype(BF16)

    wire = Wire(sums_send, sums_recv)
    sums = scatter(peers, wire, part, slots, rows, make)
    gain_row = gain_two[...]
    half = rows // 2
    for h in range(2):

        def finish(k, carry, h=h):
            inner = pl.ds(pl.multiple_of(k * 16, 16), 16)
            outer = pl.ds(pl.multiple_of(h * half + k * 16, 16), 16)
            mixed = sums[h][0][inner, :].astype(F32)
            for other in sums[h][1:]:
                mixed = mixed + other[inner, :].astype(F32)
            state = tokens[outer, :].astype(F32) + mixed
            scale = lax.rsqrt(jnp.mean(state * state, axis=-1, keepdims=True) + EPSILON)
            state_out[outer, :] = state
            normed_out[outer, :] = (state * scale * gain_row).astype(BF16)
            return carry

        lax.fori_loop(0, half // 16, finish, 0)
    gather_wire.wait_sends()
    wire.wait_sends()
    for copy in (*cot_wire.copies, *saves):
        copy.wait()


def any_spec():
    return pl.BlockSpec(memory_space=pl.ANY)


def vmem_spec():
    return pl.BlockSpec(memory_space=pltpu.VMEM)


def params(collective_id):
    return pltpu.CompilerParams(
        collective_id=collective_id, has_side_effects=True, vmem_limit_bytes=VMEM_LIMIT
    )


def smem_spec():
    return pl.BlockSpec(memory_space=pltpu.SMEM)


def front(lengths, tokens, gain, gain_two, w_query, w_key, w_value, w_out, cotangent):
    n = lax.axis_size("tensor")
    m = n // 2
    rows, depth = tokens.shape
    group = rows * n
    q_width, kv_raw = w_query.shape[1], w_key.shape[1]
    kv_width = kv_raw // HD * LANES
    heads = [(group, q_width), (group, kv_width), (group, kv_width)]
    low = lambda *shape: jax.ShapeDtypeStruct(shape, BF16)
    return pl.pallas_call(
        front_kernel,
        out_shape=(
            low(group, depth),
            *[low(*shape) for shape in heads],
            jax.ShapeDtypeStruct((group, LANES), F32),
            jax.ShapeDtypeStruct((group, LANES), F32),
            low(group, q_width),
            jax.ShapeDtypeStruct((group, LANES), F32),
            jax.ShapeDtypeStruct((rows, depth), F32),
            low(rows, depth),
            low(m - 1, rows, depth),
            low(rows, depth),
        ),
        in_specs=[smem_spec()] + [vmem_spec()] * 5 + [any_spec()] * 5,
        out_specs=(
            *[any_spec()] * 4, vmem_spec(), vmem_spec(), any_spec(), any_spec(),
            vmem_spec(), vmem_spec(), any_spec(), any_spec(),
        ),
        scratch_shapes=[
            pltpu.VMEM((group, depth), BF16),
            pltpu.VMEM((depth, q_width + 2 * kv_width), BF16),
            pltpu.VMEM((depth, kv_raw), BF16),
            pltpu.VMEM((depth, kv_raw), BF16),
            *[pltpu.VMEM(shape, BF16) for shape in heads],
            pltpu.VMEM(w_out.shape, BF16),
            pltpu.VMEM((group, q_width), BF16),
            pltpu.VMEM((group, LANES), F32),
            pltpu.VMEM((group, depth), BF16),
            slots_for(n, rows, depth),
            *wires(n),
            *wires(n),
            pltpu.SemaphoreType.DMA((2 * m,)),
            pltpu.SemaphoreType.DMA((2 * m,)),
            pltpu.SemaphoreType.DMA((10,)),
        ],
        cost_estimate=pl.CostEstimate(
            flops=2 * group * depth * (2 * q_width + 2 * kv_width),
            bytes_accessed=60 * 2**20,
            transcendentals=0,
        ),
        compiler_params=params(1),
    )(
        lengths, tokens, gain, gain_two, *place_tables(group), w_query, w_key, w_value, w_out,
        cotangent,
    )


class Exchange:
    def __init__(self, wire, stage, received):
        self.wire, self.stage, self.received, self.sent = wire, stage, received, []

    def run(self, jobs, tick=lambda: None):
        mine = core_of()
        copies = []
        for k in range(len(jobs) + 1):
            if k < len(jobs):
                tile, save, pair = jobs[k]
                slot = self.stage.at[k % 2]
                if k >= 2:
                    copies[k - 2].wait_send()
                tile(2 * pair + 1 - mine, slot, False)
                copies.append(self.wire.copy(slot, self.received.at[k], other_core()))
                tick()
            if k >= 1:
                tile, save, pair = jobs[k - 1]
                copies[k - 1].wait_recv()
                tile(2 * pair + mine, self.received.at[k - 1], True)
                save(pair, self.received.at[k - 1])
                tick()
        for copy in copies[-2:]:
            copy.wait_send()


def put(target, at, value, add):
    if add:
        value = value + target[at].astype(F32)
    target[at] = value.astype(BF16)


def hidden_kernel(
    normed, cotangent, cot_minor, cot_major, w_gate, w_up,
    gathered_out, hidden_out, slope_gate_out, slope_up_out, cot_out, grad_down_out,
    gathered, gate_buf, up_buf, hidden, slope_gate, slope_up, cot, stage, received,
    send_sem, recv_sem, cot_send, cot_recv, core_send, core_recv, local_sem,
):
    peers = Peers()
    rows, depth = normed.shape
    units = w_gate.shape[1]
    me, major = peers.at(0, 0), peers.at(1, 0)
    local = Local(local_sem)
    first_load = local.copy(normed, block(gathered, me, rows))
    loads = [local.copy(w_gate, gate_buf), local.copy(w_up, up_buf)]
    cot_loads = [local.copy(cotangent, block(cot, me, rows))]
    for k, j in enumerate(peers.steps()):
        cot_loads.append(local.copy(cot_minor.at[k], block(cot, peers.at(0, -j), rows)))
    cot_loads.append(local.copy(cot_major, block(cot, major, rows)))
    greet(peers, core=True)
    first_load.wait()

    def use(spans):
        tile = 512

        def some(k, carry):
            lanes = pl.ds(pl.multiple_of(k * tile, tile), tile)
            x = load_rows(gathered, spans)
            gate = dot_nn(x, gate_buf[:, lanes])
            up = dot_nn(x, up_buf[:, lanes])
            sigmoid = jax.nn.sigmoid(gate)
            silu = gate * sigmoid
            slope = up * sigmoid * (1.0 + gate * (1.0 - sigmoid))
            store_rows(hidden, spans, lanes, (silu * up).astype(BF16))
            store_rows(slope_up, spans, lanes, silu.astype(BF16))
            store_rows(slope_gate, spans, lanes, slope.astype(BF16))
            return carry

        lax.fori_loop(0, units // tile, some, 0)

    cot_wire = Wire(cot_send, cot_recv)
    rest = ([], [])
    width = depth // 2

    def send_rest():
        for load in cot_loads:
            load.wait()
        for side in range(2):
            lanes = pl.ds(side * width, width)

            def send(index, half, device):
                ref = half_block(cot, index, rows, half).at[:, lanes]
                rest[side].append(cot_wire.copy(ref, ref, device))

            for j in peers.steps():
                send(major, 1, peers.minor(j))
            for j in peers.steps():
                send(peers.at(0, -j), 0, peers.major())

    wire = Wire(send_sem, recv_sem)
    for step, spans in enumerate(gather(peers, wire, gathered, rows)):
        if step == 0:
            for load in loads:
                load.wait()
        if step == 3:
            send_rest()
        use(spans)
    saves = [
        local.copy(gathered, gathered_out),
        local.copy(hidden, hidden_out),
        local.copy(slope_gate, slope_gate_out),
        local.copy(slope_up, slope_up_out),
    ]
    columns = stage.shape[2]
    pairs = received.shape[0]
    arrived = set()

    def tile_of(side):
        def tile(index, target, add):
            if side not in arrived:
                arrived.add(side)
                for copy in rest[side]:
                    copy.wait_recv()
            lanes = pl.ds(pl.multiple_of(index * columns, columns), columns)
            step = 512

            def some(k, carry):
                at = pl.ds(pl.multiple_of(k * step, step), step)
                put(target, (at, slice(None)), dot_tn(hidden[:, at], cot[:, lanes]), add)
                return carry

            lax.fori_loop(0, units // step, some, 0)

        return tile

    def save(k, ref):
        saves.append(local.copy(ref, grad_down_out.at[pl.ds(k * units, units)]))

    Exchange(Wire(core_send, core_recv), stage, received).run(
        [(tile_of(2 * k // pairs), save, k) for k in range(pairs)]
    )
    saves.append(local.copy(cot, cot_out))
    wire.wait_sends()
    cot_wire.wait_sends()
    for copy in saves:
        copy.wait()


def hidden_units(normed, cotangent, cot_minor, cot_major, w_gate, w_up):
    n = lax.axis_size("tensor")
    pairs = lax.axis_size("dp") // 2
    rows, depth = normed.shape
    group, units, columns = rows * n, w_gate.shape[1], depth // (2 * pairs)
    wide = lambda width: jax.ShapeDtypeStruct((group, width), BF16)
    return pl.pallas_call(
        hidden_kernel,
        out_shape=(
            wide(depth), wide(units), wide(units), wide(units), wide(depth),
            jax.ShapeDtypeStruct((pairs * units, columns), BF16),
        ),
        in_specs=[any_spec()] * 6,
        out_specs=(any_spec(),) * 6,
        scratch_shapes=[
            pltpu.VMEM((group, depth), BF16),
            pltpu.VMEM((depth, units), BF16),
            pltpu.VMEM((depth, units), BF16),
            pltpu.VMEM((group, units), BF16),
            pltpu.VMEM((group, units), BF16),
            pltpu.VMEM((group, units), BF16),
            pltpu.VMEM((group, depth), BF16),
            pltpu.VMEM((2, units, columns), BF16),
            pltpu.VMEM((pairs, units, columns), BF16),
            *wires(n),
            pltpu.SemaphoreType.DMA((2 * wire_count(n),)),
            pltpu.SemaphoreType.DMA((2 * wire_count(n),)),
            pltpu.SemaphoreType.DMA((pairs,)),
            pltpu.SemaphoreType.DMA((pairs,)),
            pltpu.SemaphoreType.DMA((3 + n // 2 + 1 + 5 + pairs,)),
        ],
        cost_estimate=pl.CostEstimate(
            flops=6 * group * depth * units, bytes_accessed=60 * 2**20, transcendentals=0
        ),
        compiler_params=params(3),
    )(normed, cotangent, cot_minor, cot_major, w_gate, w_up)


def norm_back(values, gain_row, grad_normed):
    scale = lax.rsqrt(jnp.mean(values * values, axis=-1, keepdims=True) + EPSILON)
    unit = values * scale
    scaled = grad_normed * gain_row
    grad = scale * (scaled - unit * jnp.mean(scaled * unit, axis=-1, keepdims=True))
    return grad, grad_normed * unit


def fold_rows(values):
    return values[:8] + values[8:]


def hidden_back_kernel(
    slope_gate, slope_up, cot_all, gathered_in, state, cotangent, gain, w_down, w_gate, w_up, grad_down,
    grad_state_out, grad_mixed_out, gain_out, grad_gate_up_out, landing, total_down,
    gate_buf, up_buf, down_buf, grad_gate, grad_up, cot, part, slots, stage, received,
    send_sem, recv_sem, core_send, core_recv, local_sem, *chip_scratch,
):
    peers = Peers()
    rows, depth = state.shape
    group, units = slope_gate.shape
    chunk = down_buf.shape[1]
    chunks = units // chunk
    local = Local(local_sem)

    def load_rows_of(flip):
        row = 1 - peers.y if flip else peers.y
        at = pl.ds(pl.multiple_of(row * (peers.m * rows), peers.m * rows), peers.m * rows)
        pairs = ((cot_all, cot), (slope_gate, grad_gate), (slope_up, grad_up))
        return [local.copy(source.at[at], target.at[at]) for source, target in pairs]

    def load_down(k):
        source = w_down.at[pl.ds(k % chunks * chunk, chunk)]
        return local.copy(source, down_buf.at[k % 2])

    downs = [load_down(0)]
    inputs = load_rows_of(True)
    downs.append(load_down(1))
    greet(peers, core=True, chips=True)
    clock = Clock([ChipSum(grad_down, 0, chip_scratch, landing, total_down, 4.0, 72.0)])
    clock.to(1.0)
    later = []

    def make(first, count):
        at = pl.ds(pl.multiple_of(first * rows, rows), count * rows)
        base = chunks if later else 0
        for c in range(chunks):
            downs[base + c].wait()
            while inputs:
                inputs.pop().wait()
            if not later:
                later.extend(
                    [
                        local.copy(w_gate, gate_buf),
                        local.copy(w_up, up_buf),
                        local.copy(state, grad_state_out),
                    ]
                )
            lanes = slice(c * chunk, (c + 1) * chunk)
            grad_hidden = dot_nt(cot[at, :], down_buf[c % 2])
            grad_gate[at, lanes] = (grad_hidden * grad_gate[at, lanes].astype(F32)).astype(BF16)
            grad_up[at, lanes] = (grad_hidden * grad_up[at, lanes].astype(F32)).astype(BF16)
            if base + c + 2 < 2 * chunks:
                downs.append(load_down(base + c + 2))
            clock.by(5.0 if base + c == 0 else 1.5)
        if base == 0:
            for load in later[:2]:
                load.wait()
            inputs.extend(load_rows_of(False))
        else:
            later.append(local.copy(gathered_in, cot))
        step = 512

        for k in range(depth // step):
            inner = slice(k * step, (k + 1) * step)
            total = dot_nt(grad_gate[at, :], gate_buf[inner, :])
            total = total + dot_nt(grad_up[at, :], up_buf[inner, :])
            part[at, inner] = total.astype(BF16)
            clock.by(2.7)

    deep = stage.shape[1]
    saves = []

    def tile_of(grad):
        def tile(index, target, add):
            lanes = pl.ds(pl.multiple_of(index * deep, deep), deep)
            step = min(1024, units)

            def some(k, carry):
                inner = pl.ds(pl.multiple_of(k * step, step), step)
                put(target, (slice(None), inner), dot_tn(cot[:, lanes], grad[:, inner]), add)
                return carry

            lax.fori_loop(0, units // step, some, 0)

        return tile

    def save_at(base):
        def save(k, ref):
            target = grad_gate_up_out.at[pl.ds(k * deep, deep), pl.ds(base, units)]
            saves.append(local.copy(ref, target))

        return save

    def weight_grads():
        later[3].wait()
        pairs = received.shape[0] // 2
        Exchange(Wire(core_send, core_recv), stage, received).run(
            [(tile_of(grad_gate), save_at(0), k) for k in range(pairs)]
            + [(tile_of(grad_up), save_at(units), k) for k in range(pairs)],
            lambda: clock.by(1.6),
        )

    wire = Wire(send_sem, recv_sem)
    sums = scatter(peers, wire, part, slots, rows, make, weight_grads, lambda: clock.by(0.5))
    later[2].wait()
    gain_row = gain[...]
    half = rows // 2
    gain_out[...] = jnp.zeros_like(gain_out)
    for h in range(2):

        def finish(k, carry, h=h):
            inner = pl.ds(pl.multiple_of(k * 16, 16), 16)
            outer = pl.ds(pl.multiple_of(h * half + k * 16, 16), 16)
            grad_normed = sums[h][0][inner, :].astype(F32)
            for other in sums[h][1:]:
                grad_normed = grad_normed + other[inner, :].astype(F32)
            grad, gain_part = norm_back(grad_state_out[outer, :], gain_row, grad_normed)
            grad = grad + cotangent[outer, :].astype(F32)
            gain_out[...] += fold_rows(gain_part)
            grad_state_out[outer, :] = grad
            grad_mixed_out[outer, :] = grad.astype(BF16)
            return carry

        lax.fori_loop(0, half // 16, finish, 0)
    clock.finish()
    wire.wait_sends()
    for copy in saves:
        copy.wait()


def hidden_back(
    slope_gate, slope_up, cot_all, gathered, state, cotangent, gain, w_down, w_gate, w_up, grad_down
):
    n = lax.axis_size("tensor")
    pairs = lax.axis_size("dp") // 2
    rows, depth = state.shape
    group, units = slope_gate.shape
    deep = depth // (2 * pairs)
    chunk = 512
    landing, chip_scratch = chip_sum_shapes(pairs, units, grad_down.shape[1])
    return pl.pallas_call(
        hidden_back_kernel,
        out_shape=(
            jax.ShapeDtypeStruct((rows, depth), F32),
            jax.ShapeDtypeStruct((rows, depth), BF16),
            jax.ShapeDtypeStruct((8, depth), F32),
            jax.ShapeDtypeStruct((pairs * deep, 2 * units), BF16),
            landing,
            jax.ShapeDtypeStruct((units, grad_down.shape[1]), BF16),
        ),
        in_specs=[any_spec()] * 5 + [vmem_spec()] * 2 + [any_spec()] * 4,
        out_specs=(vmem_spec(), vmem_spec(), vmem_spec(), any_spec(), any_spec(), any_spec()),
        scratch_shapes=[
            pltpu.VMEM((depth, units), BF16),
            pltpu.VMEM((depth, units), BF16),
            pltpu.VMEM((2, chunk, depth), BF16),
            pltpu.VMEM((group, units), BF16),
            pltpu.VMEM((group, units), BF16),
            pltpu.VMEM((group, depth), BF16),
            pltpu.VMEM((group, depth), BF16),
            slots_for(n, rows, depth),
            pltpu.VMEM((2, deep, units), BF16),
            pltpu.VMEM((2 * pairs, deep, units), BF16),
            *wires(n),
            pltpu.SemaphoreType.DMA((2 * pairs,)),
            pltpu.SemaphoreType.DMA((2 * pairs,)),
            pltpu.SemaphoreType.DMA((10 + 2 * (units // chunk) + 2 * pairs,)),
            *chip_scratch,
        ],
        cost_estimate=pl.CostEstimate(
            flops=10 * group * depth * units, bytes_accessed=80 * 2**20, transcendentals=0
        ),
        compiler_params=params(4),
    )(
        slope_gate, slope_up, cot_all, gathered, state, cotangent, gain, w_down, w_gate, w_up,
        grad_down,
    )


def attend_back_kernel(
    lengths, gain, grad_mixed, query_in, key_in, value_in, attended_in, log_in, cos_in, sin_in,
    tokens_in, state_in, gathered_in, w_out, w_query, w_key, w_value, grad_gate_up,
    grad_tokens_out, gain_out, grads_out, total_gate_up,
    query, key, value, attended, log_total, cos_table, sin_table, tokens, grad_state,
    mixed, out_buf, query_buf, key_buf, value_buf, gathered, grad_att, key_acc, value_acc, grads, part, slots,
    stage_out, got_out, stage_qkv, got_qkv,
    send_sem, recv_sem, sums_send, sums_recv, out_send, out_recv, qkv_send, qkv_recv, local_sem, *chip_scratch,
):
    peers = Peers()
    rows, depth = tokens.shape
    group, q_width = query.shape
    kv_heads = w_key.shape[1] // HD
    kv_raw = kv_heads * HD
    pairs_per_kv = q_width // LANES // kv_heads
    me = peers.at(0, 0)
    local = Local(local_sem)
    first_load = local.copy(grad_mixed, block(mixed, me, rows))
    load_out = local.copy(w_out, out_buf)
    sources = (
        query_in, key_in, value_in, attended_in, log_in, cos_in, sin_in, tokens_in, state_in
    )
    buffers = (query, key, value, attended, log_total, cos_table, sin_table, tokens, grad_state)
    loads = [local.copy(source, buffer) for source, buffer in zip(sources, buffers)]
    loads += [
        local.copy(w_query, query_buf),
        local.copy(w_key, key_buf),
        local.copy(w_value, value_buf),
        local.copy(gathered_in, gathered),
    ]
    greet(peers, core=True, chips=True)
    clock = Clock([NearChipSum(grad_gate_up, 0, chip_scratch, total_gate_up, 0.0, 108.0)])
    clock.start()
    clock.to(0.5)
    first_load.wait()
    ends, saves = ends_of(lengths), []
    gather_wire = Wire(send_sem, recv_sem)
    for step, spans in enumerate(gather(peers, gather_wire, mixed, rows)):
        if step == 0:
            load_out.wait()
        grad_rows = dot_nt(load_rows(mixed, spans), out_buf[...]).astype(BF16)
        store_rows(grad_att, spans, slice(None), grad_rows)
        clock.to(1.0 + 12.0 * step)

    for load in loads:
        load.wait()
    columns = stage_out.shape[2]

    def out_tile(index, target, add):
        lanes = pl.ds(pl.multiple_of(index * columns, columns), columns)
        put(target, (slice(None), slice(None)), dot_tn(attended[...], mixed[:, lanes]), add)

    pairs = got_out.shape[0]
    width = grads.shape[1]

    def out_save(k, ref):
        for c in range(q_width // columns):
            target = grads_out.at[
                pl.ds(k * columns, columns), pl.ds(width + c * columns, columns)
            ]
            saves.append(local.copy(ref.at[pl.ds(c * columns, columns)], target))

    key_acc[...] = jnp.zeros_like(key_acc)
    value_acc[...] = jnp.zeros_like(value_acc)
    tile = 256
    for i in range(group // tile):
        keys = (i + 1) * tile

        def one_pair(pair, carry, i=i, keys=keys):
            at = pl.ds(i * tile, tile)
            lanes = pl.ds(pl.multiple_of(pair * LANES, LANES), LANES)
            kv_lanes = pl.ds(
                pl.multiple_of(lax.div(pair, np.int32(pairs_per_kv)) * LANES, LANES), LANES
            )
            both, grad_both = query[at, lanes], grad_att[at, lanes]
            key_rows, value_rows = key[0:keys, kv_lanes], value[0:keys, kv_lanes]
            first = first_head(tile)
            dots = grad_both.astype(F32) * attended[at, lanes].astype(F32)
            column = lax.broadcasted_iota(jnp.int32, (tile, keys), 1)
            row = lax.broadcasted_iota(jnp.int32, (tile, keys), 0) + i * tile
            start = starts_of(lax.broadcasted_iota(jnp.int32, (tile, 1), 0) + i * tile, ends)
            allowed = (column >= start) & (column <= row)
            logs = log_total[at, :]
            grad_queries, grad_keys, grad_values = [], 0.0, 0.0
            for h in range(2):
                own = first if h == 0 else jnp.logical_not(first)
                own_query = jnp.where(own, both, jnp.zeros_like(both))
                own_grad = jnp.where(own, grad_both, jnp.zeros_like(grad_both))
                row_dot = jnp.sum(jnp.where(own, dots, 0.0), axis=-1, keepdims=True)
                scores = dot_nt(own_query, key_rows)
                log_row = jnp.sum(
                    jnp.where(lane_of(tile) == pair * 2 + h, logs, 0.0), axis=-1, keepdims=True
                )
                probs = jnp.exp2(scores * SCALE2 - log_row)
                probs = jnp.where(allowed, probs, 0.0)
                grad_probs = dot_nt(own_grad, value_rows)
                grad_scores = (probs * (grad_probs - row_dot)).astype(BF16)
                grad_queries.append(dot_nn(grad_scores, key_rows))
                grad_keys = grad_keys + dot_tn(grad_scores, own_query)
                grad_values = grad_values + dot_tn(probs.astype(BF16), own_grad)
            key_acc[0:keys, kv_lanes] += grad_keys
            value_acc[0:keys, kv_lanes] += grad_values
            turned = jnp.where(first, grad_queries[0], grad_queries[1]) * 0.125
            turned = turned * cos_table[at, :] - swap_halves(turned) * sin_table[at, :]
            grads[at, lanes] = turned.astype(BF16)
            return carry

        lax.fori_loop(0, q_width // LANES, one_pair, 0)
        clock.by(2.1 * (i + 1))

    def fold(k, carry):
        at = pl.ds(pl.multiple_of(k * 128, 128), 128)
        cos, sin = cos_table[at, :], sin_table[at, :]
        key_heads, value_heads = [], []
        for j in range(kv_heads):
            lanes = slice(j * LANES, (j + 1) * LANES)
            both = key_acc[at, lanes] * 0.125
            both = both + pltpu.roll(both, HD, 1)
            key_heads.append(both * cos - swap_halves(both) * sin)
            both = value_acc[at, lanes]
            value_heads.append(both + pltpu.roll(both, HD, 1))
        for heads, base in ((key_heads, q_width), (value_heads, q_width + kv_raw)):
            if kv_heads == 1:
                grads[at, base : base + HD] = heads[0][:, :HD].astype(BF16)
            for j in range(0, kv_heads - 1, 2):
                pair = jnp.where(first_head(128), heads[j], heads[j + 1])
                grads[at, base + j * HD : base + (j + 2) * HD] = pair.astype(BF16)
        return carry

    lax.fori_loop(0, group // 128, fold, 0)

    def make(first, count):
        at = pl.ds(pl.multiple_of(first * rows, rows), count * rows)
        step = 1024
        for c in range(0, depth, step):
            inner = slice(c, c + step)
            total = dot_nt(grads[at, 0:q_width], query_buf[inner, :])
            total = total + dot_nt(grads[at, q_width : q_width + kv_raw], key_buf[inner, :])
            total = total + dot_nt(grads[at, q_width + kv_raw :], value_buf[inner, :])
            part[at, inner] = total.astype(BF16)
            clock.by(1.2)

    deep = stage_qkv.shape[1]

    def qkv_tile(index, target, add):
        lanes = pl.ds(pl.multiple_of(index * deep, deep), deep)
        put(target, (slice(None), slice(None)), dot_tn(gathered[:, lanes], grads[...]), add)

    def qkv_save(k, ref):
        target = grads_out.at[pl.ds(k * deep, deep), pl.ds(0, width)]
        saves.append(local.copy(ref, target))

    def weight_grads():
        Exchange(Wire(out_send, out_recv), stage_out, got_out).run(
            [(out_tile, out_save, k) for k in range(pairs)], lambda: clock.by(0.5)
        )
        Exchange(Wire(qkv_send, qkv_recv), stage_qkv, got_qkv).run(
            [(qkv_tile, qkv_save, k) for k in range(pairs)], lambda: clock.by(0.9)
        )

    wire = Wire(sums_send, sums_recv)
    sums = scatter(
        peers, wire, part, slots, rows, make, tick=clock.at(66.0, 80.0, 90.0, 101.0), early=weight_grads
    )
    gain_row = gain[...]
    half = rows // 2
    gain_out[...] = jnp.zeros_like(gain_out)
    for h in range(2):

        def finish(k, carry, h=h):
            inner = pl.ds(pl.multiple_of(k * 16, 16), 16)
            outer = pl.ds(pl.multiple_of(h * half + k * 16, 16), 16)
            grad_normed = sums[h][0][inner, :].astype(F32)
            for other in sums[h][1:]:
                grad_normed = grad_normed + other[inner, :].astype(F32)
            grad, gain_part = norm_back(tokens[outer, :].astype(F32), gain_row, grad_normed)
            gain_out[...] += fold_rows(gain_part)
            grad_tokens_out[outer, :] = (grad + grad_state[outer, :]).astype(BF16)
            return carry

        lax.fori_loop(0, half // 16, finish, 0)
    clock.finish()
    gather_wire.wait_sends()
    wire.wait_sends()
    for copy in saves:
        copy.wait()


def attend_back(
    lengths, grad_mixed, query, key, value, attended, log_total, cos_table, sin_table,
    tokens, gain, grad_state, gathered, w_out, w_query, w_key, w_value, grad_gate_up,
):
    n = lax.axis_size("tensor")
    pairs = lax.axis_size("dp") // 2
    rows, depth = tokens.shape
    group, q_width = query.shape
    kv_width, kv_raw = key.shape[1], w_key.shape[1]
    width = q_width + 2 * kv_raw
    deep = depth // (2 * pairs)
    dma = lambda count: pltpu.SemaphoreType.DMA((count,))
    early = deep - deep // 4
    chip_scratch = near_chip_sum_scratch(pairs, early, grad_gate_up.shape[1])
    return pl.pallas_call(
        attend_back_kernel,
        out_shape=(
            jax.ShapeDtypeStruct((rows, depth), BF16),
            jax.ShapeDtypeStruct((8, depth), F32),
            jax.ShapeDtypeStruct((pairs * deep, width + q_width), BF16),
            jax.ShapeDtypeStruct((early, grad_gate_up.shape[1]), BF16),
        ),
        in_specs=[smem_spec(), vmem_spec()] + [any_spec()] * 16,
        out_specs=(vmem_spec(), vmem_spec(), any_spec(), any_spec()),
        scratch_shapes=[
            *[
                pltpu.VMEM(source.shape, source.dtype)
                for source in (
                    query, key, value, attended, log_total, cos_table, sin_table, tokens, grad_state
                )
            ],
            pltpu.VMEM((group, depth), BF16),
            pltpu.VMEM(w_out.shape, BF16),
            pltpu.VMEM(w_query.shape, BF16),
            pltpu.VMEM(w_key.shape, BF16),
            pltpu.VMEM(w_value.shape, BF16),
            pltpu.VMEM((group, depth), BF16),
            pltpu.VMEM((group, q_width), BF16),
            pltpu.VMEM((group, kv_width), F32),
            pltpu.VMEM((group, kv_width), F32),
            pltpu.VMEM((group, width), BF16),
            pltpu.VMEM((group, depth), BF16),
            slots_for(n, rows, depth),
            pltpu.VMEM((2, q_width, deep), BF16),
            pltpu.VMEM((pairs, q_width, deep), BF16),
            pltpu.VMEM((2, deep, width), BF16),
            pltpu.VMEM((pairs, deep, width), BF16),
            *wires(n),
            *wires(n),
            dma(pairs), dma(pairs), dma(pairs), dma(pairs), dma(15 + pairs * (1 + q_width // deep)),
            *chip_scratch,
        ],
        cost_estimate=pl.CostEstimate(
            flops=2 * group * depth * q_width * 12, bytes_accessed=60 * 2**20, transcendentals=0
        ),
        compiler_params=params(5),
    )(lengths, gain, grad_mixed, query, key, value, attended, log_total, cos_table, sin_table,
      tokens, grad_state, gathered, w_out, w_query, w_key, w_value, grad_gate_up)


class GainSums:
    def __init__(self, gains, tiles, from_tensor, from_dp, wire, chunk):
        self.gains, self.tiles, self.from_tensor, self.from_dp = gains, tiles, from_tensor, from_dp
        self.wire, self.n, self.dps = wire, lax.axis_size("tensor"), lax.axis_size("dp")
        self.chunk = chunk
        self.me, self.dp = lax.axis_index("tensor"), lax.axis_index("dp")

    def tensor(self, step):
        return lax.rem(self.me + np.int32(step), np.int32(self.n))

    def data(self, step):
        return lax.rem(self.dp + np.int32(step), np.int32(self.dps))

    def greet(self):
        barrier = pltpu.get_barrier_semaphore()
        for step in range(1, self.n):
            device = {"tensor": self.tensor(step)}
            pl.semaphore_signal(barrier, inc=1, device_id=device, device_id_type=MESH)
        for step in range(1, self.dps):
            device = {"dp": self.data(step)}
            pl.semaphore_signal(barrier, inc=1, device_id=device, device_id_type=MESH)
        pl.semaphore_wait(barrier, self.n + self.dps - 2)

    def start(self):
        for t in range(self.n):
            for d in range(self.dps):
                lane = (d * self.n + t) * self.chunk // LANES * LANES
                for k, gain in enumerate(self.gains):
                    self.tiles[t, d, k] = gain[:, lane : lane + LANES]
        self.first = [
            self.wire.copy(
                self.tiles.at[self.tensor(step)],
                self.from_tensor.at[step - 1],
                {"tensor": self.tensor(step)},
            )
            for step in range(1, self.n)
        ]

    def forward(self):
        for copy in self.first:
            copy.wait_recv()
        total = self.tiles[self.me]
        for step in range(1, self.n):
            total = total + self.from_tensor[step - 1]
        self.from_tensor[0] = total
        self.second = [
            self.wire.copy(
                self.from_tensor.at[0, self.data(step)],
                self.from_dp.at[step - 1],
                {"dp": self.data(step)},
            )
            for step in range(1, self.dps)
        ]

    def finish(self, out):
        for copy in self.second:
            copy.wait_recv()
        total = self.from_tensor[0, self.dp]
        for step in range(1, self.dps):
            total = total + self.from_dp[step - 1]
        out[...] = total


def output_kernel(
    hidden_in, w_down, state, gain_one, gain_two, grad_gate_up, grads,
    output, gains_out, total_gate_up, total_grads,
    hidden, down_buf, part, slots, tiles, from_tensor, from_dp,
    send_sem, recv_sem, gain_send, gain_recv, local_sem, *chip_scratch,
):
    peers = Peers()
    rows, depth = state.shape
    local = Local(local_sem)
    loads = [local.copy(hidden_in, hidden), local.copy(w_down, down_buf)]
    chunk = depth // (lax.axis_size("tensor") * lax.axis_size("dp"))
    gains = GainSums(
        (gain_one, gain_two), tiles, from_tensor, from_dp, Wire(gain_send, gain_recv), chunk
    )
    gains.greet()
    base = grad_gate_up.shape[0] // (lax.axis_size("dp") // 2) - total_gate_up.shape[0]
    half = len(chip_scratch) // 2
    clock = Clock(
        [
            NearChipSum(grad_gate_up, base, chip_scratch[:half], total_gate_up, 0.0, 36.0),
            NearChipSum(grads, 0, chip_scratch[half:], total_grads, 36.0, 45.0),
        ]
    )
    clock.start()
    clock.to(0.5)
    gains.start()
    for load in loads:
        load.wait()

    def make(first, count):
        at = pl.ds(pl.multiple_of(first * rows, rows), count * rows)
        step = 512

        for k in range(depth // step):
            lanes = slice(k * step, (k + 1) * step)
            part[at, lanes] = dot_nn(hidden[at, :], down_buf[:, lanes]).astype(BF16)
            clock.by(1.6)

    wire = Wire(send_sem, recv_sem)
    ticks = clock.at(17.0, 29.0, 35.0, 47.0)
    sums = scatter(peers, wire, part, slots, rows, make, gains.forward, ticks)
    half = rows // 2
    for h in range(2):

        def finish(k, carry, h=h):
            inner = pl.ds(pl.multiple_of(k * 16, 16), 16)
            outer = pl.ds(pl.multiple_of(h * half + k * 16, 16), 16)
            total = sums[h][0][inner, :].astype(F32)
            for other in sums[h][1:]:
                total = total + other[inner, :].astype(F32)
            output[outer, :] = (state[outer, :] + total).astype(BF16)
            return carry

        lax.fori_loop(0, half // 16, finish, 0)
    gains.finish(gains_out)
    clock.finish()
    wire.wait_sends()
    gains.wire.wait_sends()


def layer_output(hidden, w_down, state, gain_one, gain_two, grad_gate_up, grads):
    n, dps = lax.axis_size("tensor"), lax.axis_size("dp")
    rows, depth = state.shape
    dma = lambda count: pltpu.SemaphoreType.DMA((count,))
    pairs = dps // 2
    deep = grads.shape[0] // pairs
    scratch_a = near_chip_sum_scratch(pairs, deep // 4, grad_gate_up.shape[1])
    scratch_b = near_chip_sum_scratch(pairs, deep, grads.shape[1])
    return pl.pallas_call(
        output_kernel,
        out_shape=(
            jax.ShapeDtypeStruct((rows, depth), BF16),
            jax.ShapeDtypeStruct((2, 8, LANES), F32),
            jax.ShapeDtypeStruct((deep // 4, grad_gate_up.shape[1]), BF16),
            jax.ShapeDtypeStruct((deep, grads.shape[1]), BF16),
        ),
        in_specs=[any_spec()] * 2 + [vmem_spec()] * 3 + [any_spec()] * 2,
        out_specs=(vmem_spec(), vmem_spec()) + (any_spec(),) * 2,
        scratch_shapes=[
            pltpu.VMEM(hidden.shape, BF16),
            pltpu.VMEM(w_down.shape, BF16),
            pltpu.VMEM((hidden.shape[0], depth), BF16),
            slots_for(n, rows, depth),
            pltpu.VMEM((n, dps, 2, 8, LANES), F32),
            pltpu.VMEM((n - 1, dps, 2, 8, LANES), F32),
            pltpu.VMEM((dps - 1, 2, 8, LANES), F32),
            *wires(n),
            dma(n + dps - 2), dma(n + dps - 2), dma(2),
            *scratch_a,
            *scratch_b,
        ],
        cost_estimate=pl.CostEstimate(
            flops=2 * hidden.shape[0] * depth * hidden.shape[1],
            bytes_accessed=20 * 2**20,
            transcendentals=0,
        ),
        compiler_params=params(6),
    )(hidden, w_down, state, gain_one, gain_two, grad_gate_up, grads)


def unpack_kernel(
    down, gate_up_a, gate_up_b, packed, output_in, tokens_in,
    grad_down, grad_gate, grad_up, grad_query, grad_key, grad_value, grad_out, output, grad_tokens,
):
    output[...] = output_in[...]
    grad_tokens[...] = tokens_in[...]
    grad_down[...] = down[...].astype(F32)
    units = grad_gate.shape[1]
    last = pl.num_programs(0) * 3 // 4

    @pl.when(pl.program_id(0) < last)
    def _():
        grad_gate[...] = gate_up_a[:, :units].astype(F32)
        grad_up[...] = gate_up_a[:, units:].astype(F32)

    @pl.when(pl.program_id(0) >= last)
    def _():
        grad_gate[...] = gate_up_b[:, :units].astype(F32)
        grad_up[...] = gate_up_b[:, units:].astype(F32)

    first = 0
    for target in (grad_query, grad_key, grad_value):
        width = target.shape[1]
        target[...] = packed[:, first : first + width].astype(F32)
        first += width
    deep = grad_out.shape[2]
    for c in range(grad_out.shape[0]):
        grad_out[c] = packed[:, first + c * deep : first + (c + 1) * deep].astype(F32)


def unpack(down, gate_up_a, gate_up_b, packed, output, tokens, q_width, kv_raw):
    deep, units = packed.shape[0], gate_up_a.shape[1] // 2
    steps = 8
    rows = lambda array: (array[0] // steps, array[1])
    spec = lambda array: pl.BlockSpec(rows(array), lambda i: (i, 0))
    early = pl.BlockSpec((deep // steps, 2 * units), lambda i: (jnp.minimum(i, steps * 3 // 4 - 1), 0))
    late = pl.BlockSpec((deep // steps, 2 * units), lambda i: (jnp.maximum(i - steps * 3 // 4, 0), 0))
    flat = (
        (down.shape, F32), ((deep, units), F32), ((deep, units), F32),
        ((deep, q_width), F32), ((deep, kv_raw), F32), ((deep, kv_raw), F32),
    )
    pieces = q_width // deep
    *grads, grad_out, output, tokens = pl.pallas_call(
        unpack_kernel,
        grid=(steps,),
        out_shape=(
            *[jax.ShapeDtypeStruct(shape, kind) for shape, kind in flat],
            jax.ShapeDtypeStruct((pieces, deep, deep), F32),
            jax.ShapeDtypeStruct(output.shape, BF16),
            jax.ShapeDtypeStruct(tokens.shape, BF16),
        ),
        in_specs=[
            spec(down.shape), early, late, spec(packed.shape), spec(output.shape),
            spec(tokens.shape),
        ],
        out_specs=(
            *[spec(shape) for shape, _ in flat],
            pl.BlockSpec((pieces, deep // steps, deep), lambda i: (0, i, 0)),
            spec(output.shape),
            spec(tokens.shape),
        ),
    )(down, gate_up_a, gate_up_b, packed, output, tokens)
    return *grads, grad_out.reshape(q_width, deep), output, tokens


def local(
    tokens, lengths, gain_one, w_query, w_key, w_value, w_out, gain_two, w_gate, w_up, w_down,
    cotangent,
):
    depth = tokens.shape[1]
    gain_one, gain_two = gain_one[None], gain_two[None]
    (
        gathered_one, query, key, value, cos_table, sin_table, attended, log_total, state, normed_two,
        cot_minor, cot_major,
    ) = front(
        lengths, tokens, gain_one, gain_two, w_query, w_key, w_value, w_out, cotangent
    )
    gathered_two, hidden, slope_gate, slope_up, cot_all, grad_down = hidden_units(
        normed_two, cotangent, cot_minor, cot_major, w_gate, w_up
    )
    grad_state, grad_mixed, gain_two_part, grad_gate_up, _, total_down = hidden_back(
        slope_gate, slope_up, cot_all, gathered_two, state, cotangent, gain_two,
        w_down, w_gate, w_up, grad_down,
    )
    grad_tokens, gain_one_part, grads, gate_up_a = attend_back(
        lengths, grad_mixed, query, key, value, attended, log_total, cos_table, sin_table,
        tokens, gain_one, grad_state, gathered_one, w_out, w_query, w_key, w_value, grad_gate_up,
    )
    output, gains, gate_up_b, packed = layer_output(
        hidden, w_down, state, gain_one_part, gain_two_part, grad_gate_up, grads
    )
    share = depth // (lax.axis_size("tensor") * lax.axis_size("dp"))
    place = lax.rem(
        (lax.axis_index("dp") * lax.axis_size("tensor") + lax.axis_index("tensor")) * share, LANES
    )
    gains = lax.dynamic_slice_in_dim(jnp.sum(gains, axis=1), place, share, axis=1)
    (
        grad_w_down, grad_w_gate, grad_w_up, grad_w_query, grad_w_key, grad_w_value, grad_w_out,
        output, grad_tokens,
    ) = unpack(
        total_down, gate_up_a, gate_up_b, packed, output, grad_tokens,
        w_query.shape[1], w_key.shape[1],
    )
    return (
        output, grad_tokens, gains[0], grad_w_query, grad_w_key, grad_w_value, grad_w_out,
        gains[1], grad_w_gate, grad_w_up, grad_w_down,
    )


def solution(mesh):
    return jax.shard_map(
        local,
        mesh=mesh,
        in_specs=(
            P(("dp", "tensor"), None),
            P("dp", None),
            P(),
            P(None, "tensor"),
            P(None, "tensor"),
            P(None, "tensor"),
            P("tensor", None),
            P(),
            P(None, "tensor"),
            P(None, "tensor"),
            P("tensor", None),
            P(("dp", "tensor"), None),
        ),
        out_specs=(
            P(("dp", "tensor"), None),
            P(("dp", "tensor"), None),
            P(("dp", "tensor")),
            P("dp", "tensor"),
            P("dp", "tensor"),
            P("dp", "tensor"),
            P("tensor", "dp"),
            P(("dp", "tensor")),
            P("dp", "tensor"),
            P("dp", "tensor"),
            P("tensor", "dp"),
        ),
        check_vma=False,
    )
```
